32 devices in a mesh: dp: 4 (over y, x), col: 8 (over z, core).
Axes of the slice: x: 2, y: 2, z: 4, core: 2. Of those that a mesh axis runs over, the one named last changes fastest.
Arguments:
- inputs: bfloat16 [32, 768, 960], P(('dp', 'col')), may hold values from -6 to 6
- segment_ids: int32 [32, 768], P(('dp', 'col')), may hold values from 0 to 3, never falling along the last dimension, each value on 1 to 384 neighbouring positions
- cotangent: bfloat16 [32, 768, 960], P(('dp', 'col')), may hold values from -6 to 6
- attn_gain: bfloat16 [2, 960], replicated, may hold values from 0.5 to 1.5
- query_weight: bfloat16 [2, 960, 960], P(None, None, 'col'), may hold values from -0.1875 to 0.1875
- key_value_weight: bfloat16 [2, 960, 640], P(None, None, 'col'), may hold values from -0.1875 to 0.1875
- output_weight: bfloat16 [2, 960, 960], P(None, 'col'), may hold values from -0.75 to 0.75
- ffn_gain: bfloat16 [2, 960], replicated, may hold values from 0.5 to 1.5
- gate_weight: bfloat16 [2, 960, 2560], P(None, None, 'col'), may hold values from -0.1875 to 0.1875
- upward_weight: bfloat16 [2, 960, 2560], P(None, None, 'col'), may hold values from -0.1875 to 0.1875
- down_weight: bfloat16 [2, 2560, 960], P(None, 'col'), may hold values from -0.125 to 0.125
Outputs:
- final: bfloat16 [32, 768, 960], P(('dp', 'col'))
- input_grad: float32 [32, 768, 960], P(('dp', 'col'))
- attn_gain_grad: float32 [2, 960], replicated
- query_grad: float32 [2, 960, 960], P(None, None, 'col')
- keyval_grad: float32 [2, 960, 640], P(None, None, 'col')
- output_grad: float32 [2, 960, 960], P(None, 'col')
- ffn_gain_grad: float32 [2, 960], replicated
- gate_grad: float32 [2, 960, 2560], P(None, None, 'col')
- upward_grad: float32 [2, 960, 2560], P(None, None, 'col')
- down_grad: float32 [2, 2560, 960], P(None, 'col')
The draws below stay inside these ranges and needn't reach their ends.
Inputs may be any that keep to these rules, and one draw needn't show every extreme that they name: `segment_ids`: within each sequence of 768 tokens the segment numbers never fall, and each segment holds at most 384 tokens.
All inputs are finite; a program needn't handle non-finite values.
Results may differ from the reference program's by a relative error of at most 0.025.
Values may be sent and summed in bfloat16 or wider, within the bound.
No kernel may reach another device: no remote copies, remote signals or barrier semaphores. Data moves between devices by JAX's collectives and lax.ppermute only.
A program may use at most 384 MiB of HBM per device.

```python
import math
import jax
import jax.numpy as jnp
import numpy as np
from jax import lax

MODEL_WIDTH = 960
QUERY_HEADS = 15
KEY_VALUE_HEADS = 5
HEAD_WIDTH = 64
FF = 2560
LAYER_COUNT = 2
SEQ = 768
SEQS = 32


def shard_levels(stream_key, shape, shards, least, high):
    factor_of, own = 1.0, jax.random.fold_in(stream_key, 6)
    for dim, shards_of in shards:
        heights = jnp.exp(jax.random.uniform(jax.random.fold_in(own, dim), (shards_of,), jnp.float32, least / len(shards), high / len(shards)))
        factor_of = factor_of * jnp.repeat(heights, shape[dim] // shards_of).reshape([-1 if axis == dim else 1 for axis in range(len(shape))])
    return factor_of


def profile(amount, total, limit, skew):
    portions = [(1 << 20) // math.isqrt(standing ** skew) + 1 for standing in range(2, amount + 1)]
    surplus, given = total - limit - (amount - 1), [1] * (amount - 1)
    while surplus > 0:
        candidates = [i for i in range(amount - 1) if given[i] < limit]
        pool, budget = sum([portions[i] for i in candidates]), surplus
        for i in candidates:
            addition = min(limit - given[i], max(1, budget * portions[i] // pool), surplus)
            given[i] = given[i] + addition
            surplus = surplus - addition
    return np.array([limit] + given)


def ragged_sizes(key, count, total, most, slope):
    if count == 2:
        one = jax.random.randint(key, (), max(1, total - most), min(most, total - 1) + 1)
        return jnp.stack([one, total - one])
    tallies = jnp.asarray(profile(count, total, most, slope), jnp.int32)
    pairs = (count - 1) // 2
    donor, receiver = tallies[1:1 + 2 * pairs:2], tallies[2:2 + 2 * pairs:2]
    margin = jnp.minimum(donor - 1, most - receiver)
    shifted = jax.random.randint(jax.random.fold_in(key, 1), (pairs,), 0, 1 << 20) % (margin + 1)
    tallies = tallies.at[1:1 + 2 * pairs:2].set(donor - shifted).at[2:2 + 2 * pairs:2].set(receiver + shifted)
    return tallies[jax.random.permutation(jax.random.fold_in(key, 2), count)]


def bell_draw(own_key, extent, width, reach, shards=(), kind=jnp.bfloat16):
    loudness = shard_levels(own_key, extent, shards, -0.22, 0.18) if shards else 1.0
    array = jax.random.normal(own_key, extent, jnp.float32) * width * loudness
    return jnp.minimum(jnp.maximum(array, -reach), reach).astype(kind)


def setup_inputs(seed: int = 0) -> dict:
    key_of = jax.random.split(jax.random.key(seed), 12)
    return {
        "inputs": bell_draw(key_of[0], (SEQS, SEQ, MODEL_WIDTH), 1.0, 6.0, ((0, 32),)),
        "segment_ids": jax.vmap(lambda own: jnp.searchsorted(jnp.cumsum(ragged_sizes(own, 4, SEQ, SEQ // 2, 0)), jnp.arange(SEQ), side="right"))(jax.random.split(key_of[1], SEQS)).reshape((SEQS, SEQ)).astype(jnp.int32),
        "cotangent": bell_draw(key_of[2], (SEQS, SEQ, MODEL_WIDTH), 1.0, 6.0, ((0, 32),)),
        "attn_gain": jnp.clip(1.0 + 0.1 * jax.random.normal(key_of[3], (LAYER_COUNT, MODEL_WIDTH), jnp.float32), 0.5, 1.5).astype(jnp.bfloat16),
        "query_weight": bell_draw(key_of[4], (LAYER_COUNT, MODEL_WIDTH, QUERY_HEADS * HEAD_WIDTH), MODEL_WIDTH ** -0.5, 0.1875, ((2, 8),)),
        "key_value_weight": bell_draw(key_of[5], (LAYER_COUNT, MODEL_WIDTH, 2 * KEY_VALUE_HEADS * HEAD_WIDTH), MODEL_WIDTH ** -0.5, 0.1875, ((2, 8),)),
        "output_weight": bell_draw(key_of[6], (LAYER_COUNT, QUERY_HEADS * HEAD_WIDTH, MODEL_WIDTH), (QUERY_HEADS * HEAD_WIDTH // 16) ** -0.5, 0.75, ((1, 8),)),
        "ffn_gain": jnp.clip(1.0 + 0.1 * jax.random.normal(key_of[7], (LAYER_COUNT, MODEL_WIDTH), jnp.float32), 0.5, 1.5).astype(jnp.bfloat16),
        "gate_weight": bell_draw(key_of[8], (LAYER_COUNT, MODEL_WIDTH, FF), MODEL_WIDTH ** -0.5, 0.1875, ((2, 8),)),
        "upward_weight": bell_draw(key_of[9], (LAYER_COUNT, MODEL_WIDTH, FF), MODEL_WIDTH ** -0.5, 0.1875, ((2, 8),)),
        "down_weight": bell_draw(key_of[10], (LAYER_COUNT, FF, MODEL_WIDTH), FF ** -0.5, 0.125, ((1, 8),)),
    }


@jax.custom_vjp
def reduced_precision(v):
    return lax.optimization_barrier(v.astype(jnp.bfloat16)).astype(jnp.float32)

@jax.custom_vjp
def low_back(v):
    return v

def low_keep(v):
    return (reduced_precision(v), None)

def low_pass(kept, grad):
    return (grad,)

def back_keep(v):
    return (v, None)

def back_low(kept, grad):
    return (reduced_precision(grad),)
reduced_precision.defvjp(low_keep, low_pass)
low_back.defvjp(back_keep, back_low)
epsilon = 1e-05
theta_base = 10000.0

def rms_norm(value_rows, gain):
    return value_rows * lax.rsqrt(lax.optimization_barrier(jnp.mean(value_rows * value_rows, axis=-1, keepdims=True)) + epsilon) * gain

def apply_rotary(value_rows, cosine_table, sine_table):
    half = value_rows.shape[-1] // 2
    first = value_rows[..., :half]
    second = value_rows[..., half:]
    return jnp.concatenate([first * cosine_table - second * sine_table, second * cosine_table + first * sine_table], axis=-1)

def tables(segments, head_size):
    sequence_length = segments.shape[0]
    rows = jnp.arange(sequence_length, dtype=jnp.int32)
    before = lax.optimization_barrier(jnp.sum((segments[None, :] < segments[:, None]).astype(jnp.int32), axis=1))
    places = (rows - before).astype(jnp.float32)
    half = head_size // 2
    freqs = jnp.exp(-math.log(theta_base) * (2.0 * jnp.arange(half, dtype=jnp.float32) / head_size))
    angles = places[:, None] * freqs[None, :]
    permitted_mask = (rows[None, :] <= rows[:, None]) & (segments[None, :] == segments[:, None])
    return (permitted_mask, jnp.cos(angles)[:, None, :], jnp.sin(angles)[:, None, :])

def matmul(left, right):
    return jnp.dot(left, right, precision=lax.Precision.HIGHEST)

def attention_probs(query_grouped, keys, value_rows, permitted_mask):
    raw = jnp.einsum('qkgd,ckd->kgqc', query_grouped, keys, precision=lax.Precision.HIGHEST) * HEAD_WIDTH ** (-0.5)
    logits = jnp.where(permitted_mask[None, None], low_back(raw), -1e+30)
    peak = lax.optimization_barrier(jnp.max(logits, axis=-1, keepdims=True))
    expo = jnp.exp(logits - peak)
    probs = reduced_precision(expo / lax.optimization_barrier(jnp.sum(expo, axis=-1, keepdims=True)))
    return jnp.einsum('kgqc,ckd->qkgd', probs, value_rows, precision=lax.Precision.HIGHEST)

def layer_forward(hidden, params, permitted_mask, cosine_table, sine_table):
    attn_g, query_w, keyval_w, output_w, ffn_g, gate_w, upward_w, down_w = params
    sequence_length = hidden.shape[0]
    feature_width = KEY_VALUE_HEADS * HEAD_WIDTH
    normed = reduced_precision(rms_norm(hidden, attn_g))
    query = low_back(matmul(normed, query_w))
    key_value_rows = low_back(matmul(normed, keyval_w))
    rotated_queries = reduced_precision(apply_rotary(query.reshape(sequence_length, QUERY_HEADS, HEAD_WIDTH), cosine_table, sine_table))
    rotated_keys = reduced_precision(apply_rotary(key_value_rows[:, :feature_width].reshape(sequence_length, KEY_VALUE_HEADS, HEAD_WIDTH), cosine_table, sine_table))
    value_rows = reduced_precision(key_value_rows[:, feature_width:].reshape(sequence_length, KEY_VALUE_HEADS, HEAD_WIDTH))
    attended_values = jax.checkpoint(attention_probs)(rotated_queries.reshape(sequence_length, KEY_VALUE_HEADS, QUERY_HEADS // KEY_VALUE_HEADS, HEAD_WIDTH), rotated_keys, value_rows, permitted_mask)
    attended_values = reduced_precision(low_back(attended_values.reshape(sequence_length, QUERY_HEADS * HEAD_WIDTH)))
    middle = hidden + low_back(matmul(attended_values, output_w))
    normed2 = reduced_precision(rms_norm(middle, ffn_g))
    gate = low_back(matmul(normed2, gate_w))
    upward = low_back(matmul(normed2, upward_w))
    active = reduced_precision(jax.nn.silu(gate) * upward)
    return middle + low_back(matmul(active, down_w))

def reference(inputs, segment_ids, cotangent, attn_gain, query_weight, key_value_weight, output_weight, ffn_gain, gate_weight, upward_weight, down_weight):
    params = tuple((w.astype(jnp.float32) for w in (attn_gain, query_weight, key_value_weight, output_weight, ffn_gain, gate_weight, upward_weight, down_weight)))
    layers = attn_gain.shape[0]

    def forward(hidden, weights, permitted_mask, cosine_table, sine_table):
        for layer_index in range(layers):
            hidden = layer_forward(hidden, tuple((w[layer_index] for w in weights)), permitted_mask, cosine_table, sine_table)
        return hidden
    zeros = tuple((jnp.zeros(w.shape, jnp.float32) for w in params))

    def one_sequence(totals, item):
        rows, segments, upstream = item
        permitted_mask, cosine_table, sine_table = tables(segments, HEAD_WIDTH)
        result, pull = jax.vjp(lambda h, w: forward(h, w, permitted_mask, cosine_table, sine_table), rows.astype(jnp.float32), params)
        grad_rows, grad_params = pull(upstream.astype(jnp.float32))
        totals = tuple((t + g for t, g in zip(totals, grad_params)))
        return (totals, (result.astype(jnp.bfloat16), grad_rows))
    totals, outputs = lax.scan(one_sequence, zeros, (inputs, segment_ids, cotangent))
    return (outputs[0], outputs[1], totals[0], totals[1], totals[2], totals[3], totals[4], totals[5], totals[6], totals[7])
```

```python
import functools
import math

import jax
import jax.numpy as jnp
from jax import lax
from jax.experimental import pallas as pl
from jax.experimental.pallas import tpu as pltpu
from jax.sharding import PartitionSpec as P

QUERY_HEADS = 15
KEY_VALUE_HEADS = 5
HEAD_WIDTH = 64


epsilon = 1e-05
theta_base = 10000.0


def rms_norm(value_rows, gain):
    return (
        value_rows
        * lax.rsqrt(jnp.mean(value_rows * value_rows, axis=-1, keepdims=True) + epsilon)
        * gain
    )


def tables(segments, head_size):
    sequence_length = segments.shape[0]
    rows = jnp.arange(sequence_length, dtype=jnp.int32)
    before = jnp.sum((segments[None, :] < segments[:, None]).astype(jnp.int32), axis=1)
    places = (rows - before).astype(jnp.float32)
    half = head_size // 2
    freqs = jnp.exp(-math.log(theta_base) * (2.0 * jnp.arange(half, dtype=jnp.float32) / head_size))
    angles = places[:, None] * freqs[None, :]
    cosine, sine = jnp.cos(angles), jnp.sin(angles)
    return (jnp.tile(cosine, (1, 4)), jnp.tile(jnp.concatenate([-sine, sine], axis=1), (1, 2)))


BLOCK = 256
REACH = 384
MEGA = 2**20


def call(body, outs, args, after=(), scratch=(), limit=56, flops=0, nbytes=0, **grid):
    given = len(args)
    late = len(after)

    def run(*refs):
        body(*refs[:given], *refs[given + late :])

    specs = grid.pop("in_specs", None) or [pl.BlockSpec(memory_space=pltpu.VMEM)] * given
    out_specs = grid.pop("out_specs", None) or [pl.BlockSpec(memory_space=pltpu.VMEM)] * len(outs)
    return pl.pallas_call(
        run,
        out_shape=outs,
        in_specs=list(specs) + [pl.BlockSpec(memory_space=pl.ANY)] * late,
        out_specs=out_specs,
        scratch_shapes=list(scratch),
        compiler_params=pltpu.CompilerParams(vmem_limit_bytes=limit * MEGA),
        cost_estimate=pl.CostEstimate(flops=flops, bytes_accessed=nbytes, transcendentals=0),
        **grid,
    )(*args, *after)


def dot(left, right, dims=((1,), (0,))):
    return lax.dot_general(left, right, (dims, ((), ())), preferred_element_type=jnp.float32)


NT = ((1,), (1,))
TN = ((0,), (0,))


def swap_halves(value):
    lane = lax.broadcasted_iota(jnp.int32, value.shape, 1)
    return jnp.where(lane % HEAD_WIDTH < HEAD_WIDTH // 2, pltpu.roll(value, 96, 1), pltpu.roll(value, 32, 1))


def spans(length):
    for start in range(0, length, BLOCK):
        yield start, max(0, start - REACH + 1) // 128 * 128, start + BLOCK


def fill_bias(bias, seg_col, seg_row, length):
    for index, (start, low, high) in enumerate(spans(length)):
        shape = (high - low, BLOCK)
        key = lax.broadcasted_iota(jnp.int32, shape, 0) + low
        query = lax.broadcasted_iota(jnp.int32, shape, 1) + start
        same = seg_col[low:high, :] == seg_row[:, start : start + BLOCK]
        bias[index, : high - low, :] = jnp.where((key <= query) & same, 0.0, -1e30)


def attention_forward(raw, cosine, sine, seg_col, seg_row, after=()):
    length, width = raw.shape
    q_width = QUERY_HEADS * HEAD_WIDTH
    kv_width = KEY_VALUE_HEADS * HEAD_WIDTH
    group = QUERY_HEADS // KEY_VALUE_HEADS
    rotated = q_width + kv_width
    most = max(high - low for _, low, high in spans(length))

    def body(raw, cosine, sine, seg_col, seg_row, qkv, attended, logsum, bias, turned):
        for lane in range(0, rotated, 128):
            value = raw[:, lane : lane + 128]
            qkv[:, lane : lane + 128] = (value * cosine[...] + swap_halves(value) * sine[...]).astype(jnp.bfloat16)
        qkv[:, rotated:] = raw[:, rotated:].astype(jnp.bfloat16)
        fill_bias(bias, seg_col, seg_row, length)
        logsum[...] = jnp.zeros_like(logsum)
        turned[...] = raw[:, rotated:].T.astype(jnp.bfloat16)
        for index, (start, low, high) in enumerate(spans(length)):
            columns = []
            for head in range(QUERY_HEADS):
                kv = head // group
                query = qkv[start : start + BLOCK, head * HEAD_WIDTH : (head + 1) * HEAD_WIDTH] * 0.125
                at = q_width + kv * HEAD_WIDTH
                key = qkv[low:high, at : at + HEAD_WIDTH]
                logits = dot(key, query, NT) + bias[index, : high - low, :]
                peak = jnp.max(logits, axis=0, keepdims=True)
                expo = jnp.exp(logits - peak)
                total = jnp.sum(expo, axis=0, keepdims=True)
                value = turned[kv * HEAD_WIDTH : (kv + 1) * HEAD_WIDTH, low:high]
                columns.append(dot(value, expo.astype(jnp.bfloat16)) / total)
                logsum[head : head + 1, start : start + BLOCK] = peak + jnp.log(total)
            attended[start : start + BLOCK, :] = jnp.concatenate(columns, axis=0).T.astype(jnp.bfloat16)

    return call(
        body,
        [
            jax.ShapeDtypeStruct((length, width), jnp.bfloat16),
            jax.ShapeDtypeStruct((length, q_width), jnp.bfloat16),
            jax.ShapeDtypeStruct((16, length), jnp.float32),
        ],
        [raw, cosine, sine, seg_col, seg_row],
        after,
        [
            pltpu.VMEM((length // BLOCK, most, BLOCK), jnp.float32),
            pltpu.VMEM((kv_width, length), jnp.bfloat16),
        ],
        flops=15 * 10**9,
        nbytes=15 * MEGA,
    )


def attention_backward(qkv, grad, logsum, cosine, sine, seg_col, seg_row, after=()):
    length, width = qkv.shape
    q_width = QUERY_HEADS * HEAD_WIDTH
    kv_width = KEY_VALUE_HEADS * HEAD_WIDTH
    group = QUERY_HEADS // KEY_VALUE_HEADS
    rotated = q_width + kv_width
    most = max(high - low for _, low, high in spans(length))
    scale = 0.125

    def body(qkv, grad, logsum, cosine, sine, seg_col, seg_row, out, bias, turned, key_sum, value_sum, query_sum):
        fill_bias(bias, seg_col, seg_row, length)
        turned[...] = qkv[:, q_width:rotated].astype(jnp.float32).T.astype(jnp.bfloat16) * scale
        key_sum[...] = jnp.zeros_like(key_sum)
        value_sum[...] = jnp.zeros_like(value_sum)
        for index, (start, low, high) in enumerate(spans(length)):
            for head in range(QUERY_HEADS):
                kv = head // group
                lanes = slice(head * HEAD_WIDTH, (head + 1) * HEAD_WIDTH)
                query = qkv[start : start + BLOCK, lanes] * scale
                upstream = grad[start : start + BLOCK, lanes]
                at = q_width + kv * HEAD_WIDTH
                key = qkv[low:high, at : at + HEAD_WIDTH]
                value = qkv[low:high, at + kv_width : at + kv_width + HEAD_WIDTH]
                logits = dot(key, query, NT) + bias[index, : high - low, :]
                probs = jnp.exp(logits - logsum[head : head + 1, start : start + BLOCK])
                grad_probs = dot(value, upstream, NT)
                inner = jnp.sum(probs * grad_probs, axis=0, keepdims=True)
                grad_logits = (probs * (grad_probs - inner)).astype(jnp.bfloat16)
                value_sum[kv, low:high, :] += dot(probs.astype(jnp.bfloat16), upstream)
                key_sum[kv, low:high, :] += dot(grad_logits, query)
                query_sum[lanes, start : start + BLOCK] = dot(
                    turned[kv * HEAD_WIDTH : (kv + 1) * HEAD_WIDTH, low:high], grad_logits
                )
        raw = [query_sum[...].T] + [key_sum[kv] for kv in range(KEY_VALUE_HEADS)]
        raw = jnp.concatenate(raw, axis=1)
        for lane in range(0, rotated, 128):
            value = raw[:, lane : lane + 128]
            out[:, lane : lane + 128] = (value * cosine[...] - swap_halves(value) * sine[...]).astype(jnp.bfloat16)
        out[:, rotated:] = jnp.concatenate([value_sum[kv] for kv in range(KEY_VALUE_HEADS)], axis=1).astype(jnp.bfloat16)

    return call(
        body,
        [jax.ShapeDtypeStruct((length, width), jnp.bfloat16)],
        [qkv, grad, logsum, cosine, sine, seg_col, seg_row],
        after,
        [
            pltpu.VMEM((length // BLOCK, most, BLOCK), jnp.float32),
            pltpu.VMEM((kv_width, length), jnp.bfloat16),
            pltpu.VMEM((KEY_VALUE_HEADS, length, HEAD_WIDTH), jnp.float32),
            pltpu.VMEM((KEY_VALUE_HEADS, length, HEAD_WIDTH), jnp.float32),
            pltpu.VMEM((q_width, length), jnp.float32),
        ],
        flops=30 * 10**9,
        nbytes=20 * MEGA,
    )[0]


TILE = 256


def ffn_forward(middle, normed, here, there, after=()):
    length, width = middle.shape
    units = here[0].shape[0]
    tile = math.gcd(TILE, units)
    steps = units // tile

    def body(middle, normed, gate_a, upward_a, down_a, gate_b, upward_b, down_b, out, gate_one, up_one, gate_two, up_two):
        step = pl.program_id(0)

        @pl.when(step == 0)
        def _():
            out[...] = middle[...]

        def half(gate_w, upward_w, down_w, gate_out, upward_out):
            gate = dot(normed[...], gate_w[...], NT)
            upward = dot(normed[...], upward_w[...], NT)
            gate_out[...] = gate.astype(jnp.bfloat16)
            upward_out[...] = upward.astype(jnp.bfloat16)
            active = (gate * jax.nn.sigmoid(gate) * upward).astype(jnp.bfloat16)
            out[...] += dot(active, down_w[...])

        @pl.when(step < steps)
        def _():
            half(gate_a, upward_a, down_a, gate_one, up_one)

        @pl.when(step >= steps)
        def _():
            half(gate_b, upward_b, down_b, gate_two, up_two)

    whole = pl.BlockSpec((length, width), lambda i: (0, 0))
    weight_a = pl.BlockSpec((tile, width), lambda i: (jnp.minimum(i, steps - 1), 0))
    weight_b = pl.BlockSpec((tile, width), lambda i: (jnp.maximum(i - steps, 0), 0))
    columns_a = pl.BlockSpec((length, tile), lambda i: (0, jnp.minimum(i, steps - 1)))
    columns_b = pl.BlockSpec((length, tile), lambda i: (0, jnp.maximum(i - steps, 0)))
    low = jax.ShapeDtypeStruct((length, units), jnp.bfloat16)
    return call(
        body,
        [jax.ShapeDtypeStruct((length, width), jnp.float32), low, low, low, low],
        [middle, normed, *here, *there],
        after,
        grid=(2 * steps,),
        in_specs=[whole, whole] + [weight_a] * 3 + [weight_b] * 3,
        out_specs=[whole, columns_a, columns_a, columns_b, columns_b],
        flops=11 * 10**9,
        nbytes=20 * MEGA,
    )


def ffn_backward(grad_low, normed, gate, upward, gate_full, upward_full, down_full, earlier=None):
    length, width = normed.shape
    units = gate_full.shape[0]
    tile = math.gcd(TILE, units)

    def body(grad_low, normed, gate, upward, gate_w, upward_w, down_w, *rest):
        *before, gate_grad, upward_grad, down_grad, out = rest

        @pl.when(pl.program_id(0) == 0)
        def _():
            out[...] = before[0][...] if before else jnp.zeros_like(out)

        grad_active = dot(grad_low[...], down_w[...], NT)
        gate_value = gate[...].astype(jnp.float32)
        up_value = upward[...].astype(jnp.float32)
        sigma = jax.nn.sigmoid(gate_value)
        silu = gate_value * sigma
        down_grad[...] = dot((silu * up_value).astype(jnp.bfloat16), grad_low[...], TN).astype(jnp.bfloat16)
        grad_up = (grad_active * silu).astype(jnp.bfloat16)
        grad_gate = (grad_active * up_value * (sigma + silu * (1.0 - sigma))).astype(jnp.bfloat16)
        gate_grad[...] = dot(grad_gate, normed[...], TN).astype(jnp.bfloat16)
        upward_grad[...] = dot(grad_up, normed[...], TN).astype(jnp.bfloat16)
        out[...] += dot(grad_gate, gate_w[...]) + dot(grad_up, upward_w[...])

    whole = pl.BlockSpec((length, width), lambda i: (0, 0))
    weight = pl.BlockSpec((tile, width), lambda i: (i, 0))
    columns = pl.BlockSpec((length, tile), lambda i: (0, i))
    shape = jax.ShapeDtypeStruct((units, width), jnp.bfloat16)
    before = [] if earlier is None else [earlier]
    return call(
        body,
        [shape, shape, shape, jax.ShapeDtypeStruct((length, width), jnp.float32)],
        [grad_low, normed, gate, upward, gate_full, upward_full, down_full, *before],
        grid=(units // tile,),
        in_specs=[whole, whole, columns, columns, weight, weight, weight] + [whole] * len(before),
        out_specs=[weight, weight, weight, whole],
        flops=22 * 10**9,
        nbytes=45 * MEGA,
    )


class Links:
    def __init__(self, dp, col):
        self.dp, self.col, self.line = dp, col, col // 2
        self.rest = [list(range(r, dp, 4)) for r in range(4)]
        self.quarter = lax.axis_index("dp") % 4
        self.core = lax.axis_index("col") % 2
        self.chip = lax.axis_index("col") // 2

    def x(self, value):
        return lax.ppermute(value, "dp", [(i, i ^ 1) for i in range(self.dp)])

    def y(self, value):
        return lax.ppermute(value, "dp", [(i, i ^ 2) for i in range(self.dp)])

    def other_core(self, value):
        return lax.ppermute(value, "col", [(i, i ^ 1) for i in range(self.col)])

    def send(self, value, step):
        return lax.ppermute(value, "col", [(i, (i + 2 * step) % self.col) for i in range(self.col)])

    def sum_all(self, value):
        for axis, size in (("dp", self.dp), ("col", self.col)):
            step = 1
            while step < size:
                value = value + lax.ppermute(value, axis, [(i, i ^ step) for i in range(size)])
                step *= 2
        return value


def add(*terms):
    total = terms[0].astype(jnp.float32)
    for term in terms[1:]:
        total = total + term.astype(jnp.float32)
    return total.astype(jnp.bfloat16)


class Transfer:
    def __init__(self, stages):
        self.stages = stages
        self.result = None
        self.flying = next(stages)

    def advance(self, arrays=None):
        try:
            self.flying = self.stages.send(self.flying if arrays is None else arrays)
        except StopIteration as stop:
            self.flying, self.result = [], stop.value

    def finish(self):
        while self.result is None:
            self.advance()
        return self.result


def advance(value, *transfers):
    flying = [transfer.flying for transfer in transfers]
    value, flying = lax.optimization_barrier((value, flying))
    for transfer, arrays in zip(transfers, flying, strict=True):
        transfer.advance(arrays)
    return value


def gather_stages(links, part):
    far = yield [links.send(part, -step) for step in range(1, links.line)]
    own = jnp.stack([part, *far])
    half = links.line // 2
    from_x, from_y, own_c = yield [links.x(own), links.y(own), links.other_core(own)]
    low, high, x_c, y_c = yield [
        links.y(from_x[:half]),
        links.x(from_y[half:]),
        links.other_core(from_x),
        links.other_core(from_y),
    ]
    low_c, high_c = yield [links.other_core(low), links.other_core(high)]
    return [
        [own, from_x, from_y, jnp.concatenate([low, high])],
        [own_c, x_c, y_c, jnp.concatenate([low_c, high_c])],
    ]


def scatter_stages(links, here, there):
    got = yield [links.other_core(block) for block in there]
    half = links.line // 2
    count = len(here)
    sums = [[add(mine[j], theirs[j]) for j in range(4)] for mine, theirs in zip(here, got, strict=True)]
    got = yield (
        [links.y(s[3][:half]) for s in sums]
        + [links.x(s[3][half:]) for s in sums]
        + [links.x(s[1][half:]) for s in sums]
        + [links.y(s[2][:half]) for s in sums]
    )
    low, high, x_high, y_low = (got[i * count : (i + 1) * count] for i in range(4))
    got = yield (
        [links.x(add(s[1][:half], v)) for s, v in zip(sums, low, strict=True)]
        + [links.y(add(s[2][half:], v)) for s, v in zip(sums, high, strict=True)]
    )
    x_low, y_high = got[:count], got[count:]
    own = []
    for i, s in enumerate(sums):
        own.append(
            [add(s[0][j], x_low[i][j], y_low[i][j]) for j in range(half)]
            + [add(s[0][half + j], x_high[i][j], y_high[i][j]) for j in range(links.line - half)]
        )
    got = yield [links.send(blocks[step], step) for blocks in own for step in range(1, links.line)]
    each = links.line - 1
    total = [add(blocks[0], *got[i * each : (i + 1) * each]) for i, blocks in enumerate(own)]
    if links.dp > 4:
        total = [lax.psum(t, "dp", axis_index_groups=links.rest) for t in total]
    got = yield [links.x(t) for t in total] + [links.y(t) for t in total]
    both = yield [links.y(t) for t in got[:count]]
    return [(t, got[i], got[count + i], both[i]) for i, t in enumerate(total)]


def in_order(links, quarters):
    whole = jnp.zeros((4, *quarters[0].shape), quarters[0].dtype)
    for place, block in enumerate(quarters):
        whole = lax.dynamic_update_index_in_dim(whole, block, links.quarter ^ place, 0)
    return whole


def own_quarter(links, packed, axis):
    shape = packed.shape[:axis] + (4, packed.shape[axis] // 4) + packed.shape[axis + 1 :]
    return lax.dynamic_index_in_dim(packed.reshape(shape), links.quarter, axis, False)


def attention_weights(links, blocks, rows):
    part, width = blocks[0][0].shape[1:]
    whole = jnp.zeros((links.line, 2, 4, part, width), jnp.bfloat16)
    for core in range(2):
        for place in range(4):
            whole = lax.dynamic_update_slice(
                whole,
                jnp.roll(blocks[core][place], links.chip, axis=0)[:, None, None],
                (0, links.core ^ core, links.quarter ^ place, 0, 0),
            )
    whole = whole.reshape(links.col, 4 * part, width)
    a, b = rows[0], rows[0] + rows[1]
    return (
        jnp.concatenate([whole[:, :a].reshape(-1, width), whole[:, a:b].reshape(-1, width)]),
        whole[:, b:].reshape(-1, width),
    )


def attention_blocks(links, qkv_grad, output_grad, rows):
    width = output_grad.shape[1]
    cut = rows[0] * links.col
    parts = [g.reshape(links.col, -1, width) for g in (qkv_grad[:cut], qkv_grad[cut:], output_grad)]
    whole = jnp.concatenate(parts, axis=1)
    whole = whole.reshape(links.line, 2, 4, -1, width)
    whole = jnp.roll(whole, -links.chip, axis=0)
    return [
        jnp.stack(
            [
                lax.dynamic_slice(
                    whole,
                    (0, links.core ^ core, links.quarter ^ place, 0, 0),
                    (links.line, 1, 1, *whole.shape[3:]),
                )[:, 0, 0]
                for place in range(4)
            ]
        )
        for core in range(2)
    ]


def rms_pull(value, gain, grad):
    scale = lax.rsqrt(jnp.mean(value * value, axis=-1, keepdims=True) + epsilon)
    scaled = value * scale
    pulled = grad * gain
    inner = jnp.mean(pulled * scaled, axis=-1, keepdims=True)
    return scale * (pulled - scaled * inner), jnp.sum(grad * scaled, axis=0)


def per_device(
    dp,
    col,
    inputs,
    segment_ids,
    cotangent,
    attn_gain,
    query_weight,
    key_value_weight,
    output_weight,
    ffn_gain,
    gate_weight,
    upward_weight,
    down_weight,
):
    links = Links(dp, col)
    layers, width = attn_gain.shape
    rows = (query_weight.shape[2], key_value_weight.shape[2], output_weight.shape[1])
    segments = segment_ids[0]
    where = (*tables(segments, HEAD_WIDTH), segments[:, None], segments[None, :])
    attn_gains = attn_gain.astype(jnp.float32)
    ffn_gains = ffn_gain.astype(jnp.float32)

    weights = []
    previous = None
    for layer in range(layers):
        attn_part = jnp.concatenate([query_weight[layer].T, key_value_weight[layer].T, output_weight[layer]])
        ffn_part = jnp.stack([gate_weight[layer].T, upward_weight[layer].T, down_weight[layer]])
        attn_part = own_quarter(links, attn_part, 0)
        ffn_part = own_quarter(links, ffn_part, 1)
        if previous is not None:
            attn_part = advance(attn_part, previous)
        attn_move = Transfer(gather_stages(links, attn_part))
        ffn_part = advance(ffn_part, attn_move)
        previous = Transfer(gather_stages(links, ffn_part))
        weights.append((attn_move, previous))

    hidden = inputs[0].astype(jnp.float32)
    saved = []
    for layer in range(layers):
        attn_move, ffn_move = weights[layer]
        qkv_w, output_w = attention_weights(links, attn_move.finish(), rows)
        normed = rms_norm(hidden, attn_gains[layer]).astype(jnp.bfloat16)
        raw = dot(normed, qkv_w, NT)
        qkv, attended, logsum = attention_forward(raw, *where)
        middle = hidden + dot(attended, output_w)
        normed2 = rms_norm(middle, ffn_gains[layer]).astype(jnp.bfloat16)
        ffn_w = [
            [jnp.concatenate([block[:, kind].reshape(-1, width) for block in half]) for kind in range(3)]
            for half in ffn_move.finish()
        ]
        result, *products = ffn_forward(middle, normed2, *ffn_w)
        saved.append((hidden, normed, qkv, attended, logsum, middle, normed2, products, qkv_w, output_w, ffn_w))
        hidden = result
    final = hidden.astype(jnp.bfloat16)[None]

    grad = cotangent[0].astype(jnp.float32)
    moves = [None] * layers
    gain_terms = [None] * layers
    attn_move = ffn_move = None
    for layer in reversed(range(layers)):
        hidden, normed, qkv, attended, logsum, middle, normed2, products, qkv_w, output_w, ffn_w = saved[layer]
        before = [] if attn_move is None else [attn_move]
        both = [] if attn_move is None else [ffn_move, attn_move]
        grad_low = grad.astype(jnp.bfloat16)
        shape = (4, links.line, -1, width)
        *there, grad_normed = ffn_backward(grad_low, normed2, *products[2:], *ffn_w[1])
        here = []
        new_move = Transfer(scatter_stages(links, here, [g.reshape(shape) for g in there]))
        grad_normed = advance(grad_normed, *before)
        *own, grad_normed = ffn_backward(grad_low, normed2, *products[:2], *ffn_w[0], grad_normed)
        here += [g.reshape(shape) for g in own]
        grad_normed = advance(grad_normed, new_move, *both)
        pulled, ffn_gain_grad = rms_pull(middle, ffn_gains[layer], grad_normed)
        grad = grad + pulled
        grad_low = grad.astype(jnp.bfloat16)
        output_grad = dot(attended, grad_low, TN).astype(jnp.bfloat16)
        attended_grad = dot(grad_low, output_w, NT).astype(jnp.bfloat16)
        attended_grad = advance(attended_grad, *both)
        qkv_grad = attention_backward(qkv, attended_grad, logsum, *where)
        qkv_grad = advance(qkv_grad, new_move, *both)
        qkv_w_grad = dot(qkv_grad, normed, TN).astype(jnp.bfloat16)
        blocks = attention_blocks(links, qkv_w_grad, output_grad, rows)
        ffn_move = new_move
        attn_move = Transfer(scatter_stages(links, blocks[:1], blocks[1:]))
        pulled, attn_gain_grad = rms_pull(hidden, attn_gains[layer], dot(qkv_grad, qkv_w))
        grad = grad + pulled
        if layer:
            grad = advance(grad, ffn_move, attn_move)
        moves[layer] = (attn_move, ffn_move)
        gain_terms[layer] = jnp.stack([attn_gain_grad, ffn_gain_grad])

    gains = links.sum_all(jnp.stack(gain_terms, axis=1))
    sums = [[] for _ in range(6)]
    for attn_move, ffn_move in moves:
        total = in_order(links, attn_move.finish()[0]).reshape(-1, width).astype(jnp.float32)
        a, b = rows[0], rows[0] + rows[1]
        sums[0].append(total[:a].T)
        sums[1].append(total[a:b].T)
        sums[2].append(total[b:])
        for kind, quarters in enumerate(ffn_move.finish()):
            total = in_order(links, quarters).reshape(-1, width).astype(jnp.float32)
            sums[3 + kind].append(total if kind == 2 else total.T)
    sums = [jnp.stack(values) for values in sums]
    return (final, grad[None], gains[0], *sums[:3], gains[1], *sums[3:])


def solution(mesh):
    placed = (
        P(("dp", "col"), None, None),
        P(("dp", "col"), None),
        P(("dp", "col"), None, None),
        P(),
        P(None, None, "col"),
        P(None, None, "col"),
        P(None, "col", None),
        P(),
        P(None, None, "col"),
        P(None, None, "col"),
        P(None, "col", None),
    )
    return jax.shard_map(
        functools.partial(per_device, mesh.shape["dp"], mesh.shape["col"]),
        mesh=mesh,
        in_specs=placed,
        out_specs=(
            P(("dp", "col"), None, None),
            P(("dp", "col"), None, None),
            P(),
            P(None, None, "col"),
            P(None, None, "col"),
            P(None, "col", None),
            P(),
            P(None, None, "col"),
            P(None, None, "col"),
            P(None, "col", None),
        ),
        check_vma=False,
    )
```

```python
import functools
import math

import jax
import jax.numpy as jnp
from jax import lax
from jax.experimental import pallas as pl
from jax.experimental.pallas import tpu as pltpu
from jax.sharding import PartitionSpec as P

QUERY_HEADS = 15
KEY_VALUE_HEADS = 5
HEAD_WIDTH = 64


epsilon = 1e-05
theta_base = 10000.0


def rms_norm(value_rows, gain):
    return (
        value_rows
        * lax.rsqrt(jnp.mean(value_rows * value_rows, axis=-1, keepdims=True) + epsilon)
        * gain
    )


def tables(segments, head_size):
    sequence_length = segments.shape[0]
    rows = jnp.arange(sequence_length, dtype=jnp.int32)
    before = jnp.sum((segments[None, :] < segments[:, None]).astype(jnp.int32), axis=1)
    places = (rows - before).astype(jnp.float32)
    half = head_size // 2
    freqs = jnp.exp(-math.log(theta_base) * (2.0 * jnp.arange(half, dtype=jnp.float32) / head_size))
    angles = places[:, None] * freqs[None, :]
    cosine, sine = jnp.cos(angles), jnp.sin(angles)
    return (jnp.tile(cosine, (1, 4)), jnp.tile(jnp.concatenate([-sine, sine], axis=1), (1, 2)))


BLOCK = 256
REACH = 384
MEGA = 2**20


def call(body, outs, args, after=(), scratch=(), limit=56, flops=0, nbytes=0, **grid):
    given = len(args)
    late = len(after)

    def run(*refs):
        body(*refs[:given], *refs[given + late :])

    specs = grid.pop("in_specs", None) or [pl.BlockSpec(memory_space=pltpu.VMEM)] * given
    out_specs = grid.pop("out_specs", None) or [pl.BlockSpec(memory_space=pltpu.VMEM)] * len(outs)
    return pl.pallas_call(
        run,
        out_shape=outs,
        in_specs=list(specs) + [pl.BlockSpec(memory_space=pl.ANY)] * late,
        out_specs=out_specs,
        scratch_shapes=list(scratch),
        compiler_params=pltpu.CompilerParams(vmem_limit_bytes=limit * MEGA),
        cost_estimate=pl.CostEstimate(flops=flops, bytes_accessed=nbytes, transcendentals=0),
        **grid,
    )(*args, *after)


def dot(left, right, dims=((1,), (0,))):
    return lax.dot_general(left, right, (dims, ((), ())), preferred_element_type=jnp.float32)


NT = ((1,), (1,))
TN = ((0,), (0,))


def swap_halves(value):
    lane = lax.broadcasted_iota(jnp.int32, value.shape, 1)
    return jnp.where(lane % HEAD_WIDTH < HEAD_WIDTH // 2, pltpu.roll(value, 96, 1), pltpu.roll(value, 32, 1))


def spans(length):
    for start in range(0, length, BLOCK):
        yield start, max(0, start - REACH + 1) // 128 * 128, start + BLOCK


def fill_bias(bias, seg_col, seg_row, length):
    for index, (start, low, high) in enumerate(spans(length)):
        shape = (high - low, BLOCK)
        key = lax.broadcasted_iota(jnp.int32, shape, 0) + low
        query = lax.broadcasted_iota(jnp.int32, shape, 1) + start
        same = seg_col[low:high, :] == seg_row[:, start : start + BLOCK]
        bias[index, : high - low, :] = jnp.where((key <= query) & same, 0.0, -1e30)


def attention_forward(raw, cosine, sine, seg_col, seg_row, after=()):
    length, width = raw.shape
    q_width = QUERY_HEADS * HEAD_WIDTH
    kv_width = KEY_VALUE_HEADS * HEAD_WIDTH
    group = QUERY_HEADS // KEY_VALUE_HEADS
    rotated = q_width + kv_width
    most = max(high - low for _, low, high in spans(length))

    def body(raw, cosine, sine, seg_col, seg_row, qkv, attended, logsum, bias, turned):
        for lane in range(0, rotated, 128):
            value = raw[:, lane : lane + 128]
            qkv[:, lane : lane + 128] = (value * cosine[...] + swap_halves(value) * sine[...]).astype(jnp.bfloat16)
        qkv[:, rotated:] = raw[:, rotated:].astype(jnp.bfloat16)
        fill_bias(bias, seg_col, seg_row, length)
        logsum[...] = jnp.zeros_like(logsum)
        turned[...] = raw[:, rotated:].T.astype(jnp.bfloat16)
        for index, (start, low, high) in enumerate(spans(length)):
            columns = []
            for head in range(QUERY_HEADS):
                kv = head // group
                query = qkv[start : start + BLOCK, head * HEAD_WIDTH : (head + 1) * HEAD_WIDTH] * 0.125
                at = q_width + kv * HEAD_WIDTH
                key = qkv[low:high, at : at + HEAD_WIDTH]
                logits = dot(key, query, NT) + bias[index, : high - low, :]
                peak = jnp.max(logits, axis=0, keepdims=True)
                expo = jnp.exp(logits - peak)
                total = jnp.sum(expo, axis=0, keepdims=True)
                value = turned[kv * HEAD_WIDTH : (kv + 1) * HEAD_WIDTH, low:high]
                columns.append(dot(value, expo.astype(jnp.bfloat16)) / total)
                logsum[head : head + 1, start : start + BLOCK] = peak + jnp.log(total)
            attended[start : start + BLOCK, :] = jnp.concatenate(columns, axis=0).T.astype(jnp.bfloat16)

    return call(
        body,
        [
            jax.ShapeDtypeStruct((length, width), jnp.bfloat16),
            jax.ShapeDtypeStruct((length, q_width), jnp.bfloat16),
            jax.ShapeDtypeStruct((16, length), jnp.float32),
        ],
        [raw, cosine, sine, seg_col, seg_row],
        after,
        [
            pltpu.VMEM((length // BLOCK, most, BLOCK), jnp.float32),
            pltpu.VMEM((kv_width, length), jnp.bfloat16),
        ],
        flops=15 * 10**9,
        nbytes=15 * MEGA,
    )


def attention_backward(qkv, grad, logsum, cosine, sine, seg_col, seg_row, after=()):
    length, width = qkv.shape
    q_width = QUERY_HEADS * HEAD_WIDTH
    kv_width = KEY_VALUE_HEADS * HEAD_WIDTH
    group = QUERY_HEADS // KEY_VALUE_HEADS
    rotated = q_width + kv_width
    most = max(high - low for _, low, high in spans(length))
    scale = 0.125

    def body(qkv, grad, logsum, cosine, sine, seg_col, seg_row, out, bias, turned, key_sum, value_sum, query_sum):
        fill_bias(bias, seg_col, seg_row, length)
        turned[...] = qkv[:, q_width:rotated].astype(jnp.float32).T.astype(jnp.bfloat16) * scale
        key_sum[...] = jnp.zeros_like(key_sum)
        value_sum[...] = jnp.zeros_like(value_sum)
        for index, (start, low, high) in enumerate(spans(length)):
            for head in range(QUERY_HEADS):
                kv = head // group
                lanes = slice(head * HEAD_WIDTH, (head + 1) * HEAD_WIDTH)
                query = qkv[start : start + BLOCK, lanes] * scale
                upstream = grad[start : start + BLOCK, lanes]
                at = q_width + kv * HEAD_WIDTH
                key = qkv[low:high, at : at + HEAD_WIDTH]
                value = qkv[low:high, at + kv_width : at + kv_width + HEAD_WIDTH]
                logits = dot(key, query, NT) + bias[index, : high - low, :]
                probs = jnp.exp(logits - logsum[head : head + 1, start : start + BLOCK])
                grad_probs = dot(value, upstream, NT)
                inner = jnp.sum(probs * grad_probs, axis=0, keepdims=True)
                grad_logits = (probs * (grad_probs - inner)).astype(jnp.bfloat16)
                value_sum[kv, low:high, :] += dot(probs.astype(jnp.bfloat16), upstream)
                key_sum[kv, low:high, :] += dot(grad_logits, query)
                query_sum[lanes, start : start + BLOCK] = dot(
                    turned[kv * HEAD_WIDTH : (kv + 1) * HEAD_WIDTH, low:high], grad_logits
                )
        raw = [query_sum[...].T] + [key_sum[kv] for kv in range(KEY_VALUE_HEADS)]
        raw = jnp.concatenate(raw, axis=1)
        for lane in range(0, rotated, 128):
            value = raw[:, lane : lane + 128]
            out[:, lane : lane + 128] = (value * cosine[...] - swap_halves(value) * sine[...]).astype(jnp.bfloat16)
        out[:, rotated:] = jnp.concatenate([value_sum[kv] for kv in range(KEY_VALUE_HEADS)], axis=1).astype(jnp.bfloat16)

    return call(
        body,
        [jax.ShapeDtypeStruct((length, width), jnp.bfloat16)],
        [qkv, grad, logsum, cosine, sine, seg_col, seg_row],
        after,
        [
            pltpu.VMEM((length // BLOCK, most, BLOCK), jnp.float32),
            pltpu.VMEM((kv_width, length), jnp.bfloat16),
            pltpu.VMEM((KEY_VALUE_HEADS, length, HEAD_WIDTH), jnp.float32),
            pltpu.VMEM((KEY_VALUE_HEADS, length, HEAD_WIDTH), jnp.float32),
            pltpu.VMEM((q_width, length), jnp.float32),
        ],
        flops=30 * 10**9,
        nbytes=20 * MEGA,
    )[0]


TILE = 256


def collect(pieces, store, semaphores):
    copies = [[], [], []]
    for kind in range(3):
        at = 0
        for piece in pieces:
            line, _, rows, _ = piece.shape
            for z in range(line):
                copies[kind].append(
                    pltpu.make_async_copy(
                        piece.at[z, kind], store.at[kind, pl.ds(at, rows)], semaphores.at[kind, len(copies[kind])]
                    )
                )
                at += rows
    return copies


def blocks_of(pieces):
    return sum(piece.shape[0] for piece in pieces)


def units_of(pieces):
    return sum(piece.shape[0] * piece.shape[2] for piece in pieces)


def ffn_forward(middle, normed, here, there):
    length, width = middle.shape
    units = units_of(here)
    tile = math.gcd(TILE, units)

    def body(middle, normed, *rest):
        pieces = rest[: len(here) + len(there)]
        out, gate_one, up_one, gate_two, up_two, store, semaphores = rest[len(pieces) :]
        halves = (pieces[: len(here)], pieces[len(here) :])
        copies = [collect(halves[i], store.at[i], semaphores.at[i]) for i in range(2)]
        for half in copies:
            for kind in half:
                for copy in kind:
                    copy.start()
        out[...] = middle[...]
        for i, (gate_out, upward_out) in enumerate(((gate_one, up_one), (gate_two, up_two))):
            for kind in copies[i]:
                for copy in kind:
                    copy.wait()

            def step(t, carry, i=i, gate_out=gate_out, upward_out=upward_out):
                rows = pl.ds(pl.multiple_of(t * tile, tile), tile)
                gate = dot(normed[...], store[i, 0, rows, :], NT)
                upward = dot(normed[...], store[i, 1, rows, :], NT)
                gate_out[:, rows] = gate.astype(jnp.bfloat16)
                upward_out[:, rows] = upward.astype(jnp.bfloat16)
                active = (gate * jax.nn.sigmoid(gate) * upward).astype(jnp.bfloat16)
                out[...] += dot(active, store[i, 2, rows, :])
                return carry

            lax.fori_loop(0, units // tile, step, 0)

    low = jax.ShapeDtypeStruct((length, units), jnp.bfloat16)
    return call(
        body,
        [jax.ShapeDtypeStruct((length, width), jnp.float32), low, low, low, low],
        [middle, normed, *here, *there],
        (),
        [
            pltpu.VMEM((2, 3, units, width), jnp.bfloat16),
            pltpu.SemaphoreType.DMA((2, 3, blocks_of(here))),
        ],
        in_specs=[pl.BlockSpec(memory_space=pltpu.VMEM)] * 2
        + [pl.BlockSpec(memory_space=pl.ANY)] * (len(here) + len(there)),
        flops=11 * 10**9,
        nbytes=30 * MEGA,
    )


def ffn_backward(grad_low, normed, gate, upward, pieces, earlier=None):
    length, width = normed.shape
    units = units_of(pieces)
    tile = math.gcd(TILE, units)
    before = [] if earlier is None else [earlier]

    def body(grad_low, normed, gate, upward, *rest):
        before, rest = rest[: len(rest) - 6 - len(pieces)], rest[len(rest) - 6 - len(pieces) :]
        parts, (grads, out, store, ready, semaphores, sent) = rest[: len(pieces)], rest[len(pieces) :]
        copies = collect(parts, store, semaphores)
        for kind in (2, 0, 1):
            for copy in copies[kind]:
                copy.start()
        out[...] = before[0][...] if before else jnp.zeros_like(out)
        for kind in (2, 0, 1):
            for copy in copies[kind]:
                copy.wait()

        def step(t, carry):
            rows = pl.ds(pl.multiple_of(t * tile, tile), tile)
            grad_active = dot(grad_low[...], store[2, rows, :], NT)
            gate_value = gate[:, rows].astype(jnp.float32)
            up_value = upward[:, rows].astype(jnp.float32)
            sigma = jax.nn.sigmoid(gate_value)
            silu = gate_value * sigma
            active = (silu * up_value).astype(jnp.bfloat16)
            grad_up = (grad_active * silu).astype(jnp.bfloat16)
            grad_gate = (grad_active * up_value * (sigma + silu * (1.0 - sigma))).astype(jnp.bfloat16)
            ready[2, rows, :] = dot(active, grad_low[...], TN).astype(jnp.bfloat16)
            ready[0, rows, :] = dot(grad_gate, normed[...], TN).astype(jnp.bfloat16)
            ready[1, rows, :] = dot(grad_up, normed[...], TN).astype(jnp.bfloat16)
            out[...] += dot(grad_gate, store[0, rows, :]) + dot(grad_up, store[1, rows, :])
            for kind in range(3):
                pltpu.make_async_copy(ready.at[kind, rows], grads.at[kind, rows], sent.at[kind, t]).start()
            return carry

        lax.fori_loop(0, units // tile, step, 0)
        for t in range(units // tile):
            rows = pl.ds(t * tile, tile)
            for kind in range(3):
                pltpu.make_async_copy(ready.at[kind, rows], grads.at[kind, rows], sent.at[kind, t]).wait()

    return call(
        body,
        [
            jax.ShapeDtypeStruct((3, units, width), jnp.bfloat16),
            jax.ShapeDtypeStruct((length, width), jnp.float32),
        ],
        [grad_low, normed, gate, upward, *before, *pieces],
        (),
        [
            pltpu.VMEM((3, units, width), jnp.bfloat16),
            pltpu.VMEM((3, units, width), jnp.bfloat16),
            pltpu.SemaphoreType.DMA((3, blocks_of(pieces))),
            pltpu.SemaphoreType.DMA((3, units // tile)),
        ],
        in_specs=[pl.BlockSpec(memory_space=pltpu.VMEM)] * (4 + len(before))
        + [pl.BlockSpec(memory_space=pl.ANY)] * len(pieces),
        out_specs=[pl.BlockSpec(memory_space=pl.ANY), pl.BlockSpec(memory_space=pltpu.VMEM)],
        flops=11 * 10**9,
        nbytes=30 * MEGA,
    )


class Links:
    def __init__(self, dp, col):
        self.dp, self.col, self.line = dp, col, col // 2
        self.rest = [list(range(r, dp, 4)) for r in range(4)]
        self.quarter = lax.axis_index("dp") % 4
        self.core = lax.axis_index("col") % 2
        self.chip = lax.axis_index("col") // 2

    def x(self, value):
        return lax.ppermute(value, "dp", [(i, i ^ 1) for i in range(self.dp)])

    def y(self, value):
        return lax.ppermute(value, "dp", [(i, i ^ 2) for i in range(self.dp)])

    def other_core(self, value):
        return lax.ppermute(value, "col", [(i, i ^ 1) for i in range(self.col)])

    def send(self, value, step):
        return lax.ppermute(value, "col", [(i, (i + 2 * step) % self.col) for i in range(self.col)])

    def sum_all(self, value):
        for axis, size in (("dp", self.dp), ("col", self.col)):
            step = 1
            while step < size:
                value = value + lax.ppermute(value, axis, [(i, i ^ step) for i in range(size)])
                step *= 2
        return value


def add(*terms):
    total = terms[0].astype(jnp.float32)
    for term in terms[1:]:
        total = total + term.astype(jnp.float32)
    return total.astype(jnp.bfloat16)


class Transfer:
    def __init__(self, stages):
        self.stages = stages
        self.result = None
        self.flying = next(stages)

    def advance(self, arrays=None):
        try:
            self.flying = self.stages.send(self.flying if arrays is None else arrays)
        except StopIteration as stop:
            self.flying, self.result = [], stop.value

    def finish(self):
        while self.result is None:
            self.advance()
        return self.result


def advance(value, *transfers):
    flying = [transfer.flying for transfer in transfers]
    value, flying = lax.optimization_barrier((value, flying))
    for transfer, arrays in zip(transfers, flying, strict=True):
        transfer.advance(arrays)
    return value


def gather_stages(links, part):
    far = yield [links.send(part, -step) for step in range(1, links.line)]
    own = jnp.roll(jnp.stack([part, *far]), links.chip, axis=0)
    half = links.line // 2
    from_x, from_y, own_c = yield [links.x(own), links.y(own), links.other_core(own)]
    low, high, x_c, y_c = yield [
        links.y(from_x[:half]),
        links.x(from_y[half:]),
        links.other_core(from_x),
        links.other_core(from_y),
    ]
    low_c, high_c = yield [links.other_core(low), links.other_core(high)]
    return [[own, from_x, from_y, low, high], [own_c, x_c, y_c, low_c, high_c]]


def scatter_stages(links, kept, there, pick):
    (got,) = yield [links.other_core(there)]
    here = kept[0]
    half = links.line // 2
    low, high = slice(0, half), slice(half, links.line)

    def part(place, piece):
        return add(pick(here, place, piece), pick(got, place, piece))

    from_x, from_y = yield [
        links.x(jnp.stack([part(3, high), part(1, high)])),
        links.y(jnp.stack([part(3, low), part(2, low)])),
    ]
    x_low, y_high = yield [
        links.x(add(pick(here, 1, low), pick(got, 1, low), from_y[0])),
        links.y(add(pick(here, 2, high), pick(got, 2, high), from_x[0])),
    ]
    own = jnp.concatenate(
        [
            add(pick(here, 0, low), pick(got, 0, low), from_y[1], x_low),
            add(pick(here, 0, high), pick(got, 0, high), from_x[1], y_high),
        ]
    )

    def chip(step):
        return lax.dynamic_index_in_dim(own, (links.chip + step) % links.line, 0, False)

    far = yield [links.send(chip(step), step) for step in range(1, links.line)]
    total = add(chip(0), *far)
    if links.dp > 4:
        total = lax.psum(total, "dp", axis_index_groups=links.rest)
    at_x, at_y = yield [links.x(total), links.y(total)]
    (at_both,) = yield [links.y(at_x)]
    return (total, at_x, at_y, at_both)


def in_order(links, quarters):
    whole = jnp.zeros((4, *quarters[0].shape), quarters[0].dtype)
    for place, block in enumerate(quarters):
        whole = lax.dynamic_update_index_in_dim(whole, block, links.quarter ^ place, 0)
    return whole


def own_quarter(links, packed, axis):
    shape = packed.shape[:axis] + (4, packed.shape[axis] // 4) + packed.shape[axis + 1 :]
    return lax.dynamic_index_in_dim(packed.reshape(shape), links.quarter, axis, False)


def attention_weights(links, blocks, rows):
    part, width = blocks[0][0].shape[1:]
    half = links.line // 2
    whole = jnp.zeros((links.line, 2, 4, part, width), jnp.bfloat16)
    for core in range(2):
        for place, start, block in zip((0, 1, 2, 3, 3), (0, 0, 0, 0, half), blocks[core], strict=True):
            whole = lax.dynamic_update_slice(
                whole, block[:, None, None], (start, links.core ^ core, links.quarter ^ place, 0, 0)
            )
    whole = whole.reshape(links.col, 4 * part, width)
    a, b = rows[0], rows[0] + rows[1]
    return (
        jnp.concatenate([whole[:, :a].reshape(-1, width), whole[:, a:b].reshape(-1, width)]),
        whole[:, b:].reshape(-1, width),
    )


def attention_shares(links, qkv_grad, output_grad, rows):
    width = output_grad.shape[1]
    cut = rows[0] * links.col
    parts = [g.reshape(links.col, -1, width) for g in (qkv_grad[:cut], qkv_grad[cut:], output_grad)]
    whole = jnp.concatenate(parts, axis=1).reshape(links.line, 2, 4, -1, width)
    return [lax.dynamic_index_in_dim(whole, links.core ^ core, 1, False) for core in range(2)]


def ffn_pieces(blocks):
    if blocks[0].shape[2] % 16 == 0:
        return blocks
    line, kinds, _, width = blocks[0].shape
    joined = [jnp.moveaxis(block, 1, 0).reshape(kinds, -1, width) for block in blocks]
    return [jnp.concatenate(joined, axis=1)[None]]


def rms_pull(value, gain, grad):
    scale = lax.rsqrt(jnp.mean(value * value, axis=-1, keepdims=True) + epsilon)
    scaled = value * scale
    pulled = grad * gain
    inner = jnp.mean(pulled * scaled, axis=-1, keepdims=True)
    return scale * (pulled - scaled * inner), jnp.sum(grad * scaled, axis=0)


def per_device(
    dp,
    col,
    inputs,
    segment_ids,
    cotangent,
    attn_gain,
    query_weight,
    key_value_weight,
    output_weight,
    ffn_gain,
    gate_weight,
    upward_weight,
    down_weight,
):
    links = Links(dp, col)
    layers, width = attn_gain.shape
    rows = (query_weight.shape[2], key_value_weight.shape[2], output_weight.shape[1])
    segments = segment_ids[0]
    where = (*tables(segments, HEAD_WIDTH), segments[:, None], segments[None, :])
    attn_gains = attn_gain.astype(jnp.float32)
    ffn_gains = ffn_gain.astype(jnp.float32)

    weights = []
    previous = None
    for layer in range(layers):
        attn_part = jnp.concatenate([query_weight[layer].T, key_value_weight[layer].T, output_weight[layer]])
        ffn_part = jnp.stack([gate_weight[layer].T, upward_weight[layer].T, down_weight[layer]])
        attn_part = own_quarter(links, attn_part, 0)
        ffn_part = own_quarter(links, ffn_part, 1)
        weights.append((attn_part, ffn_part))

    hidden = inputs[0].astype(jnp.float32)
    saved = []
    attn_move = Transfer(gather_stages(links, weights[0][0]))
    for layer in range(layers):
        ffn_part = weights[layer][1]
        if layer == 0:
            ffn_part = advance(ffn_part, attn_move)
            ffn_move = Transfer(gather_stages(links, ffn_part))
            hidden = advance(hidden, attn_move)
            hidden = advance(hidden, attn_move)
        qkv_w, output_w = attention_weights(links, attn_move.finish(), rows)
        normed = rms_norm(hidden, attn_gains[layer]).astype(jnp.bfloat16)
        raw = dot(normed, qkv_w, NT)
        raw = advance(raw, ffn_move)
        if layer + 1 < layers:
            attn_part, raw = lax.optimization_barrier((weights[layer + 1][0], raw))
            attn_move = Transfer(gather_stages(links, attn_part))
        qkv, attended, logsum = attention_forward(raw, *where)
        middle = hidden + dot(attended, output_w)
        normed2 = rms_norm(middle, ffn_gains[layer]).astype(jnp.bfloat16)
        normed2 = advance(normed2, ffn_move)
        if layer + 1 < layers:
            ffn_part = advance(weights[layer + 1][1], attn_move)
            next_move = Transfer(gather_stages(links, ffn_part))
        ffn_w = [ffn_pieces(half) for half in ffn_move.finish()]
        if layer + 1 < layers:
            normed2 = advance(normed2, attn_move)
        result, *products = ffn_forward(middle, normed2, *ffn_w)
        saved.append((hidden, normed, qkv, attended, logsum, middle, normed2, products, qkv_w, output_w, ffn_w))
        hidden = result
        if layer + 1 < layers:
            hidden = advance(hidden, attn_move)
            ffn_move = next_move
    final = hidden.astype(jnp.bfloat16)[None]

    grad = cotangent[0].astype(jnp.float32)
    moves = [None] * layers
    gain_terms = [None] * layers
    attn_move = ffn_move = None

    def ffn_pick(share, place, part):
        return jnp.moveaxis(share.reshape(3, 4, links.line, -1, width)[:, place, part], 1, 0)

    def attn_pick(share, place, part):
        return lax.dynamic_index_in_dim(share[part], links.quarter ^ place, 1, False)

    for layer in reversed(range(layers)):
        hidden, normed, qkv, attended, logsum, middle, normed2, products, qkv_w, output_w, ffn_w = saved[layer]
        both = [] if attn_move is None else [ffn_move, attn_move]
        grad_low = grad.astype(jnp.bfloat16)
        there, grad_normed = ffn_backward(grad_low, normed2, *products[2:], ffn_w[1])
        here = []
        new_move = Transfer(scatter_stages(links, here, there, ffn_pick))
        grad_normed = advance(grad_normed, *both[1:])
        own, grad_normed = ffn_backward(grad_low, normed2, *products[:2], ffn_w[0], grad_normed)
        here.append(own)
        grad_normed = advance(grad_normed, new_move, *both)
        pulled, ffn_gain_grad = rms_pull(middle, ffn_gains[layer], grad_normed)
        grad = grad + pulled
        grad_low = grad.astype(jnp.bfloat16)
        output_grad = dot(attended, grad_low, TN).astype(jnp.bfloat16)
        attended_grad = dot(grad_low, output_w, NT).astype(jnp.bfloat16)
        attended_grad = advance(attended_grad, *both)
        qkv_grad = attention_backward(qkv, attended_grad, logsum, *where)
        qkv_grad = advance(qkv_grad, new_move, *both)
        qkv_w_grad = dot(qkv_grad, normed, TN).astype(jnp.bfloat16)
        ours, others = attention_shares(links, qkv_w_grad, output_grad, rows)
        ffn_move = new_move
        attn_move = Transfer(scatter_stages(links, [ours], others, attn_pick))
        pulled, attn_gain_grad = rms_pull(hidden, attn_gains[layer], dot(qkv_grad, qkv_w))
        grad = grad + pulled
        if layer:
            grad = advance(grad, ffn_move, attn_move)
        moves[layer] = (attn_move, ffn_move)
        gain_terms[layer] = jnp.stack([attn_gain_grad, ffn_gain_grad])

    gains = links.sum_all(jnp.stack(gain_terms, axis=1))
    sums = [[] for _ in range(6)]
    for attn_move, ffn_move in moves:
        total = in_order(links, attn_move.finish()).reshape(-1, width).astype(jnp.float32)
        a, b = rows[0], rows[0] + rows[1]
        sums[0].append(total[:a].T)
        sums[1].append(total[a:b].T)
        sums[2].append(total[b:])
        quarters = in_order(links, ffn_move.finish())
        for kind in range(3):
            total = quarters[:, kind].reshape(-1, width).astype(jnp.float32)
            sums[3 + kind].append(total if kind == 2 else total.T)
    sums = [jnp.stack(values) for values in sums]
    return (final, grad[None], gains[0], *sums[:3], gains[1], *sums[3:])


def solution(mesh):
    placed = (
        P(("dp", "col"), None, None),
        P(("dp", "col"), None),
        P(("dp", "col"), None, None),
        P(),
        P(None, None, "col"),
        P(None, None, "col"),
        P(None, "col", None),
        P(),
        P(None, None, "col"),
        P(None, None, "col"),
        P(None, "col", None),
    )
    return jax.shard_map(
        functools.partial(per_device, mesh.shape["dp"], mesh.shape["col"]),
        mesh=mesh,
        in_specs=placed,
        out_specs=(
            P(("dp", "col"), None, None),
            P(("dp", "col"), None, None),
            P(),
            P(None, None, "col"),
            P(None, None, "col"),
            P(None, "col", None),
            P(),
            P(None, None, "col"),
            P(None, None, "col"),
            P(None, "col", None),
        ),
        check_vma=False,
    )
```

```python
import functools
import math

import jax
import jax.numpy as jnp
from jax import lax
from jax.experimental import pallas as pl
from jax.experimental.pallas import tpu as pltpu
from jax.sharding import PartitionSpec as P

QUERY_HEADS = 15
KEY_VALUE_HEADS = 5
HEAD_WIDTH = 64


epsilon = 1e-05
theta_base = 10000.0


def rms_norm(value_rows, gain):
    return (
        value_rows
        * lax.rsqrt(jnp.mean(value_rows * value_rows, axis=-1, keepdims=True) + epsilon)
        * gain
    )


def tables(segments, head_size):
    sequence_length = segments.shape[0]
    rows = jnp.arange(sequence_length, dtype=jnp.int32)
    before = jnp.sum((segments[None, :] < segments[:, None]).astype(jnp.int32), axis=1)
    places = (rows - before).astype(jnp.float32)
    half = head_size // 2
    freqs = jnp.exp(-math.log(theta_base) * (2.0 * jnp.arange(half, dtype=jnp.float32) / head_size))
    angles = places[:, None] * freqs[None, :]
    cosine, sine = jnp.cos(angles), jnp.sin(angles)
    return (jnp.tile(cosine, (1, 4)), jnp.tile(jnp.concatenate([-sine, sine], axis=1), (1, 2)))


BLOCK = 256
REACH = 384
MEGA = 2**20


def call(body, outs, args, after=(), scratch=(), limit=56, flops=0, nbytes=0, **grid):
    given = len(args)
    late = len(after)

    def run(*refs):
        body(*refs[:given], *refs[given + late :])

    specs = grid.pop("in_specs", None) or [pl.BlockSpec(memory_space=pltpu.VMEM)] * given
    out_specs = grid.pop("out_specs", None) or [pl.BlockSpec(memory_space=pltpu.VMEM)] * len(outs)
    return pl.pallas_call(
        run,
        out_shape=outs,
        in_specs=list(specs) + [pl.BlockSpec(memory_space=pl.ANY)] * late,
        out_specs=out_specs,
        scratch_shapes=list(scratch),
        compiler_params=pltpu.CompilerParams(vmem_limit_bytes=limit * MEGA),
        cost_estimate=pl.CostEstimate(flops=flops, bytes_accessed=nbytes, transcendentals=0),
        **grid,
    )(*args, *after)


def dot(left, right, dims=((1,), (0,))):
    return lax.dot_general(left, right, (dims, ((), ())), preferred_element_type=jnp.float32)


NT = ((1,), (1,))
TN = ((0,), (0,))


def swap_halves(value):
    lane = lax.broadcasted_iota(jnp.int32, value.shape, 1)
    return jnp.where(lane % HEAD_WIDTH < HEAD_WIDTH // 2, pltpu.roll(value, 96, 1), pltpu.roll(value, 32, 1))


def spans(length):
    for start in range(0, length, BLOCK):
        yield start, max(0, start - REACH + 1) // 128 * 128, start + BLOCK


def fill_bias(bias, seg_col, seg_row, length):
    for index, (start, low, high) in enumerate(spans(length)):
        shape = (high - low, BLOCK)
        key = lax.broadcasted_iota(jnp.int32, shape, 0) + low
        query = lax.broadcasted_iota(jnp.int32, shape, 1) + start
        same = seg_col[low:high, :] == seg_row[:, start : start + BLOCK]
        bias[index, : high - low, :] = jnp.where((key <= query) & same, 0.0, -1e30)


def scale_of(value):
    return lax.rsqrt(jnp.mean(value * value, axis=-1, keepdims=True) + epsilon)


def attention_forward(hidden, gain, next_gain, qkv_w, output_w, cosine, sine, seg_col, seg_row):
    length, model = hidden.shape
    width = qkv_w.shape[0]
    q_width = QUERY_HEADS * HEAD_WIDTH
    kv_width = KEY_VALUE_HEADS * HEAD_WIDTH
    group = QUERY_HEADS // KEY_VALUE_HEADS
    rotated = q_width + kv_width
    most = max(high - low for _, low, high in spans(length))

    def body(hidden, gain, next_gain, qkv_w, output_w, cosine, sine, seg_col, seg_row, *rest):
        normed, qkv, attended, logsum, middle, normed2, raw, bias, turned = rest
        value = hidden[...]
        normed[...] = (value * scale_of(value) * gain[...]).astype(jnp.bfloat16)
        raw[...] = dot(normed[...], qkv_w[...], NT)
        for lane in range(0, rotated, 128):
            value = raw[:, lane : lane + 128]
            qkv[:, lane : lane + 128] = (value * cosine[...] + swap_halves(value) * sine[...]).astype(jnp.bfloat16)
        qkv[:, rotated:] = raw[:, rotated:].astype(jnp.bfloat16)
        fill_bias(bias, seg_col, seg_row, length)
        logsum[...] = jnp.zeros_like(logsum)
        turned[...] = raw[:, rotated:].T.astype(jnp.bfloat16)
        for index, (start, low, high) in enumerate(spans(length)):
            columns = []
            for head in range(QUERY_HEADS):
                kv = head // group
                query = qkv[start : start + BLOCK, head * HEAD_WIDTH : (head + 1) * HEAD_WIDTH] * 0.125
                at = q_width + kv * HEAD_WIDTH
                key = qkv[low:high, at : at + HEAD_WIDTH]
                logits = dot(key, query, NT) + bias[index, : high - low, :]
                peak = jnp.max(logits, axis=0, keepdims=True)
                expo = jnp.exp(logits - peak)
                total = jnp.sum(expo, axis=0, keepdims=True)
                value = turned[kv * HEAD_WIDTH : (kv + 1) * HEAD_WIDTH, low:high]
                columns.append(dot(value, expo.astype(jnp.bfloat16)) / total)
                logsum[head : head + 1, start : start + BLOCK] = peak + jnp.log(total)
            attended[start : start + BLOCK, :] = jnp.concatenate(columns, axis=0).T.astype(jnp.bfloat16)
        value = hidden[...] + dot(attended[...], output_w[...])
        middle[...] = value
        normed2[...] = (value * scale_of(value) * next_gain[...]).astype(jnp.bfloat16)

    low = jax.ShapeDtypeStruct((length, model), jnp.bfloat16)
    return call(
        body,
        [
            low,
            jax.ShapeDtypeStruct((length, width), jnp.bfloat16),
            jax.ShapeDtypeStruct((length, q_width), jnp.bfloat16),
            jax.ShapeDtypeStruct((16, length), jnp.float32),
            jax.ShapeDtypeStruct((length, model), jnp.float32),
            low,
        ],
        [hidden, gain, next_gain, qkv_w, output_w, cosine, sine, seg_col, seg_row],
        (),
        [
            pltpu.VMEM((length, width), jnp.float32),
            pltpu.VMEM((length // BLOCK, most, BLOCK), jnp.float32),
            pltpu.VMEM((kv_width, length), jnp.bfloat16),
        ],
        flops=20 * 10**9,
        nbytes=20 * MEGA,
    )


def attention_backward(
    grad, grad_normed2, hidden, normed, qkv, attended, logsum, middle, gain, next_gain, qkv_w, output_w, *where
):
    length, model = hidden.shape
    width = qkv.shape[1]
    q_width = QUERY_HEADS * HEAD_WIDTH
    kv_width = KEY_VALUE_HEADS * HEAD_WIDTH
    group = QUERY_HEADS // KEY_VALUE_HEADS
    rotated = q_width + kv_width
    most = max(high - low for _, low, high in spans(length))

    def body(grad, grad_normed2, hidden, normed, qkv, attended, logsum, middle, gain, next_gain, qkv_w, output_w, *rest):
        cosine, sine, seg_col, seg_row, *rest = rest
        qkv_w_grad, output_w_grad, out, out_low, gain_grad, next_gain_grad, *rest = rest
        bias, turned, key_sum, value_sum, query_sum, upstream_all, qkv_grad = rest

        def pull(value, g, upstream, gain_out):
            scale = scale_of(value)
            scaled = value * scale
            gain_out[...] = jnp.sum(upstream * scaled, axis=0, keepdims=True)
            pulled = upstream * g
            return scale * (pulled - scaled * jnp.mean(pulled * scaled, axis=-1, keepdims=True))

        out[...] = grad[...] + pull(middle[...], next_gain[...], grad_normed2[...], next_gain_grad)
        out_low[...] = out[...].astype(jnp.bfloat16)
        output_w_grad[...] = dot(attended[...], out_low[...], TN).astype(jnp.bfloat16)
        upstream_all[...] = dot(out_low[...], output_w[...], NT).astype(jnp.bfloat16)
        fill_bias(bias, seg_col, seg_row, length)
        turned[...] = qkv[:, q_width:rotated].astype(jnp.float32).T.astype(jnp.bfloat16) * 0.125
        key_sum[...] = jnp.zeros_like(key_sum)
        value_sum[...] = jnp.zeros_like(value_sum)
        for index, (start, low, high) in enumerate(spans(length)):
            for head in range(QUERY_HEADS):
                kv = head // group
                lanes = slice(head * HEAD_WIDTH, (head + 1) * HEAD_WIDTH)
                query = qkv[start : start + BLOCK, lanes] * 0.125
                upstream = upstream_all[start : start + BLOCK, lanes]
                at = q_width + kv * HEAD_WIDTH
                key = qkv[low:high, at : at + HEAD_WIDTH]
                value = qkv[low:high, at + kv_width : at + kv_width + HEAD_WIDTH]
                logits = dot(key, query, NT) + bias[index, : high - low, :]
                probs = jnp.exp(logits - logsum[head : head + 1, start : start + BLOCK])
                grad_probs = dot(value, upstream, NT)
                inner = jnp.sum(probs * grad_probs, axis=0, keepdims=True)
                grad_logits = (probs * (grad_probs - inner)).astype(jnp.bfloat16)
                value_sum[kv, low:high, :] += dot(probs.astype(jnp.bfloat16), upstream)
                key_sum[kv, low:high, :] += dot(grad_logits, query)
                query_sum[lanes, start : start + BLOCK] = dot(
                    turned[kv * HEAD_WIDTH : (kv + 1) * HEAD_WIDTH, low:high], grad_logits
                )
        raw = [query_sum[...].T] + [key_sum[kv] for kv in range(KEY_VALUE_HEADS)]
        raw = jnp.concatenate(raw, axis=1)
        for lane in range(0, rotated, 128):
            value = raw[:, lane : lane + 128]
            qkv_grad[:, lane : lane + 128] = (value * cosine[...] - swap_halves(value) * sine[...]).astype(jnp.bfloat16)
        values = [value_sum[kv] for kv in range(KEY_VALUE_HEADS)]
        qkv_grad[:, rotated:] = jnp.concatenate(values, axis=1).astype(jnp.bfloat16)
        qkv_w_grad[...] = dot(qkv_grad[...], normed[...], TN).astype(jnp.bfloat16)
        pulled = pull(hidden[...], gain[...], dot(qkv_grad[...], qkv_w[...]), gain_grad)
        out[...] += pulled
        out_low[...] = out[...].astype(jnp.bfloat16)

    gains = jax.ShapeDtypeStruct((1, model), jnp.float32)
    args = [grad, grad_normed2, hidden, normed, qkv, attended, logsum, middle, gain, next_gain, qkv_w, output_w, *where]
    return call(
        body,
        [
            jax.ShapeDtypeStruct(qkv_w.shape, jnp.bfloat16),
            jax.ShapeDtypeStruct(output_w.shape, jnp.bfloat16),
            jax.ShapeDtypeStruct((length, model), jnp.float32),
            jax.ShapeDtypeStruct((length, model), jnp.bfloat16),
            gains,
            gains,
        ],
        args,
        (),
        [
            pltpu.VMEM((length // BLOCK, most, BLOCK), jnp.float32),
            pltpu.VMEM((kv_width, length), jnp.bfloat16),
            pltpu.VMEM((KEY_VALUE_HEADS, length, HEAD_WIDTH), jnp.float32),
            pltpu.VMEM((KEY_VALUE_HEADS, length, HEAD_WIDTH), jnp.float32),
            pltpu.VMEM((q_width, length), jnp.float32),
            pltpu.VMEM((length, q_width), jnp.bfloat16),
            pltpu.VMEM((length, width), jnp.bfloat16),
        ],
        flops=35 * 10**9,
        nbytes=40 * MEGA,
    )


TILE = 256


def block_list(pieces):
    blocks, at = [], 0
    for piece in pieces:
        for z in range(piece.shape[0]):
            blocks.append((piece, z, at, at + piece.shape[2]))
            at += piece.shape[2]
    return blocks, at


def collect(pieces, store, semaphores):
    blocks, _ = block_list(pieces)
    copies = [
        [
            pltpu.make_async_copy(piece.at[z, kind], store.at[kind, pl.ds(at, end - at)], semaphores.at[kind, i])
            for kind in range(3)
        ]
        for i, (piece, z, at, end) in enumerate(blocks)
    ]
    for block in copies:
        for copy in block:
            copy.start()
    waited = [0]

    def until(limit):
        while waited[0] < len(blocks) and blocks[waited[0]][2] < limit:
            for copy in copies[waited[0]]:
                copy.wait()
            waited[0] += 1

    return until


def ffn_forward(middle, normed, here, there):
    length, width = middle.shape
    blocks, units = block_list(here)
    tile = math.gcd(TILE, units)

    def body(middle, normed, *rest):
        pieces = rest[: len(here) + len(there)]
        out, gate_one, up_one, gate_two, up_two, store, semaphores = rest[len(pieces) :]
        untils = [
            collect(half, store.at[i], semaphores.at[i])
            for i, half in enumerate((pieces[: len(here)], pieces[len(here) :]))
        ]
        out[...] = middle[...]
        for i, (gate_out, upward_out) in enumerate(((gate_one, up_one), (gate_two, up_two))):
            for at in range(0, units, tile):
                untils[i](at + tile)
                rows = slice(at, at + tile)
                gate = dot(normed[...], store[i, 0, rows, :], NT)
                upward = dot(normed[...], store[i, 1, rows, :], NT)
                gate_out[:, rows] = gate.astype(jnp.bfloat16)
                upward_out[:, rows] = upward.astype(jnp.bfloat16)
                active = (gate * jax.nn.sigmoid(gate) * upward).astype(jnp.bfloat16)
                out[...] += dot(active, store[i, 2, rows, :])

    low = jax.ShapeDtypeStruct((length, units), jnp.bfloat16)
    return call(
        body,
        [jax.ShapeDtypeStruct((length, width), jnp.float32), low, low, low, low],
        [middle, normed, *here, *there],
        (),
        [
            pltpu.VMEM((2, 3, units, width), jnp.bfloat16),
            pltpu.SemaphoreType.DMA((2, 3, len(blocks))),
        ],
        in_specs=[pl.BlockSpec(memory_space=pltpu.VMEM)] * 2
        + [pl.BlockSpec(memory_space=pl.ANY)] * (len(here) + len(there)),
        flops=11 * 10**9,
        nbytes=30 * MEGA,
    )


def ffn_backward(grad_low, normed, gate, upward, pieces, earlier=None):
    length, width = normed.shape
    blocks, units = block_list(pieces)
    rows_of_block = blocks[0][3]
    tile = math.gcd(TILE, units)
    before = [] if earlier is None else [earlier]

    def body(grad_low, normed, gate, upward, *rest):
        before, rest = rest[: len(rest) - 6 - len(pieces)], rest[len(rest) - 6 - len(pieces) :]
        parts, (grads, out, store, ready, semaphores, sent) = rest[: len(pieces)], rest[len(pieces) :]
        until = collect(parts, store, semaphores)
        out[...] = before[0][...] if before else jnp.zeros_like(out)
        sends = []
        for at in range(0, units, tile):
            until(at + tile)
            rows = slice(at, at + tile)
            grad_active = dot(grad_low[...], store[2, rows, :], NT)
            gate_value = gate[:, rows].astype(jnp.float32)
            up_value = upward[:, rows].astype(jnp.float32)
            sigma = jax.nn.sigmoid(gate_value)
            silu = gate_value * sigma
            active = (silu * up_value).astype(jnp.bfloat16)
            grad_up = (grad_active * silu).astype(jnp.bfloat16)
            grad_gate = (grad_active * up_value * (sigma + silu * (1.0 - sigma))).astype(jnp.bfloat16)
            ready[2, rows, :] = dot(active, grad_low[...], TN).astype(jnp.bfloat16)
            ready[0, rows, :] = dot(grad_gate, normed[...], TN).astype(jnp.bfloat16)
            ready[1, rows, :] = dot(grad_up, normed[...], TN).astype(jnp.bfloat16)
            out[...] += dot(grad_gate, store[0, rows, :]) + dot(grad_up, store[1, rows, :])
            while len(sends) < len(blocks) and blocks[len(sends)][3] <= at + tile:
                i = len(sends)
                span = pl.ds(blocks[i][2], rows_of_block)
                sends.append(
                    [
                        pltpu.make_async_copy(ready.at[kind, span], grads.at[i, kind], sent.at[kind, i])
                        for kind in range(3)
                    ]
                )
                for copy in sends[-1]:
                    copy.start()
        for block in sends:
            for copy in block:
                copy.wait()

    return call(
        body,
        [
            jax.ShapeDtypeStruct((len(blocks), 3, rows_of_block, width), jnp.bfloat16),
            jax.ShapeDtypeStruct((length, width), jnp.float32),
        ],
        [grad_low, normed, gate, upward, *before, *pieces],
        (),
        [
            pltpu.VMEM((3, units, width), jnp.bfloat16),
            pltpu.VMEM((3, units, width), jnp.bfloat16),
            pltpu.SemaphoreType.DMA((3, len(blocks))),
            pltpu.SemaphoreType.DMA((3, len(blocks))),
        ],
        in_specs=[pl.BlockSpec(memory_space=pltpu.VMEM)] * (4 + len(before))
        + [pl.BlockSpec(memory_space=pl.ANY)] * len(pieces),
        out_specs=[pl.BlockSpec(memory_space=pl.ANY), pl.BlockSpec(memory_space=pltpu.VMEM)],
        flops=11 * 10**9,
        nbytes=30 * MEGA,
    )


class Links:
    def __init__(self, dp, col):
        self.dp, self.col, self.line = dp, col, col // 2
        self.rest = [list(range(r, dp, 4)) for r in range(4)]
        self.quarter = lax.axis_index("dp") % 4
        self.core = lax.axis_index("col") % 2
        self.chip = lax.axis_index("col") // 2

    def x(self, value):
        return lax.ppermute(value, "dp", [(i, i ^ 1) for i in range(self.dp)])

    def y(self, value):
        return lax.ppermute(value, "dp", [(i, i ^ 2) for i in range(self.dp)])

    def other_core(self, value):
        return lax.ppermute(value, "col", [(i, i ^ 1) for i in range(self.col)])

    def both(self, value):
        return lax.ppermute(value, "dp", [(i, i ^ 3) for i in range(self.dp)])

    def send(self, value, step):
        return lax.ppermute(value, "col", [(i, (i + 2 * step) % self.col) for i in range(self.col)])

    def sum_all(self, value):
        for axis, size in (("dp", self.dp), ("col", self.col)):
            step = 1
            while step < size:
                value = value + lax.ppermute(value, axis, [(i, i ^ step) for i in range(size)])
                step *= 2
        return value


def add(*terms):
    total = terms[0].astype(jnp.float32)
    for term in terms[1:]:
        total = total + term.astype(jnp.float32)
    return total.astype(jnp.bfloat16)


class Transfer:
    def __init__(self, stages):
        self.stages = stages
        self.result = None
        self.flying = next(stages)

    def advance(self, arrays=None):
        try:
            self.flying = self.stages.send(self.flying if arrays is None else arrays)
        except StopIteration as stop:
            self.flying, self.result = [], stop.value

    def finish(self):
        while self.result is None:
            self.advance()
        return self.result


def advance(value, *transfers):
    flying = [transfer.flying for transfer in transfers]
    value, flying = lax.optimization_barrier((value, flying))
    for transfer, arrays in zip(transfers, flying, strict=True):
        transfer.advance(arrays)
    return value


def gather_stages(links, part):
    far = yield [links.send(part, -step) for step in range(1, links.line)]
    own = jnp.stack([part, *far])
    half = links.line // 2
    from_x, from_y, own_c = yield [links.x(own), links.y(own), links.other_core(own)]
    low, high, x_c, y_c = yield [
        links.y(from_x[:half]),
        links.x(from_y[half:]),
        links.other_core(from_x),
        links.other_core(from_y),
    ]
    low_c, high_c = yield [links.other_core(low), links.other_core(high)]
    return [[own, from_x, from_y, low, high], [own_c, x_c, y_c, low_c, high_c]]


def scatter_stages(links, kept, there, pick, in_line):
    (got,) = yield [links.other_core(there)]
    here = kept[0]
    half = links.line // 2
    low, high = slice(0, half), slice(half, links.line)

    def part(place, piece):
        return add(pick(here, place, piece), pick(got, place, piece))

    from_x, from_y = yield [
        links.x(jnp.stack([part(3, high), part(1, high)])),
        links.y(jnp.stack([part(3, low), part(2, low)])),
    ]
    x_low, y_high = yield [
        links.x(add(pick(here, 1, low), pick(got, 1, low), from_y[0])),
        links.y(add(pick(here, 2, high), pick(got, 2, high), from_x[0])),
    ]
    own = jnp.concatenate(
        [
            add(pick(here, 0, low), pick(got, 0, low), from_y[1], x_low),
            add(pick(here, 0, high), pick(got, 0, high), from_x[1], y_high),
        ]
    )

    def chip(step):
        if not in_line:
            return own[step]
        return lax.dynamic_index_in_dim(own, (links.chip + step) % links.line, 0, False)

    far = yield [links.send(chip(step), step) for step in range(1, links.line)]
    total = add(chip(0), *far)
    if links.dp > 4:
        total = lax.psum(total, "dp", axis_index_groups=links.rest)
    others = yield [links.x(total), links.y(total), links.both(total)]
    return (total, *others)


def in_order(links, quarters):
    whole = jnp.zeros((4, *quarters[0].shape), quarters[0].dtype)
    for place, block in enumerate(quarters):
        whole = lax.dynamic_update_index_in_dim(whole, block, links.quarter ^ place, 0)
    return whole


def own_quarter(links, packed, axis):
    shape = packed.shape[:axis] + (4, packed.shape[axis] // 4) + packed.shape[axis + 1 :]
    return lax.dynamic_index_in_dim(packed.reshape(shape), links.quarter, axis, False)


def attention_weights(links, blocks, rows):
    part, width = blocks[0][0].shape[1:]
    line = links.line
    places, starts = (0, 1, 2, 3, 3), (0, 0, 0, 0, line // 2)
    pieces = blocks[0] + blocks[1]
    total = sum(piece.shape[0] for piece in pieces)

    def body(*refs):
        whole, semaphores = refs[len(pieces) :]
        quarter = lax.axis_index("dp") % 4
        core = lax.axis_index("col") % 2
        chip = lax.axis_index("col") // 2
        copies = []
        for i, piece in enumerate(refs[: len(pieces)]):
            side, j = divmod(i, len(places))
            for z in range(piece.shape[0]):
                target = whole.at[(chip + starts[j] + z) % line, core ^ side, quarter ^ places[j]]
                copies.append(pltpu.make_async_copy(piece.at[z], target, semaphores.at[len(copies)]))
        for copy in copies:
            copy.start()
        for copy in copies:
            copy.wait()

    (whole,) = call(
        body,
        [jax.ShapeDtypeStruct((line, 2, 4, part, width), jnp.bfloat16)],
        pieces,
        (),
        [pltpu.SemaphoreType.DMA((total,))],
        in_specs=[pl.BlockSpec(memory_space=pl.ANY)] * len(pieces),
        out_specs=[pl.BlockSpec(memory_space=pl.ANY)],
        limit=16,
        nbytes=10 * MEGA,
    )
    whole = whole.reshape(links.col, 4 * part, width)
    a, b = rows[0], rows[0] + rows[1]
    return (
        jnp.concatenate([whole[:, :a].reshape(-1, width), whole[:, a:b].reshape(-1, width)]),
        whole[:, b:].reshape(-1, width),
    )


def attention_shares(links, qkv_grad, output_grad, rows):
    width = output_grad.shape[1]
    cut = rows[0] * links.col
    parts = [g.reshape(links.col, -1, width) for g in (qkv_grad[:cut], qkv_grad[cut:], output_grad)]
    whole = jnp.concatenate(parts, axis=1).reshape(links.line, 2, 4, -1, width)
    return [lax.dynamic_index_in_dim(whole, links.core ^ core, 1, False) for core in range(2)]


def ffn_pieces(blocks):
    if blocks[0].shape[2] % 16 == 0:
        return blocks
    line, kinds, _, width = blocks[0].shape
    joined = [jnp.moveaxis(block, 1, 0).reshape(kinds, -1, width) for block in blocks]
    return [jnp.concatenate(joined, axis=1)[None]]


def ffn_share(links, grads):
    if grads.shape[0] == 1:
        grads = jnp.moveaxis(grads.reshape(3, 4 * links.line, -1, grads.shape[-1]), 0, 1)
    return grads.reshape(4, links.line, *grads.shape[1:])


def per_device(
    dp,
    col,
    inputs,
    segment_ids,
    cotangent,
    attn_gain,
    query_weight,
    key_value_weight,
    output_weight,
    ffn_gain,
    gate_weight,
    upward_weight,
    down_weight,
):
    links = Links(dp, col)
    layers, width = attn_gain.shape
    rows = (query_weight.shape[2], key_value_weight.shape[2], output_weight.shape[1])
    segments = segment_ids[0]
    where = (*tables(segments, HEAD_WIDTH), segments[:, None], segments[None, :])
    attn_gains = attn_gain.astype(jnp.float32)
    ffn_gains = ffn_gain.astype(jnp.float32)

    weights = []
    previous = None
    for layer in range(layers):
        attn_part = jnp.concatenate([query_weight[layer].T, key_value_weight[layer].T, output_weight[layer]])
        ffn_part = jnp.stack([gate_weight[layer].T, upward_weight[layer].T, down_weight[layer]])
        attn_part = own_quarter(links, attn_part, 0)
        ffn_part = own_quarter(links, ffn_part, 1)
        weights.append((attn_part, ffn_part))

    hidden = inputs[0].astype(jnp.float32)
    gains = [(attn_gains[layer][None], ffn_gains[layer][None]) for layer in range(layers)]
    saved = []
    attn_move = Transfer(gather_stages(links, weights[0][0]))
    for layer in range(layers):
        if layer == 0:
            ffn_part = advance(weights[0][1], attn_move)
            ffn_move = Transfer(gather_stages(links, ffn_part))
            hidden = advance(hidden, attn_move)
            hidden = advance(hidden, attn_move)
        qkv_w, output_w = attention_weights(links, attn_move.finish(), rows)
        qkv_w = advance(qkv_w, ffn_move)
        if layer + 1 < layers:
            attn_part, qkv_w = lax.optimization_barrier((weights[layer + 1][0], qkv_w))
            attn_move = Transfer(gather_stages(links, attn_part))
        normed, qkv, attended, logsum, middle, normed2 = attention_forward(
            hidden, *gains[layer], qkv_w, output_w, *where
        )
        normed2 = advance(normed2, ffn_move)
        if layer + 1 < layers:
            ffn_part = advance(weights[layer + 1][1], attn_move)
            next_move = Transfer(gather_stages(links, ffn_part))
        ffn_w = [ffn_pieces(half) for half in ffn_move.finish()]
        if layer + 1 < layers:
            normed2 = advance(normed2, attn_move)
        result, *products = ffn_forward(middle, normed2, *ffn_w)
        saved.append(((hidden, normed, qkv, attended, logsum, middle), normed2, products, (qkv_w, output_w), ffn_w))
        hidden = result
        if layer + 1 < layers:
            hidden = advance(hidden, attn_move)
            ffn_move = next_move
    final = hidden.astype(jnp.bfloat16)[None]

    grad_low = cotangent[0]
    grad = grad_low.astype(jnp.float32)
    moves = [None] * layers
    gain_terms = [None] * layers
    attn_move = ffn_move = None

    def ffn_pick(share, place, part):
        return share[place, part]

    def attn_pick(share, place, part):
        return lax.dynamic_index_in_dim(share[part], links.quarter ^ place, 1, False)

    for layer in reversed(range(layers)):
        kept, normed2, products, attn_w, ffn_w = saved[layer]
        both = [] if attn_move is None else [ffn_move, attn_move]
        there, grad_normed = ffn_backward(grad_low, normed2, *products[2:], ffn_w[1])
        here = []
        new_move = Transfer(scatter_stages(links, here, ffn_share(links, there), ffn_pick, False))
        grad_normed = advance(grad_normed, *both)
        own, grad_normed = ffn_backward(grad_low, normed2, *products[:2], ffn_w[0], grad_normed)
        here.append(ffn_share(links, own))
        grad_normed = advance(grad_normed, new_move, *both)
        qkv_w_grad, output_grad, grad, grad_low, *gain_grads = attention_backward(
            grad, grad_normed, *kept, *gains[layer], *attn_w, *where
        )
        ours, others = attention_shares(links, qkv_w_grad, output_grad, rows)
        (ours, others) = advance((ours, others), new_move, *both)
        ffn_move = new_move
        attn_move = Transfer(scatter_stages(links, [ours], others, attn_pick, True))
        if layer:
            grad_low = advance(grad_low, attn_move)
        moves[layer] = (attn_move, ffn_move)
        gain_terms[layer] = jnp.stack(gain_grads)
    advance(None, ffn_move, attn_move)
    advance(None, attn_move)
    advance(None, attn_move)
    advance(None, ffn_move, attn_move)

    gains = links.sum_all(jnp.concatenate(gain_terms, axis=1))
    sums = [[] for _ in range(6)]
    for attn_move, ffn_move in moves:
        total = in_order(links, attn_move.finish()).reshape(-1, width).astype(jnp.float32)
        a, b = rows[0], rows[0] + rows[1]
        sums[0].append(total[:a].T)
        sums[1].append(total[a:b].T)
        sums[2].append(total[b:])
        quarters = in_order(links, ffn_move.finish())
        for kind in range(3):
            total = quarters[:, kind].reshape(-1, width).astype(jnp.float32)
            sums[3 + kind].append(total if kind == 2 else total.T)
    sums = [jnp.stack(values) for values in sums]
    return (final, grad[None], gains[0], *sums[:3], gains[1], *sums[3:])


def solution(mesh):
    placed = (
        P(("dp", "col"), None, None),
        P(("dp", "col"), None),
        P(("dp", "col"), None, None),
        P(),
        P(None, None, "col"),
        P(None, None, "col"),
        P(None, "col", None),
        P(),
        P(None, None, "col"),
        P(None, None, "col"),
        P(None, "col", None),
    )
    return jax.shard_map(
        functools.partial(per_device, mesh.shape["dp"], mesh.shape["col"]),
        mesh=mesh,
        in_specs=placed,
        out_specs=(
            P(("dp", "col"), None, None),
            P(("dp", "col"), None, None),
            P(),
            P(None, None, "col"),
            P(None, None, "col"),
            P(None, "col", None),
            P(),
            P(None, None, "col"),
            P(None, None, "col"),
            P(None, "col", None),
        ),
        check_vma=False,
    )
```

```python
import functools
import math

import jax
import jax.numpy as jnp
from jax import lax
from jax.experimental import pallas as pl
from jax.experimental.pallas import tpu as pltpu
from jax.sharding import PartitionSpec as P

QUERY_HEADS = 15
KEY_VALUE_HEADS = 5
HEAD_WIDTH = 64


epsilon = 1e-05
theta_base = 10000.0


def rms_norm(value_rows, gain):
    return (
        value_rows
        * lax.rsqrt(jnp.mean(value_rows * value_rows, axis=-1, keepdims=True) + epsilon)
        * gain
    )


def tables(segments, head_size):
    sequence_length = segments.shape[0]
    rows = jnp.arange(sequence_length, dtype=jnp.int32)
    before = jnp.sum((segments[None, :] < segments[:, None]).astype(jnp.int32), axis=1)
    places = (rows - before).astype(jnp.float32)
    half = head_size // 2
    freqs = jnp.exp(-math.log(theta_base) * (2.0 * jnp.arange(half, dtype=jnp.float32) / head_size))
    angles = places[:, None] * freqs[None, :]
    cosine, sine = jnp.cos(angles), jnp.sin(angles)
    return (jnp.tile(cosine, (1, 4)), jnp.tile(jnp.concatenate([-sine, sine], axis=1), (1, 2)))


BLOCK = 256
REACH = 384
MEGA = 2**20


def call(body, outs, args, after=(), scratch=(), limit=56, flops=0, nbytes=0, **grid):
    given = len(args)
    late = len(after)

    def run(*refs):
        body(*refs[:given], *refs[given + late :])

    specs = grid.pop("in_specs", None) or [pl.BlockSpec(memory_space=pltpu.VMEM)] * given
    out_specs = grid.pop("out_specs", None) or [pl.BlockSpec(memory_space=pltpu.VMEM)] * len(outs)
    return pl.pallas_call(
        run,
        out_shape=outs,
        in_specs=list(specs) + [pl.BlockSpec(memory_space=pl.ANY)] * late,
        out_specs=out_specs,
        scratch_shapes=list(scratch),
        compiler_params=pltpu.CompilerParams(vmem_limit_bytes=limit * MEGA),
        cost_estimate=pl.CostEstimate(flops=flops, bytes_accessed=nbytes, transcendentals=0),
        **grid,
    )(*args, *after)


def dot(left, right, dims=((1,), (0,))):
    return lax.dot_general(left, right, (dims, ((), ())), preferred_element_type=jnp.float32)


NT = ((1,), (1,))
TN = ((0,), (0,))


def swap_halves(value):
    lane = lax.broadcasted_iota(jnp.int32, value.shape, 1)
    return jnp.where(lane % HEAD_WIDTH < HEAD_WIDTH // 2, pltpu.roll(value, 96, 1), pltpu.roll(value, 32, 1))


def spans(length):
    for start in range(0, length, BLOCK):
        yield start, max(0, start - REACH + 1) // 128 * 128, start + BLOCK


def fill_bias(bias, seg_col, seg_row, length):
    for index, (start, low, high) in enumerate(spans(length)):
        shape = (high - low, BLOCK)
        key = lax.broadcasted_iota(jnp.int32, shape, 0) + low
        query = lax.broadcasted_iota(jnp.int32, shape, 1) + start
        same = seg_col[low:high, :] == seg_row[:, start : start + BLOCK]
        bias[index, : high - low, :] = jnp.where((key <= query) & same, 0.0, -1e30)


def scale_of(value):
    return lax.rsqrt(jnp.mean(value * value, axis=-1, keepdims=True) + epsilon)


def attention_forward(hidden, gain, next_gain, qkv_w, output_w, cosine, sine, seg_col, seg_row):
    length, model = hidden.shape
    width = qkv_w.shape[0]
    q_width = QUERY_HEADS * HEAD_WIDTH
    kv_width = KEY_VALUE_HEADS * HEAD_WIDTH
    group = QUERY_HEADS // KEY_VALUE_HEADS
    rotated = q_width + kv_width
    most = max(high - low for _, low, high in spans(length))

    def body(hidden, gain, next_gain, qkv_w, output_w, cosine, sine, seg_col, seg_row, *rest):
        normed, qkv, attended, logsum, middle, normed2, raw, bias, turned = rest
        value = hidden[...]
        normed[...] = (value * scale_of(value) * gain[...]).astype(jnp.bfloat16)
        raw[...] = dot(normed[...], qkv_w[...], NT)
        for lane in range(0, rotated, 128):
            value = raw[:, lane : lane + 128]
            qkv[:, lane : lane + 128] = (value * cosine[...] + swap_halves(value) * sine[...]).astype(jnp.bfloat16)
        qkv[:, rotated:] = raw[:, rotated:].astype(jnp.bfloat16)
        fill_bias(bias, seg_col, seg_row, length)
        logsum[...] = jnp.zeros_like(logsum)
        turned[...] = raw[:, rotated:].T.astype(jnp.bfloat16)
        for index, (start, low, high) in enumerate(spans(length)):
            columns = []
            for head in range(QUERY_HEADS):
                kv = head // group
                query = qkv[start : start + BLOCK, head * HEAD_WIDTH : (head + 1) * HEAD_WIDTH] * 0.125
                at = q_width + kv * HEAD_WIDTH
                key = qkv[low:high, at : at + HEAD_WIDTH]
                logits = dot(key, query, NT) + bias[index, : high - low, :]
                peak = jnp.max(logits, axis=0, keepdims=True)
                expo = jnp.exp(logits - peak)
                total = jnp.sum(expo, axis=0, keepdims=True)
                value = turned[kv * HEAD_WIDTH : (kv + 1) * HEAD_WIDTH, low:high]
                columns.append(dot(value, expo.astype(jnp.bfloat16)) / total)
                logsum[head : head + 1, start : start + BLOCK] = peak + jnp.log(total)
            attended[start : start + BLOCK, :] = jnp.concatenate(columns, axis=0).T.astype(jnp.bfloat16)
        value = hidden[...] + dot(attended[...], output_w[...])
        middle[...] = value
        normed2[...] = (value * scale_of(value) * next_gain[...]).astype(jnp.bfloat16)

    low = jax.ShapeDtypeStruct((length, model), jnp.bfloat16)
    return call(
        body,
        [
            low,
            jax.ShapeDtypeStruct((length, width), jnp.bfloat16),
            jax.ShapeDtypeStruct((length, q_width), jnp.bfloat16),
            jax.ShapeDtypeStruct((16, length), jnp.float32),
            jax.ShapeDtypeStruct((length, model), jnp.float32),
            low,
        ],
        [hidden, gain, next_gain, qkv_w, output_w, cosine, sine, seg_col, seg_row],
        (),
        [
            pltpu.VMEM((length, width), jnp.float32),
            pltpu.VMEM((length // BLOCK, most, BLOCK), jnp.float32),
            pltpu.VMEM((kv_width, length), jnp.bfloat16),
        ],
        flops=20 * 10**9,
        nbytes=20 * MEGA,
    )


def attention_backward(
    grad, grad_normed2, hidden, normed, qkv, attended, logsum, middle, gain, next_gain, qkv_w, output_w, *where
):
    length, model = hidden.shape
    width = qkv.shape[1]
    q_width = QUERY_HEADS * HEAD_WIDTH
    kv_width = KEY_VALUE_HEADS * HEAD_WIDTH
    group = QUERY_HEADS // KEY_VALUE_HEADS
    rotated = q_width + kv_width
    most = max(high - low for _, low, high in spans(length))

    def body(grad, grad_normed2, hidden, normed, qkv, attended, logsum, middle, gain, next_gain, qkv_w, output_w, *rest):
        cosine, sine, seg_col, seg_row, *rest = rest
        qkv_w_grad, output_w_grad, out, out_low, gain_grad, next_gain_grad, *rest = rest
        bias, turned, key_sum, value_sum, query_sum, upstream_all, qkv_grad = rest

        def pull(value, g, upstream, gain_out):
            scale = scale_of(value)
            scaled = value * scale
            gain_out[...] = jnp.sum(upstream * scaled, axis=0, keepdims=True)
            pulled = upstream * g
            return scale * (pulled - scaled * jnp.mean(pulled * scaled, axis=-1, keepdims=True))

        out[...] = grad[...] + pull(middle[...], next_gain[...], grad_normed2[...], next_gain_grad)
        out_low[...] = out[...].astype(jnp.bfloat16)
        output_w_grad[...] = dot(attended[...], out_low[...], TN).astype(jnp.bfloat16)
        upstream_all[...] = dot(out_low[...], output_w[...], NT).astype(jnp.bfloat16)
        fill_bias(bias, seg_col, seg_row, length)
        turned[...] = qkv[:, q_width:rotated].astype(jnp.float32).T.astype(jnp.bfloat16) * 0.125
        key_sum[...] = jnp.zeros_like(key_sum)
        value_sum[...] = jnp.zeros_like(value_sum)
        for index, (start, low, high) in enumerate(spans(length)):
            for head in range(QUERY_HEADS):
                kv = head // group
                lanes = slice(head * HEAD_WIDTH, (head + 1) * HEAD_WIDTH)
                query = qkv[start : start + BLOCK, lanes] * 0.125
                upstream = upstream_all[start : start + BLOCK, lanes]
                at = q_width + kv * HEAD_WIDTH
                key = qkv[low:high, at : at + HEAD_WIDTH]
                value = qkv[low:high, at + kv_width : at + kv_width + HEAD_WIDTH]
                logits = dot(key, query, NT) + bias[index, : high - low, :]
                probs = jnp.exp(logits - logsum[head : head + 1, start : start + BLOCK])
                grad_probs = dot(value, upstream, NT)
                inner = jnp.sum(probs * grad_probs, axis=0, keepdims=True)
                grad_logits = (probs * (grad_probs - inner)).astype(jnp.bfloat16)
                value_sum[kv, low:high, :] += dot(probs.astype(jnp.bfloat16), upstream)
                key_sum[kv, low:high, :] += dot(grad_logits, query)
                query_sum[lanes, start : start + BLOCK] = dot(
                    turned[kv * HEAD_WIDTH : (kv + 1) * HEAD_WIDTH, low:high], grad_logits
                )
        raw = [query_sum[...].T] + [key_sum[kv] for kv in range(KEY_VALUE_HEADS)]
        raw = jnp.concatenate(raw, axis=1)
        for lane in range(0, rotated, 128):
            value = raw[:, lane : lane + 128]
            qkv_grad[:, lane : lane + 128] = (value * cosine[...] - swap_halves(value) * sine[...]).astype(jnp.bfloat16)
        values = [value_sum[kv] for kv in range(KEY_VALUE_HEADS)]
        qkv_grad[:, rotated:] = jnp.concatenate(values, axis=1).astype(jnp.bfloat16)
        qkv_w_grad[...] = dot(qkv_grad[...], normed[...], TN).astype(jnp.bfloat16)
        pulled = pull(hidden[...], gain[...], dot(qkv_grad[...], qkv_w[...]), gain_grad)
        out[...] += pulled
        out_low[...] = out[...].astype(jnp.bfloat16)

    gains = jax.ShapeDtypeStruct((1, model), jnp.float32)
    args = [grad, grad_normed2, hidden, normed, qkv, attended, logsum, middle, gain, next_gain, qkv_w, output_w, *where]
    return call(
        body,
        [
            jax.ShapeDtypeStruct(qkv_w.shape, jnp.bfloat16),
            jax.ShapeDtypeStruct(output_w.shape, jnp.bfloat16),
            jax.ShapeDtypeStruct((length, model), jnp.float32),
            jax.ShapeDtypeStruct((length, model), jnp.bfloat16),
            gains,
            gains,
        ],
        args,
        (),
        [
            pltpu.VMEM((length // BLOCK, most, BLOCK), jnp.float32),
            pltpu.VMEM((kv_width, length), jnp.bfloat16),
            pltpu.VMEM((KEY_VALUE_HEADS, length, HEAD_WIDTH), jnp.float32),
            pltpu.VMEM((KEY_VALUE_HEADS, length, HEAD_WIDTH), jnp.float32),
            pltpu.VMEM((q_width, length), jnp.float32),
            pltpu.VMEM((length, q_width), jnp.bfloat16),
            pltpu.VMEM((length, width), jnp.bfloat16),
        ],
        flops=35 * 10**9,
        nbytes=40 * MEGA,
    )


TILE = 256


def block_list(pieces):
    blocks, at = [], 0
    for piece in pieces:
        for z in range(piece.shape[0]):
            blocks.append((piece, z, at, at + piece.shape[2]))
            at += piece.shape[2]
    return blocks, at


def collect(pieces, store, semaphores):
    blocks, _ = block_list(pieces)
    copies = [
        [
            pltpu.make_async_copy(piece.at[z, kind], store.at[kind, pl.ds(at, end - at)], semaphores.at[kind, i])
            for kind in range(3)
        ]
        for i, (piece, z, at, end) in enumerate(blocks)
    ]
    for block in copies:
        for copy in block:
            copy.start()
    waited = [0]

    def until(limit):
        while waited[0] < len(blocks) and blocks[waited[0]][2] < limit:
            for copy in copies[waited[0]]:
                copy.wait()
            waited[0] += 1

    return until


def ffn_forward(middle, normed, here, there):
    length, width = middle.shape
    blocks, units = block_list(here)
    tile = math.gcd(TILE, units)

    def body(middle, normed, *rest):
        pieces = rest[: len(here) + len(there)]
        out, gate_one, up_one, gate_two, up_two, store, semaphores = rest[len(pieces) :]
        untils = [
            collect(half, store.at[i], semaphores.at[i])
            for i, half in enumerate((pieces[: len(here)], pieces[len(here) :]))
        ]
        out[...] = middle[...]
        for i, (gate_out, upward_out) in enumerate(((gate_one, up_one), (gate_two, up_two))):
            for at in range(0, units, tile):
                untils[i](at + tile)
                rows = slice(at, at + tile)
                gate = dot(normed[...], store[i, 0, rows, :], NT)
                upward = dot(normed[...], store[i, 1, rows, :], NT)
                gate_out[:, rows] = gate.astype(jnp.bfloat16)
                upward_out[:, rows] = upward.astype(jnp.bfloat16)
                active = (gate * jax.nn.sigmoid(gate) * upward).astype(jnp.bfloat16)
                out[...] += dot(active, store[i, 2, rows, :])

    low = jax.ShapeDtypeStruct((length, units), jnp.bfloat16)
    return call(
        body,
        [jax.ShapeDtypeStruct((length, width), jnp.float32), low, low, low, low],
        [middle, normed, *here, *there],
        (),
        [
            pltpu.VMEM((2, 3, units, width), jnp.bfloat16),
            pltpu.SemaphoreType.DMA((2, 3, len(blocks))),
        ],
        in_specs=[pl.BlockSpec(memory_space=pltpu.VMEM)] * 2
        + [pl.BlockSpec(memory_space=pl.ANY)] * (len(here) + len(there)),
        flops=11 * 10**9,
        nbytes=30 * MEGA,
    )


def ffn_backward(grad_low, normed, gate, upward, pieces, earlier=None):
    length, width = normed.shape
    blocks, units = block_list(pieces)
    rows_of_block = blocks[0][3]
    tile = math.gcd(TILE, units)
    before = [] if earlier is None else [earlier]

    def body(grad_low, normed, gate, upward, *rest):
        before, rest = rest[: len(rest) - 6 - len(pieces)], rest[len(rest) - 6 - len(pieces) :]
        parts, (grads, out, store, ready, semaphores, sent) = rest[: len(pieces)], rest[len(pieces) :]
        until = collect(parts, store, semaphores)
        out[...] = before[0][...] if before else jnp.zeros_like(out)
        sends = []
        for at in range(0, units, tile):
            until(at + tile)
            rows = slice(at, at + tile)
            grad_active = dot(grad_low[...], store[2, rows, :], NT)
            gate_value = gate[:, rows].astype(jnp.float32)
            up_value = upward[:, rows].astype(jnp.float32)
            sigma = jax.nn.sigmoid(gate_value)
            silu = gate_value * sigma
            active = (silu * up_value).astype(jnp.bfloat16)
            grad_up = (grad_active * silu).astype(jnp.bfloat16)
            grad_gate = (grad_active * up_value * (sigma + silu * (1.0 - sigma))).astype(jnp.bfloat16)
            ready[2, rows, :] = dot(active, grad_low[...], TN).astype(jnp.bfloat16)
            ready[0, rows, :] = dot(grad_gate, normed[...], TN).astype(jnp.bfloat16)
            ready[1, rows, :] = dot(grad_up, normed[...], TN).astype(jnp.bfloat16)
            out[...] += dot(grad_gate, store[0, rows, :]) + dot(grad_up, store[1, rows, :])
            while len(sends) < len(blocks) and blocks[len(sends)][3] <= at + tile:
                i = len(sends)
                span = pl.ds(blocks[i][2], rows_of_block)
                sends.append(
                    [
                        pltpu.make_async_copy(ready.at[kind, span], grads.at[i, kind], sent.at[kind, i])
                        for kind in range(3)
                    ]
                )
                for copy in sends[-1]:
                    copy.start()
        for block in sends:
            for copy in block:
                copy.wait()

    return call(
        body,
        [
            jax.ShapeDtypeStruct((len(blocks), 3, rows_of_block, width), jnp.bfloat16),
            jax.ShapeDtypeStruct((length, width), jnp.float32),
        ],
        [grad_low, normed, gate, upward, *before, *pieces],
        (),
        [
            pltpu.VMEM((3, units, width), jnp.bfloat16),
            pltpu.VMEM((3, units, width), jnp.bfloat16),
            pltpu.SemaphoreType.DMA((3, len(blocks))),
            pltpu.SemaphoreType.DMA((3, len(blocks))),
        ],
        in_specs=[pl.BlockSpec(memory_space=pltpu.VMEM)] * (4 + len(before))
        + [pl.BlockSpec(memory_space=pl.ANY)] * len(pieces),
        out_specs=[pl.BlockSpec(memory_space=pl.ANY), pl.BlockSpec(memory_space=pltpu.VMEM)],
        flops=11 * 10**9,
        nbytes=30 * MEGA,
    )


class Links:
    def __init__(self, dp, col):
        self.dp, self.col, self.line = dp, col, col // 2
        self.rest = [list(range(r, dp, 4)) for r in range(4)]
        self.quarter = lax.axis_index("dp") % 4
        self.core = lax.axis_index("col") % 2
        self.chip = lax.axis_index("col") // 2

    def x(self, value):
        return lax.ppermute(value, "dp", [(i, i ^ 1) for i in range(self.dp)])

    def y(self, value):
        return lax.ppermute(value, "dp", [(i, i ^ 2) for i in range(self.dp)])

    def other_core(self, value):
        return lax.ppermute(value, "col", [(i, i ^ 1) for i in range(self.col)])

    def both(self, value):
        return lax.ppermute(value, "dp", [(i, i ^ 3) for i in range(self.dp)])

    def send(self, value, step):
        return lax.ppermute(value, "col", [(i, (i + 2 * step) % self.col) for i in range(self.col)])

    def sum_all(self, value):
        for axis, size in (("dp", self.dp), ("col", self.col)):
            step = 1
            while step < size:
                value = value + lax.ppermute(value, axis, [(i, i ^ step) for i in range(size)])
                step *= 2
        return value


def add(*terms):
    total = terms[0].astype(jnp.float32)
    for term in terms[1:]:
        total = total + term.astype(jnp.float32)
    return total.astype(jnp.bfloat16)


class Transfer:
    def __init__(self, stages):
        self.stages = stages
        self.result = None
        self.flying = next(stages)

    def advance(self, arrays=None):
        try:
            self.flying = self.stages.send(self.flying if arrays is None else arrays)
        except StopIteration as stop:
            self.flying, self.result = [], stop.value

    def finish(self):
        while self.result is None:
            self.advance()
        return self.result


def advance(value, *transfers):
    flying = [transfer.flying for transfer in transfers]
    value, flying = lax.optimization_barrier((value, flying))
    for transfer, arrays in zip(transfers, flying, strict=True):
        transfer.advance(arrays)
    return value


def gather_stages(links, part):
    far = yield [links.send(part, -step) for step in range(1, links.line)]
    own = jnp.stack([part, *far])
    half = links.line // 2
    from_x, from_y, own_c = yield [links.x(own), links.y(own), links.other_core(own)]
    low, high, x_c, y_c = yield [
        links.y(from_x[:half]),
        links.x(from_y[half:]),
        links.other_core(from_x),
        links.other_core(from_y),
    ]
    low_c, high_c = yield [links.other_core(low), links.other_core(high)]
    return [[own, from_x, from_y, low, high], [own_c, x_c, y_c, low_c, high_c]]


def scatter_stages(links, kept, there, pick, in_line):
    (got,) = yield [links.other_core(there)]
    here = kept[0]
    half = links.line // 2
    low, high = slice(0, half), slice(half, links.line)

    def part(place, piece):
        return add(pick(here, place, piece), pick(got, place, piece))

    from_x, from_y = yield [
        links.x(jnp.stack([part(3, high), part(1, high)])),
        links.y(jnp.stack([part(3, low), part(2, low)])),
    ]
    x_low, y_high = yield [
        links.x(add(pick(here, 1, low), pick(got, 1, low), from_y[0])),
        links.y(add(pick(here, 2, high), pick(got, 2, high), from_x[0])),
    ]
    own = jnp.concatenate(
        [
            add(pick(here, 0, low), pick(got, 0, low), from_y[1], x_low),
            add(pick(here, 0, high), pick(got, 0, high), from_x[1], y_high),
        ]
    )

    def chip(step):
        if not in_line:
            return own[step]
        return lax.dynamic_index_in_dim(own, (links.chip + step) % links.line, 0, False)

    far = yield [links.send(chip(step), step) for step in range(1, links.line)]
    total = add(chip(0), *far)
    if links.dp > 4:
        total = lax.psum(total, "dp", axis_index_groups=links.rest)
    others = yield [links.x(total), links.y(total), links.both(total)]
    return (total, *others)


def in_order(links, quarters):
    whole = jnp.zeros((4, *quarters[0].shape), quarters[0].dtype)
    for place, block in enumerate(quarters):
        whole = lax.dynamic_update_index_in_dim(whole, block, links.quarter ^ place, 0)
    return whole


def own_quarter(links, packed, axis):
    shape = packed.shape[:axis] + (4, packed.shape[axis] // 4) + packed.shape[axis + 1 :]
    return lax.dynamic_index_in_dim(packed.reshape(shape), links.quarter, axis, False)


def attention_weights(links, blocks, rows):
    part, width = blocks[0][0].shape[2:]
    line = links.line
    places, starts = (0, 1, 2, 3, 3), (0, 0, 0, 0, line // 2)
    pieces = blocks[0] + blocks[1]
    total = sum(piece.shape[0] for piece in pieces)

    def body(*refs):
        whole, semaphores = refs[len(pieces) :]
        quarter = lax.axis_index("dp") % 4
        core = lax.axis_index("col") % 2
        chip = lax.axis_index("col") // 2
        copies = []
        for i, piece in enumerate(refs[: len(pieces)]):
            side, j = divmod(i, len(places))
            for z in range(piece.shape[0]):
                target = whole.at[(chip + starts[j] + z) % line, core ^ side, quarter ^ places[j]]
                copies.append(pltpu.make_async_copy(piece.at[z, 3], target, semaphores.at[len(copies)]))
        for copy in copies:
            copy.start()
        for copy in copies:
            copy.wait()

    (whole,) = call(
        body,
        [jax.ShapeDtypeStruct((line, 2, 4, part, width), jnp.bfloat16)],
        pieces,
        (),
        [pltpu.SemaphoreType.DMA((total,))],
        in_specs=[pl.BlockSpec(memory_space=pl.ANY)] * len(pieces),
        out_specs=[pl.BlockSpec(memory_space=pl.ANY)],
        limit=16,
        nbytes=10 * MEGA,
    )
    whole = whole.reshape(links.col, 4 * part, width)
    a, b = rows[0], rows[0] + rows[1]
    return (
        jnp.concatenate([whole[:, :a].reshape(-1, width), whole[:, a:b].reshape(-1, width)]),
        whole[:, b:].reshape(-1, width),
    )


def attention_shares(links, qkv_grad, output_grad, rows):
    width = output_grad.shape[1]
    cut = rows[0] * links.col
    parts = [g.reshape(links.col, -1, width) for g in (qkv_grad[:cut], qkv_grad[cut:], output_grad)]
    whole = jnp.concatenate(parts, axis=1).reshape(links.line, 2, 4, -1, width)
    return [lax.dynamic_index_in_dim(whole, links.core ^ core, 1, False) for core in range(2)]


def ffn_pieces(blocks):
    if blocks[0].shape[2] % 16 == 0:
        return blocks
    width = blocks[0].shape[-1]
    joined = [jnp.moveaxis(block[:, :3], 1, 0).reshape(3, -1, width) for block in blocks]
    return [jnp.concatenate(joined, axis=1)[None]]


def ffn_share(links, grads):
    if grads.shape[0] == 1:
        grads = jnp.moveaxis(grads.reshape(3, 4 * links.line, -1, grads.shape[-1]), 0, 1)
    return grads.reshape(4, links.line, *grads.shape[1:])


def per_device(
    dp,
    col,
    inputs,
    segment_ids,
    cotangent,
    attn_gain,
    query_weight,
    key_value_weight,
    output_weight,
    ffn_gain,
    gate_weight,
    upward_weight,
    down_weight,
):
    links = Links(dp, col)
    layers, width = attn_gain.shape
    rows = (query_weight.shape[2], key_value_weight.shape[2], output_weight.shape[1])
    segments = segment_ids[0]
    where = (*tables(segments, HEAD_WIDTH), segments[:, None], segments[None, :])
    attn_gains = attn_gain.astype(jnp.float32)
    ffn_gains = ffn_gain.astype(jnp.float32)

    parts = []
    for layer in range(layers):
        attn_part = jnp.concatenate([query_weight[layer].T, key_value_weight[layer].T, output_weight[layer]])
        ffn_part = jnp.stack([gate_weight[layer].T, upward_weight[layer].T, down_weight[layer]])
        parts.append(
            jnp.concatenate([own_quarter(links, ffn_part, 1), own_quarter(links, attn_part, 0)[None]])
        )

    hidden = inputs[0].astype(jnp.float32)
    gains = [(attn_gains[layer][None], ffn_gains[layer][None]) for layer in range(layers)]
    saved = []
    move = Transfer(gather_stages(links, parts[0]))
    for layer in range(layers):
        later = []
        if layer + 1 < layers:
            part = advance(parts[layer + 1], move)
            later = [Transfer(gather_stages(links, part))]
        advance(None, move)
        hidden = advance(hidden, move, *later)
        blocks = move.finish()
        qkv_w, output_w = attention_weights(links, blocks, rows)
        ffn_w = [ffn_pieces(half) for half in blocks]
        normed, qkv, attended, logsum, middle, normed2 = attention_forward(
            hidden, *gains[layer], qkv_w, output_w, *where
        )
        result, *products = ffn_forward(middle, normed2, *ffn_w)
        saved.append(((hidden, normed, qkv, attended, logsum, middle), normed2, products, (qkv_w, output_w), ffn_w))
        hidden = result
        if later:
            hidden = advance(hidden, *later)
            move = later[0]
    final = hidden.astype(jnp.bfloat16)[None]

    grad_low = cotangent[0]
    grad = grad_low.astype(jnp.float32)
    moves = [None] * layers
    gain_terms = [None] * layers
    attn_move = ffn_move = None

    def ffn_pick(share, place, part):
        return share[place, part]

    def attn_pick(share, place, part):
        return lax.dynamic_index_in_dim(share[part], links.quarter ^ place, 1, False)

    for layer in reversed(range(layers)):
        kept, normed2, products, attn_w, ffn_w = saved[layer]
        last_ffn = [] if ffn_move is None else [ffn_move]
        last_attn = [] if attn_move is None else [attn_move]
        there, grad_normed = ffn_backward(grad_low, normed2, *products[2:], ffn_w[1])
        there, grad_normed = advance((there, grad_normed), *last_ffn, *last_attn)
        here = []
        new_move = Transfer(scatter_stages(links, here, ffn_share(links, there), ffn_pick, False))
        own, grad_normed = ffn_backward(grad_low, normed2, *products[:2], ffn_w[0], grad_normed)
        own, grad_normed, *new_move.flying = advance((own, grad_normed, *new_move.flying), *last_attn)
        here.append(ffn_share(links, own))
        new_move.advance()
        results = attention_backward(grad, grad_normed, *kept, *gains[layer], *attn_w, *where)
        results = advance(results, new_move, *last_ffn, *last_attn)
        qkv_w_grad, output_grad, grad, grad_low, *gain_grads = results
        ours, others = attention_shares(links, qkv_w_grad, output_grad, rows)
        moves[layer] = (attn_move, ffn_move) = (
            Transfer(scatter_stages(links, [ours], others, attn_pick, True)),
            new_move,
        )
        gain_terms[layer] = jnp.stack(gain_grads)
    gain_terms = jnp.concatenate(gain_terms, axis=1)
    gain_terms = advance(gain_terms, ffn_move, attn_move)
    gain_terms = advance(gain_terms, attn_move, *last_ffn, *last_attn)
    gain_terms = advance(gain_terms, attn_move)
    gains = links.sum_all(gain_terms)
    advance(None, ffn_move, attn_move)
    sums = [[] for _ in range(6)]
    for attn_move, ffn_move in moves:
        total = in_order(links, attn_move.finish()).reshape(-1, width).astype(jnp.float32)
        a, b = rows[0], rows[0] + rows[1]
        sums[0].append(total[:a].T)
        sums[1].append(total[a:b].T)
        sums[2].append(total[b:])
        quarters = in_order(links, ffn_move.finish())
        for kind in range(3):
            total = quarters[:, kind].reshape(-1, width).astype(jnp.float32)
            sums[3 + kind].append(total if kind == 2 else total.T)
    sums = [jnp.stack(values) for values in sums]
    return (final, grad[None], gains[0], *sums[:3], gains[1], *sums[3:])


def solution(mesh):
    placed = (
        P(("dp", "col"), None, None),
        P(("dp", "col"), None),
        P(("dp", "col"), None, None),
        P(),
        P(None, None, "col"),
        P(None, None, "col"),
        P(None, "col", None),
        P(),
        P(None, None, "col"),
        P(None, None, "col"),
        P(None, "col", None),
    )
    return jax.shard_map(
        functools.partial(per_device, mesh.shape["dp"], mesh.shape["col"]),
        mesh=mesh,
        in_specs=placed,
        out_specs=(
            P(("dp", "col"), None, None),
            P(("dp", "col"), None, None),
            P(),
            P(None, None, "col"),
            P(None, None, "col"),
            P(None, "col", None),
            P(),
            P(None, None, "col"),
            P(None, None, "col"),
            P(None, "col", None),
        ),
        check_vma=False,
    )
```

```python
import functools
import math

import jax
import jax.numpy as jnp
from jax import lax
from jax.experimental import pallas as pl
from jax.experimental.pallas import tpu as pltpu
from jax.sharding import PartitionSpec as P

QUERY_HEADS = 15
KEY_VALUE_HEADS = 5
HEAD_WIDTH = 64


epsilon = 1e-05
theta_base = 10000.0


def rms_norm(value_rows, gain):
    return (
        value_rows
        * lax.rsqrt(jnp.mean(value_rows * value_rows, axis=-1, keepdims=True) + epsilon)
        * gain
    )


def tables(segments, head_size):
    sequence_length = segments.shape[0]
    rows = jnp.arange(sequence_length, dtype=jnp.int32)
    before = jnp.sum((segments[None, :] < segments[:, None]).astype(jnp.int32), axis=1)
    places = (rows - before).astype(jnp.float32)
    half = head_size // 2
    freqs = jnp.exp(-math.log(theta_base) * (2.0 * jnp.arange(half, dtype=jnp.float32) / head_size))
    angles = places[:, None] * freqs[None, :]
    cosine, sine = jnp.cos(angles), jnp.sin(angles)
    return (jnp.tile(cosine, (1, 4)), jnp.tile(jnp.concatenate([-sine, sine], axis=1), (1, 2)))


BLOCK = 256
REACH = 384
MEGA = 2**20


def call(body, outs, args, after=(), scratch=(), limit=56, flops=0, nbytes=0, **grid):
    given = len(args)
    late = len(after)

    def run(*refs):
        body(*refs[:given], *refs[given + late :])

    specs = grid.pop("in_specs", None) or [pl.BlockSpec(memory_space=pltpu.VMEM)] * given
    out_specs = grid.pop("out_specs", None) or [pl.BlockSpec(memory_space=pltpu.VMEM)] * len(outs)
    return pl.pallas_call(
        run,
        out_shape=outs,
        in_specs=list(specs) + [pl.BlockSpec(memory_space=pl.ANY)] * late,
        out_specs=out_specs,
        scratch_shapes=list(scratch),
        compiler_params=pltpu.CompilerParams(vmem_limit_bytes=limit * MEGA),
        cost_estimate=pl.CostEstimate(flops=flops, bytes_accessed=nbytes, transcendentals=0),
        **grid,
    )(*args, *after)


def dot(left, right, dims=((1,), (0,))):
    return lax.dot_general(left, right, (dims, ((), ())), preferred_element_type=jnp.float32)


NT = ((1,), (1,))
TN = ((0,), (0,))


def swap_halves(value):
    lane = lax.broadcasted_iota(jnp.int32, value.shape, 1)
    return jnp.where(lane % HEAD_WIDTH < HEAD_WIDTH // 2, pltpu.roll(value, 96, 1), pltpu.roll(value, 32, 1))


def spans(length):
    for start in range(0, length, BLOCK):
        yield start, max(0, start - REACH + 1) // 128 * 128, start + BLOCK


def fill_bias(bias, seg_col, seg_row, length):
    for index, (start, low, high) in enumerate(spans(length)):
        shape = (high - low, BLOCK)
        key = lax.broadcasted_iota(jnp.int32, shape, 0) + low
        query = lax.broadcasted_iota(jnp.int32, shape, 1) + start
        same = seg_col[low:high, :] == seg_row[:, start : start + BLOCK]
        bias[index, : high - low, :] = jnp.where((key <= query) & same, 0.0, -1e30)


def scale_of(value):
    return lax.rsqrt(jnp.mean(value * value, axis=-1, keepdims=True) + epsilon)


def attention_forward(hidden, gain, next_gain, qkv_w, output_w, cosine, sine, seg_col, seg_row):
    length, model = hidden.shape
    width = qkv_w.shape[0]
    q_width = QUERY_HEADS * HEAD_WIDTH
    kv_width = KEY_VALUE_HEADS * HEAD_WIDTH
    group = QUERY_HEADS // KEY_VALUE_HEADS
    rotated = q_width + kv_width
    most = max(high - low for _, low, high in spans(length))

    def body(hidden, gain, next_gain, qkv_w, output_w, cosine, sine, seg_col, seg_row, *rest):
        normed, qkv, attended, logsum, middle, normed2, raw, bias, turned = rest
        value = hidden[...]
        normed[...] = (value * scale_of(value) * gain[...]).astype(jnp.bfloat16)
        raw[...] = dot(normed[...], qkv_w[...], NT)
        for lane in range(0, rotated, 128):
            value = raw[:, lane : lane + 128]
            qkv[:, lane : lane + 128] = (value * cosine[...] + swap_halves(value) * sine[...]).astype(jnp.bfloat16)
        qkv[:, rotated:] = raw[:, rotated:].astype(jnp.bfloat16)
        fill_bias(bias, seg_col, seg_row, length)
        logsum[...] = jnp.zeros_like(logsum)
        turned[...] = raw[:, rotated:].T.astype(jnp.bfloat16)
        for index, (start, low, high) in enumerate(spans(length)):
            columns = []
            for head in range(QUERY_HEADS):
                kv = head // group
                query = qkv[start : start + BLOCK, head * HEAD_WIDTH : (head + 1) * HEAD_WIDTH] * 0.125
                at = q_width + kv * HEAD_WIDTH
                key = qkv[low:high, at : at + HEAD_WIDTH]
                logits = dot(key, query, NT) + bias[index, : high - low, :]
                peak = jnp.max(logits, axis=0, keepdims=True)
                expo = jnp.exp(logits - peak)
                total = jnp.sum(expo, axis=0, keepdims=True)
                value = turned[kv * HEAD_WIDTH : (kv + 1) * HEAD_WIDTH, low:high]
                columns.append(dot(value, expo.astype(jnp.bfloat16)) / total)
                logsum[head : head + 1, start : start + BLOCK] = peak + jnp.log(total)
            attended[start : start + BLOCK, :] = jnp.concatenate(columns, axis=0).T.astype(jnp.bfloat16)
        value = hidden[...] + dot(attended[...], output_w[...])
        middle[...] = value
        normed2[...] = (value * scale_of(value) * next_gain[...]).astype(jnp.bfloat16)

    low = jax.ShapeDtypeStruct((length, model), jnp.bfloat16)
    return call(
        body,
        [
            low,
            jax.ShapeDtypeStruct((length, width), jnp.bfloat16),
            jax.ShapeDtypeStruct((length, q_width), jnp.bfloat16),
            jax.ShapeDtypeStruct((16, length), jnp.float32),
            jax.ShapeDtypeStruct((length, model), jnp.float32),
            low,
        ],
        [hidden, gain, next_gain, qkv_w, output_w, cosine, sine, seg_col, seg_row],
        (),
        [
            pltpu.VMEM((length, width), jnp.float32),
            pltpu.VMEM((length // BLOCK, most, BLOCK), jnp.float32),
            pltpu.VMEM((kv_width, length), jnp.bfloat16),
        ],
        flops=20 * 10**9,
        nbytes=20 * MEGA,
    )


def attention_backward(
    grad, grad_normed2, hidden, normed, qkv, attended, logsum, middle, gain, next_gain, qkv_w, output_w, *where
):
    length, model = hidden.shape
    width = qkv.shape[1]
    q_width = QUERY_HEADS * HEAD_WIDTH
    kv_width = KEY_VALUE_HEADS * HEAD_WIDTH
    group = QUERY_HEADS // KEY_VALUE_HEADS
    rotated = q_width + kv_width
    most = max(high - low for _, low, high in spans(length))

    def body(grad, grad_normed2, hidden, normed, qkv, attended, logsum, middle, gain, next_gain, qkv_w, output_w, *rest):
        cosine, sine, seg_col, seg_row, *rest = rest
        qkv_w_grad, output_w_grad, out, out_low, gain_grad, next_gain_grad, *rest = rest
        bias, turned, key_sum, value_sum, query_sum, upstream_all, qkv_grad = rest

        def pull(value, g, upstream, gain_out):
            scale = scale_of(value)
            scaled = value * scale
            gain_out[...] = jnp.sum(upstream * scaled, axis=0, keepdims=True)
            pulled = upstream * g
            return scale * (pulled - scaled * jnp.mean(pulled * scaled, axis=-1, keepdims=True))

        out[...] = grad[...] + pull(middle[...], next_gain[...], grad_normed2[...], next_gain_grad)
        out_low[...] = out[...].astype(jnp.bfloat16)
        output_w_grad[...] = dot(attended[...], out_low[...], TN).astype(jnp.bfloat16)
        upstream_all[...] = dot(out_low[...], output_w[...], NT).astype(jnp.bfloat16)
        fill_bias(bias, seg_col, seg_row, length)
        turned[...] = qkv[:, q_width:rotated].astype(jnp.float32).T.astype(jnp.bfloat16) * 0.125
        key_sum[...] = jnp.zeros_like(key_sum)
        value_sum[...] = jnp.zeros_like(value_sum)
        for index, (start, low, high) in enumerate(spans(length)):
            for head in range(QUERY_HEADS):
                kv = head // group
                lanes = slice(head * HEAD_WIDTH, (head + 1) * HEAD_WIDTH)
                query = qkv[start : start + BLOCK, lanes] * 0.125
                upstream = upstream_all[start : start + BLOCK, lanes]
                at = q_width + kv * HEAD_WIDTH
                key = qkv[low:high, at : at + HEAD_WIDTH]
                value = qkv[low:high, at + kv_width : at + kv_width + HEAD_WIDTH]
                logits = dot(key, query, NT) + bias[index, : high - low, :]
                probs = jnp.exp(logits - logsum[head : head + 1, start : start + BLOCK])
                grad_probs = dot(value, upstream, NT)
                inner = jnp.sum(probs * grad_probs, axis=0, keepdims=True)
                grad_logits = (probs * (grad_probs - inner)).astype(jnp.bfloat16)
                value_sum[kv, low:high, :] += dot(probs.astype(jnp.bfloat16), upstream)
                key_sum[kv, low:high, :] += dot(grad_logits, query)
                query_sum[lanes, start : start + BLOCK] = dot(
                    turned[kv * HEAD_WIDTH : (kv + 1) * HEAD_WIDTH, low:high], grad_logits
                )
        raw = [query_sum[...].T] + [key_sum[kv] for kv in range(KEY_VALUE_HEADS)]
        raw = jnp.concatenate(raw, axis=1)
        for lane in range(0, rotated, 128):
            value = raw[:, lane : lane + 128]
            qkv_grad[:, lane : lane + 128] = (value * cosine[...] - swap_halves(value) * sine[...]).astype(jnp.bfloat16)
        values = [value_sum[kv] for kv in range(KEY_VALUE_HEADS)]
        qkv_grad[:, rotated:] = jnp.concatenate(values, axis=1).astype(jnp.bfloat16)
        qkv_w_grad[...] = dot(qkv_grad[...], normed[...], TN).astype(jnp.bfloat16)
        pulled = pull(hidden[...], gain[...], dot(qkv_grad[...], qkv_w[...]), gain_grad)
        out[...] += pulled
        out_low[...] = out[...].astype(jnp.bfloat16)

    gains = jax.ShapeDtypeStruct((1, model), jnp.float32)
    args = [grad, grad_normed2, hidden, normed, qkv, attended, logsum, middle, gain, next_gain, qkv_w, output_w, *where]
    return call(
        body,
        [
            jax.ShapeDtypeStruct(qkv_w.shape, jnp.bfloat16),
            jax.ShapeDtypeStruct(output_w.shape, jnp.bfloat16),
            jax.ShapeDtypeStruct((length, model), jnp.float32),
            jax.ShapeDtypeStruct((length, model), jnp.bfloat16),
            gains,
            gains,
        ],
        args,
        (),
        [
            pltpu.VMEM((length // BLOCK, most, BLOCK), jnp.float32),
            pltpu.VMEM((kv_width, length), jnp.bfloat16),
            pltpu.VMEM((KEY_VALUE_HEADS, length, HEAD_WIDTH), jnp.float32),
            pltpu.VMEM((KEY_VALUE_HEADS, length, HEAD_WIDTH), jnp.float32),
            pltpu.VMEM((q_width, length), jnp.float32),
            pltpu.VMEM((length, q_width), jnp.bfloat16),
            pltpu.VMEM((length, width), jnp.bfloat16),
        ],
        flops=35 * 10**9,
        nbytes=40 * MEGA,
    )


TILE = 256


def block_list(pieces):
    blocks, at = [], 0
    for piece in pieces:
        for z in range(piece.shape[0]):
            blocks.append((piece, z, at, at + piece.shape[2]))
            at += piece.shape[2]
    return blocks, at


def collect(pieces, store, semaphores):
    blocks, _ = block_list(pieces)
    copies = [
        [
            pltpu.make_async_copy(piece.at[z, kind], store.at[kind, pl.ds(at, end - at)], semaphores.at[kind, i])
            for kind in range(3)
        ]
        for i, (piece, z, at, end) in enumerate(blocks)
    ]
    for block in copies:
        for copy in block:
            copy.start()
    waited = [0]

    def until(limit):
        while waited[0] < len(blocks) and blocks[waited[0]][2] < limit:
            for copy in copies[waited[0]]:
                copy.wait()
            waited[0] += 1

    return until


def ffn_forward(middle, normed, here, there):
    length, width = middle.shape
    blocks, units = block_list(here)
    tile = math.gcd(TILE, units)

    def body(middle, normed, *rest):
        pieces = rest[: len(here) + len(there)]
        out, gate_one, up_one, gate_two, up_two, store, semaphores = rest[len(pieces) :]
        untils = [
            collect(half, store.at[i], semaphores.at[i])
            for i, half in enumerate((pieces[: len(here)], pieces[len(here) :]))
        ]
        out[...] = middle[...]
        for i, (gate_out, upward_out) in enumerate(((gate_one, up_one), (gate_two, up_two))):
            for at in range(0, units, tile):
                untils[i](at + tile)
                rows = slice(at, at + tile)
                gate = dot(normed[...], store[i, 0, rows, :], NT)
                upward = dot(normed[...], store[i, 1, rows, :], NT)
                gate_out[:, rows] = gate.astype(jnp.bfloat16)
                upward_out[:, rows] = upward.astype(jnp.bfloat16)
                active = (gate * jax.nn.sigmoid(gate) * upward).astype(jnp.bfloat16)
                out[...] += dot(active, store[i, 2, rows, :])

    low = jax.ShapeDtypeStruct((length, units), jnp.bfloat16)
    return call(
        body,
        [jax.ShapeDtypeStruct((length, width), jnp.float32), low, low, low, low],
        [middle, normed, *here, *there],
        (),
        [
            pltpu.VMEM((2, 3, units, width), jnp.bfloat16),
            pltpu.SemaphoreType.DMA((2, 3, len(blocks))),
        ],
        in_specs=[pl.BlockSpec(memory_space=pltpu.VMEM)] * 2
        + [pl.BlockSpec(memory_space=pl.ANY)] * (len(here) + len(there)),
        flops=11 * 10**9,
        nbytes=30 * MEGA,
    )


def ffn_backward(grad_low, normed, gate, upward, pieces, earlier=None):
    length, width = normed.shape
    blocks, units = block_list(pieces)
    rows_of_block = blocks[0][3]
    tile = math.gcd(TILE, units)
    before = [] if earlier is None else [earlier]

    def body(grad_low, normed, gate, upward, *rest):
        before, rest = rest[: len(rest) - 6 - len(pieces)], rest[len(rest) - 6 - len(pieces) :]
        parts, (grads, out, store, ready, semaphores, sent) = rest[: len(pieces)], rest[len(pieces) :]
        until = collect(parts, store, semaphores)
        out[...] = before[0][...] if before else jnp.zeros_like(out)
        sends = []
        for at in range(0, units, tile):
            until(at + tile)
            rows = slice(at, at + tile)
            grad_active = dot(grad_low[...], store[2, rows, :], NT)
            gate_value = gate[:, rows].astype(jnp.float32)
            up_value = upward[:, rows].astype(jnp.float32)
            sigma = jax.nn.sigmoid(gate_value)
            silu = gate_value * sigma
            active = (silu * up_value).astype(jnp.bfloat16)
            grad_up = (grad_active * silu).astype(jnp.bfloat16)
            grad_gate = (grad_active * up_value * (sigma + silu * (1.0 - sigma))).astype(jnp.bfloat16)
            ready[2, rows, :] = dot(active, grad_low[...], TN).astype(jnp.bfloat16)
            ready[0, rows, :] = dot(grad_gate, normed[...], TN).astype(jnp.bfloat16)
            ready[1, rows, :] = dot(grad_up, normed[...], TN).astype(jnp.bfloat16)
            out[...] += dot(grad_gate, store[0, rows, :]) + dot(grad_up, store[1, rows, :])
            while len(sends) < len(blocks) and blocks[len(sends)][3] <= at + tile:
                i = len(sends)
                span = pl.ds(blocks[i][2], rows_of_block)
                sends.append(
                    [
                        pltpu.make_async_copy(ready.at[kind, span], grads.at[i, kind], sent.at[kind, i])
                        for kind in range(3)
                    ]
                )
                for copy in sends[-1]:
                    copy.start()
        for block in sends:
            for copy in block:
                copy.wait()

    return call(
        body,
        [
            jax.ShapeDtypeStruct((len(blocks), 3, rows_of_block, width), jnp.bfloat16),
            jax.ShapeDtypeStruct((length, width), jnp.float32),
        ],
        [grad_low, normed, gate, upward, *before, *pieces],
        (),
        [
            pltpu.VMEM((3, units, width), jnp.bfloat16),
            pltpu.VMEM((3, units, width), jnp.bfloat16),
            pltpu.SemaphoreType.DMA((3, len(blocks))),
            pltpu.SemaphoreType.DMA((3, len(blocks))),
        ],
        in_specs=[pl.BlockSpec(memory_space=pltpu.VMEM)] * (4 + len(before))
        + [pl.BlockSpec(memory_space=pl.ANY)] * len(pieces),
        out_specs=[pl.BlockSpec(memory_space=pl.ANY), pl.BlockSpec(memory_space=pltpu.VMEM)],
        flops=11 * 10**9,
        nbytes=30 * MEGA,
    )


class Links:
    def __init__(self, dp, col):
        self.dp, self.col, self.line = dp, col, col // 2
        self.rest = [list(range(r, dp, 4)) for r in range(4)]
        self.quarter = lax.axis_index("dp") % 4
        self.core = lax.axis_index("col") % 2
        self.chip = lax.axis_index("col") // 2

    def x(self, value):
        return lax.ppermute(value, "dp", [(i, i ^ 1) for i in range(self.dp)])

    def y(self, value):
        return lax.ppermute(value, "dp", [(i, i ^ 2) for i in range(self.dp)])

    def other_core(self, value):
        return lax.ppermute(value, "col", [(i, i ^ 1) for i in range(self.col)])

    def both(self, value):
        return lax.ppermute(value, "dp", [(i, i ^ 3) for i in range(self.dp)])

    def send(self, value, step):
        return lax.ppermute(value, "col", [(i, (i + 2 * step) % self.col) for i in range(self.col)])

    def sum_all(self, value):
        for axis, size in (("dp", self.dp), ("col", self.col)):
            step = 1
            while step < size:
                value = value + lax.ppermute(value, axis, [(i, i ^ step) for i in range(size)])
                step *= 2
        return value


def add(*terms):
    total = terms[0].astype(jnp.float32)
    for term in terms[1:]:
        total = total + term.astype(jnp.float32)
    return total.astype(jnp.bfloat16)


class Transfer:
    def __init__(self, stages):
        self.stages = stages
        self.result = None
        self.flying = next(stages)

    def advance(self, arrays=None):
        try:
            self.flying = self.stages.send(self.flying if arrays is None else arrays)
        except StopIteration as stop:
            self.flying, self.result = [], stop.value

    def finish(self):
        while self.result is None:
            self.advance()
        return self.result


def settle(value, *arrays):
    return lax.optimization_barrier((value, arrays))[0]


def advance(value, *transfers):
    flying = [transfer.flying for transfer in transfers]
    value, flying = lax.optimization_barrier((value, flying))
    for transfer, arrays in zip(transfers, flying, strict=True):
        transfer.advance(arrays)
    return value


def gather_stages(links, part):
    far = yield [links.send(part, -step) for step in range(1, links.line)]
    own = jnp.stack([part, *far])
    half = links.line // 2
    from_x, from_y = yield [links.x(own), links.y(own)]
    low, high, own_c, x_c, y_c = yield [
        links.y(from_x[:half]),
        links.x(from_y[half:]),
        links.other_core(own),
        links.other_core(from_x),
        links.other_core(from_y),
    ]
    low_c, high_c = yield [links.other_core(low), links.other_core(high)]
    return [[own, from_x, from_y, low, high], [own_c, x_c, y_c, low_c, high_c]]


def scatter_stages(links, kept, there, pick, in_line):
    (got,) = yield [links.other_core(there)]
    here = kept[0]
    half = links.line // 2
    low, high = slice(0, half), slice(half, links.line)

    def part(place, piece):
        return add(pick(here, place, piece), pick(got, place, piece))

    from_x, from_y = yield [
        links.x(jnp.stack([part(3, high), part(1, high)])),
        links.y(jnp.stack([part(3, low), part(2, low)])),
    ]
    x_low, y_high = yield [
        links.x(add(pick(here, 1, low), pick(got, 1, low), from_y[0])),
        links.y(add(pick(here, 2, high), pick(got, 2, high), from_x[0])),
    ]
    own = jnp.concatenate(
        [
            add(pick(here, 0, low), pick(got, 0, low), from_y[1], x_low),
            add(pick(here, 0, high), pick(got, 0, high), from_x[1], y_high),
        ]
    )

    def chip(step):
        if not in_line:
            return own[step]
        return lax.dynamic_index_in_dim(own, (links.chip + step) % links.line, 0, False)

    far = yield [links.send(chip(step), step) for step in range(1, links.line)]
    total = add(chip(0), *far)
    if links.dp > 4:
        total = lax.psum(total, "dp", axis_index_groups=links.rest)
    return total


def quarter_stages(links, total):
    others = yield [links.x(total), links.y(total), links.both(total)]
    return (total, *others)


def in_order(links, quarters):
    whole = jnp.zeros((4, *quarters[0].shape), quarters[0].dtype)
    for place, block in enumerate(quarters):
        whole = lax.dynamic_update_index_in_dim(whole, block, links.quarter ^ place, 0)
    return whole


def own_quarter(links, packed, axis):
    shape = packed.shape[:axis] + (4, packed.shape[axis] // 4) + packed.shape[axis + 1 :]
    return lax.dynamic_index_in_dim(packed.reshape(shape), links.quarter, axis, False)


def attention_weights(links, blocks, rows):
    part, width = blocks[0][0].shape[2:]
    line = links.line
    places, starts = (0, 1, 2, 3, 3), (0, 0, 0, 0, line // 2)
    pieces = blocks[0] + blocks[1]
    total = sum(piece.shape[0] for piece in pieces)

    def body(*refs):
        whole, semaphores = refs[len(pieces) :]
        quarter = lax.axis_index("dp") % 4
        core = lax.axis_index("col") % 2
        chip = lax.axis_index("col") // 2
        copies = []
        for i, piece in enumerate(refs[: len(pieces)]):
            side, j = divmod(i, len(places))
            for z in range(piece.shape[0]):
                target = whole.at[(chip + starts[j] + z) % line, core ^ side, quarter ^ places[j]]
                copies.append(pltpu.make_async_copy(piece.at[z, 3], target, semaphores.at[len(copies)]))
        for copy in copies:
            copy.start()
        for copy in copies:
            copy.wait()

    (whole,) = call(
        body,
        [jax.ShapeDtypeStruct((line, 2, 4, part, width), jnp.bfloat16)],
        pieces,
        (),
        [pltpu.SemaphoreType.DMA((total,))],
        in_specs=[pl.BlockSpec(memory_space=pl.ANY)] * len(pieces),
        out_specs=[pl.BlockSpec(memory_space=pl.ANY)],
        limit=16,
        nbytes=10 * MEGA,
    )
    whole = whole.reshape(links.col, 4 * part, width)
    a, b = rows[0], rows[0] + rows[1]
    return (
        jnp.concatenate([whole[:, :a].reshape(-1, width), whole[:, a:b].reshape(-1, width)]),
        whole[:, b:].reshape(-1, width),
    )


def attention_shares(links, qkv_grad, output_grad, rows):
    width = output_grad.shape[1]
    cut = rows[0] * links.col
    parts = [g.reshape(links.col, -1, width) for g in (qkv_grad[:cut], qkv_grad[cut:], output_grad)]
    whole = jnp.concatenate(parts, axis=1).reshape(links.line, 2, 4, -1, width)
    return [lax.dynamic_index_in_dim(whole, links.core ^ core, 1, False) for core in range(2)]


def ffn_pieces(blocks):
    if blocks[0].shape[2] % 16 == 0:
        return blocks
    width = blocks[0].shape[-1]
    joined = [jnp.moveaxis(block[:, :3], 1, 0).reshape(3, -1, width) for block in blocks]
    return [jnp.concatenate(joined, axis=1)[None]]


def ffn_share(links, grads):
    if grads.shape[0] == 1:
        grads = jnp.moveaxis(grads.reshape(3, 4 * links.line, -1, grads.shape[-1]), 0, 1)
    return grads.reshape(4, links.line, *grads.shape[1:])


def per_device(
    dp,
    col,
    inputs,
    segment_ids,
    cotangent,
    attn_gain,
    query_weight,
    key_value_weight,
    output_weight,
    ffn_gain,
    gate_weight,
    upward_weight,
    down_weight,
):
    links = Links(dp, col)
    layers, width = attn_gain.shape
    rows = (query_weight.shape[2], key_value_weight.shape[2], output_weight.shape[1])
    segments = segment_ids[0]
    where = (*tables(segments, HEAD_WIDTH), segments[:, None], segments[None, :])
    attn_gains = attn_gain.astype(jnp.float32)
    ffn_gains = ffn_gain.astype(jnp.float32)

    parts = []
    for layer in range(layers):
        attn_part = jnp.concatenate([query_weight[layer].T, key_value_weight[layer].T, output_weight[layer]])
        ffn_part = jnp.stack([gate_weight[layer].T, upward_weight[layer].T, down_weight[layer]])
        parts.append(
            jnp.concatenate([own_quarter(links, ffn_part, 1), own_quarter(links, attn_part, 0)[None]])
        )

    hidden = inputs[0].astype(jnp.float32)
    gains = [(attn_gains[layer][None], ffn_gains[layer][None]) for layer in range(layers)]
    saved = []
    move = Transfer(gather_stages(links, parts[0]))
    for layer in range(layers):
        later = []
        if layer + 1 < layers:
            part = advance(parts[layer + 1], move)
            later = [Transfer(gather_stages(links, part))]
            move.flying = settle(move.flying, *later[0].flying)
            advance(None, move)
        hidden = advance(hidden, move, *later)
        blocks = move.finish()
        qkv_w, output_w = attention_weights(links, blocks, rows)
        ffn_w = [ffn_pieces(half) for half in blocks]
        normed, qkv, attended, logsum, middle, normed2 = attention_forward(
            hidden, *gains[layer], qkv_w, output_w, *where
        )
        normed2 = advance(normed2, *later)
        result, *products = ffn_forward(middle, normed2, *ffn_w)
        saved.append(((hidden, normed, qkv, attended, logsum, middle), normed2, products, (qkv_w, output_w), ffn_w))
        hidden = result
        if later:
            move = later[0]
    final = hidden.astype(jnp.bfloat16)[None]

    grad_low = cotangent[0]
    grad = grad_low.astype(jnp.float32)
    moves = [None] * layers
    gain_terms = [None] * layers
    attn_move = ffn_move = None

    def ffn_pick(share, place, part):
        return share[place, part]

    def attn_pick(share, place, part):
        return lax.dynamic_slice_in_dim(share[part], links.quarter ^ place, 1, 1)

    for layer in reversed(range(layers)):
        kept, normed2, products, attn_w, ffn_w = saved[layer]
        last_ffn = [] if ffn_move is None else [ffn_move]
        last_attn = [] if attn_move is None else [attn_move]
        there, grad_normed = ffn_backward(grad_low, normed2, *products[2:], ffn_w[1])
        there, grad_normed = advance((there, grad_normed), *last_ffn, *last_attn)
        here = []
        new_move = Transfer(scatter_stages(links, here, ffn_share(links, there), ffn_pick, False))
        own, grad_normed = ffn_backward(grad_low, normed2, *products[:2], ffn_w[0], grad_normed)
        own, grad_normed, *new_move.flying = advance((own, grad_normed, *new_move.flying), *last_attn)
        here.append(ffn_share(links, own))
        new_move.advance()
        results = attention_backward(grad, grad_normed, *kept, *gains[layer], *attn_w, *where)
        results = advance(results, new_move, *last_ffn, *last_attn)
        qkv_w_grad, output_grad, grad, grad_low, *gain_grads = results
        ours, others = attention_shares(links, qkv_w_grad, output_grad, rows)
        moves[layer] = (attn_move, ffn_move) = (
            Transfer(scatter_stages(links, [ours], others, attn_pick, True)),
            new_move,
        )
        gain_terms[layer] = jnp.stack(gain_grads)
    gain_terms = jnp.concatenate(gain_terms, axis=1)
    gain_terms = advance(gain_terms, ffn_move, attn_move, *last_attn)
    rest = []
    for layer in range(1, layers):
        total = jnp.concatenate([moves[layer][1].finish(), moves[layer][0].finish()])
        total = settle(total, ffn_move.flying[0], ffn_move.flying[-1])
        rest.append(Transfer(quarter_stages(links, total)))
    gains = advance(links.sum_all(gain_terms), ffn_move, attn_move)
    last = Transfer(quarter_stages(links, ffn_move.finish()))
    gains = advance(gains, attn_move, *rest)
    tail = Transfer(quarter_stages(links, attn_move.finish()))
    shares = [(last.finish(), tail.finish())]
    for transfer in rest:
        quarters = transfer.finish()
        shares.append(([q[:3] for q in quarters], [q[3:] for q in quarters]))

    sums = [[] for _ in range(6)]
    for ffn_part, attn_part in shares:
        total = in_order(links, attn_part).reshape(-1, width).astype(jnp.float32)
        a, b = rows[0], rows[0] + rows[1]
        sums[0].append(total[:a].T)
        sums[1].append(total[a:b].T)
        sums[2].append(total[b:])
        quarters = in_order(links, ffn_part)
        for kind in range(3):
            total = quarters[:, kind].reshape(-1, width).astype(jnp.float32)
            sums[3 + kind].append(total if kind == 2 else total.T)
    sums = [jnp.stack(values) for values in sums]
    return (final, grad[None], gains[0], *sums[:3], gains[1], *sums[3:])


def solution(mesh):
    placed = (
        P(("dp", "col"), None, None),
        P(("dp", "col"), None),
        P(("dp", "col"), None, None),
        P(),
        P(None, None, "col"),
        P(None, None, "col"),
        P(None, "col", None),
        P(),
        P(None, None, "col"),
        P(None, None, "col"),
        P(None, "col", None),
    )
    return jax.shard_map(
        functools.partial(per_device, mesh.shape["dp"], mesh.shape["col"]),
        mesh=mesh,
        in_specs=placed,
        out_specs=(
            P(("dp", "col"), None, None),
            P(("dp", "col"), None, None),
            P(),
            P(None, None, "col"),
            P(None, None, "col"),
            P(None, "col", None),
            P(),
            P(None, None, "col"),
            P(None, None, "col"),
            P(None, "col", None),
        ),
        check_vma=False,
    )
```

```python
import functools
import math

import jax
import jax.numpy as jnp
from jax import lax
from jax.experimental import pallas as pl
from jax.experimental.pallas import tpu as pltpu
from jax.sharding import PartitionSpec as P

QUERY_HEADS = 15
KEY_VALUE_HEADS = 5
HEAD_WIDTH = 64


epsilon = 1e-05
theta_base = 10000.0


def rms_norm(value_rows, gain):
    return (
        value_rows
        * lax.rsqrt(jnp.mean(value_rows * value_rows, axis=-1, keepdims=True) + epsilon)
        * gain
    )


def tables(segments, head_size):
    sequence_length = segments.shape[0]
    rows = jnp.arange(sequence_length, dtype=jnp.int32)
    before = jnp.sum((segments[None, :] < segments[:, None]).astype(jnp.int32), axis=1)
    places = (rows - before).astype(jnp.float32)
    half = head_size // 2
    freqs = jnp.exp(-math.log(theta_base) * (2.0 * jnp.arange(half, dtype=jnp.float32) / head_size))
    angles = places[:, None] * freqs[None, :]
    cosine, sine = jnp.cos(angles), jnp.sin(angles)
    return (jnp.tile(cosine, (1, 4)), jnp.tile(jnp.concatenate([-sine, sine], axis=1), (1, 2)))


BLOCK = 256
REACH = 384
MEGA = 2**20


def call(body, outs, args, after=(), scratch=(), limit=56, flops=0, nbytes=0, **grid):
    given = len(args)
    late = len(after)

    def run(*refs):
        body(*refs[:given], *refs[given + late :])

    specs = grid.pop("in_specs", None) or [pl.BlockSpec(memory_space=pltpu.VMEM)] * given
    out_specs = grid.pop("out_specs", None) or [pl.BlockSpec(memory_space=pltpu.VMEM)] * len(outs)
    return pl.pallas_call(
        run,
        out_shape=outs,
        in_specs=list(specs) + [pl.BlockSpec(memory_space=pl.ANY)] * late,
        out_specs=out_specs,
        scratch_shapes=list(scratch),
        compiler_params=pltpu.CompilerParams(vmem_limit_bytes=limit * MEGA),
        cost_estimate=pl.CostEstimate(flops=flops, bytes_accessed=nbytes, transcendentals=0),
        **grid,
    )(*args, *after)


def dot(left, right, dims=((1,), (0,))):
    return lax.dot_general(left, right, (dims, ((), ())), preferred_element_type=jnp.float32)


NT = ((1,), (1,))
TN = ((0,), (0,))


def swap_halves(value):
    lane = lax.broadcasted_iota(jnp.int32, value.shape, 1)
    return jnp.where(lane % HEAD_WIDTH < HEAD_WIDTH // 2, pltpu.roll(value, 96, 1), pltpu.roll(value, 32, 1))


def spans(length):
    for start in range(0, length, BLOCK):
        yield start, max(0, start - REACH + 1) // 128 * 128, start + BLOCK


def fill_bias(bias, seg_col, seg_row, length):
    for index, (start, low, high) in enumerate(spans(length)):
        shape = (high - low, BLOCK)
        key = lax.broadcasted_iota(jnp.int32, shape, 0) + low
        query = lax.broadcasted_iota(jnp.int32, shape, 1) + start
        same = seg_col[low:high, :] == seg_row[:, start : start + BLOCK]
        bias[index, : high - low, :] = jnp.where((key <= query) & same, 0.0, -1e30)


def scale_of(value):
    return lax.rsqrt(jnp.mean(value * value, axis=-1, keepdims=True) + epsilon)


def attention_forward(hidden, gain, next_gain, qkv_w, output_w, cosine, sine, seg_col, seg_row):
    length, model = hidden.shape
    width = qkv_w.shape[0]
    q_width = QUERY_HEADS * HEAD_WIDTH
    kv_width = KEY_VALUE_HEADS * HEAD_WIDTH
    group = QUERY_HEADS // KEY_VALUE_HEADS
    rotated = q_width + kv_width
    most = max(high - low for _, low, high in spans(length))

    def body(hidden, gain, next_gain, qkv_w, output_w, cosine, sine, seg_col, seg_row, *rest):
        normed, qkv, attended, logsum, middle, normed2, raw, bias, turned = rest
        value = hidden[...]
        normed[...] = (value * scale_of(value) * gain[...]).astype(jnp.bfloat16)
        raw[...] = dot(normed[...], qkv_w[...], NT)
        for lane in range(0, rotated, 128):
            value = raw[:, lane : lane + 128]
            qkv[:, lane : lane + 128] = (value * cosine[...] + swap_halves(value) * sine[...]).astype(jnp.bfloat16)
        qkv[:, rotated:] = raw[:, rotated:].astype(jnp.bfloat16)
        fill_bias(bias, seg_col, seg_row, length)
        logsum[...] = jnp.zeros_like(logsum)
        turned[...] = raw[:, rotated:].T.astype(jnp.bfloat16)
        for index, (start, low, high) in enumerate(spans(length)):
            columns = []
            for head in range(QUERY_HEADS):
                kv = head // group
                query = qkv[start : start + BLOCK, head * HEAD_WIDTH : (head + 1) * HEAD_WIDTH] * 0.125
                at = q_width + kv * HEAD_WIDTH
                key = qkv[low:high, at : at + HEAD_WIDTH]
                logits = dot(key, query, NT) + bias[index, : high - low, :]
                peak = jnp.max(logits, axis=0, keepdims=True)
                expo = jnp.exp(logits - peak)
                total = jnp.sum(expo, axis=0, keepdims=True)
                value = turned[kv * HEAD_WIDTH : (kv + 1) * HEAD_WIDTH, low:high]
                columns.append(dot(value, expo.astype(jnp.bfloat16)) / total)
                logsum[head : head + 1, start : start + BLOCK] = peak + jnp.log(total)
            attended[start : start + BLOCK, :] = jnp.concatenate(columns, axis=0).T.astype(jnp.bfloat16)
        value = hidden[...] + dot(attended[...], output_w[...])
        middle[...] = value
        normed2[...] = (value * scale_of(value) * next_gain[...]).astype(jnp.bfloat16)

    low = jax.ShapeDtypeStruct((length, model), jnp.bfloat16)
    return call(
        body,
        [
            low,
            jax.ShapeDtypeStruct((length, width), jnp.bfloat16),
            jax.ShapeDtypeStruct((length, q_width), jnp.bfloat16),
            jax.ShapeDtypeStruct((16, length), jnp.float32),
            jax.ShapeDtypeStruct((length, model), jnp.float32),
            low,
        ],
        [hidden, gain, next_gain, qkv_w, output_w, cosine, sine, seg_col, seg_row],
        (),
        [
            pltpu.VMEM((length, width), jnp.float32),
            pltpu.VMEM((length // BLOCK, most, BLOCK), jnp.float32),
            pltpu.VMEM((kv_width, length), jnp.bfloat16),
        ],
        flops=20 * 10**9,
        nbytes=20 * MEGA,
    )


def attention_backward(
    grad, grad_normed2, hidden, normed, qkv, attended, logsum, middle, gain, next_gain, qkv_w, output_w, *where
):
    length, model = hidden.shape
    width = qkv.shape[1]
    q_width = QUERY_HEADS * HEAD_WIDTH
    kv_width = KEY_VALUE_HEADS * HEAD_WIDTH
    group = QUERY_HEADS // KEY_VALUE_HEADS
    rotated = q_width + kv_width
    most = max(high - low for _, low, high in spans(length))

    def body(grad, grad_normed2, hidden, normed, qkv, attended, logsum, middle, gain, next_gain, qkv_w, output_w, *rest):
        cosine, sine, seg_col, seg_row, *rest = rest
        qkv_w_grad, output_w_grad, out, out_low, gain_grad, next_gain_grad, *rest = rest
        bias, turned, key_sum, value_sum, query_sum, upstream_all, qkv_grad = rest

        def pull(value, g, upstream, gain_out):
            scale = scale_of(value)
            scaled = value * scale
            gain_out[...] = jnp.sum(upstream * scaled, axis=0, keepdims=True)
            pulled = upstream * g
            return scale * (pulled - scaled * jnp.mean(pulled * scaled, axis=-1, keepdims=True))

        out[...] = grad[...] + pull(middle[...], next_gain[...], grad_normed2[...], next_gain_grad)
        out_low[...] = out[...].astype(jnp.bfloat16)
        output_w_grad[...] = dot(attended[...], out_low[...], TN).astype(jnp.bfloat16)
        upstream_all[...] = dot(out_low[...], output_w[...], NT).astype(jnp.bfloat16)
        fill_bias(bias, seg_col, seg_row, length)
        turned[...] = qkv[:, q_width:rotated].astype(jnp.float32).T.astype(jnp.bfloat16) * 0.125
        key_sum[...] = jnp.zeros_like(key_sum)
        value_sum[...] = jnp.zeros_like(value_sum)
        for index, (start, low, high) in enumerate(spans(length)):
            for head in range(QUERY_HEADS):
                kv = head // group
                lanes = slice(head * HEAD_WIDTH, (head + 1) * HEAD_WIDTH)
                query = qkv[start : start + BLOCK, lanes] * 0.125
                upstream = upstream_all[start : start + BLOCK, lanes]
                at = q_width + kv * HEAD_WIDTH
                key = qkv[low:high, at : at + HEAD_WIDTH]
                value = qkv[low:high, at + kv_width : at + kv_width + HEAD_WIDTH]
                logits = dot(key, query, NT) + bias[index, : high - low, :]
                probs = jnp.exp(logits - logsum[head : head + 1, start : start + BLOCK])
                grad_probs = dot(value, upstream, NT)
                inner = jnp.sum(probs * grad_probs, axis=0, keepdims=True)
                grad_logits = (probs * (grad_probs - inner)).astype(jnp.bfloat16)
                value_sum[kv, low:high, :] += dot(probs.astype(jnp.bfloat16), upstream)
                key_sum[kv, low:high, :] += dot(grad_logits, query)
                query_sum[lanes, start : start + BLOCK] = dot(
                    turned[kv * HEAD_WIDTH : (kv + 1) * HEAD_WIDTH, low:high], grad_logits
                )
        raw = [query_sum[...].T] + [key_sum[kv] for kv in range(KEY_VALUE_HEADS)]
        raw = jnp.concatenate(raw, axis=1)
        for lane in range(0, rotated, 128):
            value = raw[:, lane : lane + 128]
            qkv_grad[:, lane : lane + 128] = (value * cosine[...] - swap_halves(value) * sine[...]).astype(jnp.bfloat16)
        values = [value_sum[kv] for kv in range(KEY_VALUE_HEADS)]
        qkv_grad[:, rotated:] = jnp.concatenate(values, axis=1).astype(jnp.bfloat16)
        qkv_w_grad[...] = dot(qkv_grad[...], normed[...], TN).astype(jnp.bfloat16)
        pulled = pull(hidden[...], gain[...], dot(qkv_grad[...], qkv_w[...]), gain_grad)
        out[...] += pulled
        out_low[...] = out[...].astype(jnp.bfloat16)

    gains = jax.ShapeDtypeStruct((1, model), jnp.float32)
    args = [grad, grad_normed2, hidden, normed, qkv, attended, logsum, middle, gain, next_gain, qkv_w, output_w, *where]
    return call(
        body,
        [
            jax.ShapeDtypeStruct(qkv_w.shape, jnp.bfloat16),
            jax.ShapeDtypeStruct(output_w.shape, jnp.bfloat16),
            jax.ShapeDtypeStruct((length, model), jnp.float32),
            jax.ShapeDtypeStruct((length, model), jnp.bfloat16),
            gains,
            gains,
        ],
        args,
        (),
        [
            pltpu.VMEM((length // BLOCK, most, BLOCK), jnp.float32),
            pltpu.VMEM((kv_width, length), jnp.bfloat16),
            pltpu.VMEM((KEY_VALUE_HEADS, length, HEAD_WIDTH), jnp.float32),
            pltpu.VMEM((KEY_VALUE_HEADS, length, HEAD_WIDTH), jnp.float32),
            pltpu.VMEM((q_width, length), jnp.float32),
            pltpu.VMEM((length, q_width), jnp.bfloat16),
            pltpu.VMEM((length, width), jnp.bfloat16),
        ],
        flops=35 * 10**9,
        nbytes=40 * MEGA,
    )


TILE = 256


def block_list(pieces):
    blocks, at = [], 0
    for piece in pieces:
        for z in range(piece.shape[0]):
            blocks.append((piece, z, at, at + piece.shape[2]))
            at += piece.shape[2]
    return blocks, at


def collect(pieces, store, semaphores):
    blocks, _ = block_list(pieces)
    copies = [
        [
            pltpu.make_async_copy(piece.at[z, kind], store.at[kind, pl.ds(at, end - at)], semaphores.at[kind, i])
            for kind in range(3)
        ]
        for i, (piece, z, at, end) in enumerate(blocks)
    ]
    for block in copies:
        for copy in block:
            copy.start()
    waited = [0]

    def until(limit):
        while waited[0] < len(blocks) and blocks[waited[0]][2] < limit:
            for copy in copies[waited[0]]:
                copy.wait()
            waited[0] += 1

    return until


def ffn_forward(middle, normed, here, there):
    length, width = middle.shape
    blocks, units = block_list(here)
    tile = math.gcd(TILE, units)

    def body(middle, normed, *rest):
        pieces = rest[: len(here) + len(there)]
        out, gate_one, up_one, gate_two, up_two, store, semaphores = rest[len(pieces) :]
        untils = [
            collect(half, store.at[i], semaphores.at[i])
            for i, half in enumerate((pieces[: len(here)], pieces[len(here) :]))
        ]
        out[...] = middle[...]
        for i, (gate_out, upward_out) in enumerate(((gate_one, up_one), (gate_two, up_two))):
            for at in range(0, units, tile):
                untils[i](at + tile)
                rows = slice(at, at + tile)
                gate = dot(normed[...], store[i, 0, rows, :], NT)
                upward = dot(normed[...], store[i, 1, rows, :], NT)
                gate_out[:, rows] = gate.astype(jnp.bfloat16)
                upward_out[:, rows] = upward.astype(jnp.bfloat16)
                active = (gate * jax.nn.sigmoid(gate) * upward).astype(jnp.bfloat16)
                out[...] += dot(active, store[i, 2, rows, :])

    low = jax.ShapeDtypeStruct((length, units), jnp.bfloat16)
    return call(
        body,
        [jax.ShapeDtypeStruct((length, width), jnp.float32), low, low, low, low],
        [middle, normed, *here, *there],
        (),
        [
            pltpu.VMEM((2, 3, units, width), jnp.bfloat16),
            pltpu.SemaphoreType.DMA((2, 3, len(blocks))),
        ],
        in_specs=[pl.BlockSpec(memory_space=pltpu.VMEM)] * 2
        + [pl.BlockSpec(memory_space=pl.ANY)] * (len(here) + len(there)),
        flops=11 * 10**9,
        nbytes=30 * MEGA,
    )


def ffn_backward(grad_low, normed, gate, upward, pieces, earlier=None):
    length, width = normed.shape
    blocks, units = block_list(pieces)
    rows_of_block = blocks[0][3]
    tile = math.gcd(TILE, units)
    before = [] if earlier is None else [earlier]

    def body(grad_low, normed, gate, upward, *rest):
        before, rest = rest[: len(rest) - 6 - len(pieces)], rest[len(rest) - 6 - len(pieces) :]
        parts, (grads, out, store, ready, semaphores, sent) = rest[: len(pieces)], rest[len(pieces) :]
        until = collect(parts, store, semaphores)
        out[...] = before[0][...] if before else jnp.zeros_like(out)
        sends = []
        for at in range(0, units, tile):
            until(at + tile)
            rows = slice(at, at + tile)
            grad_active = dot(grad_low[...], store[2, rows, :], NT)
            gate_value = gate[:, rows].astype(jnp.float32)
            up_value = upward[:, rows].astype(jnp.float32)
            sigma = jax.nn.sigmoid(gate_value)
            silu = gate_value * sigma
            active = (silu * up_value).astype(jnp.bfloat16)
            grad_up = (grad_active * silu).astype(jnp.bfloat16)
            grad_gate = (grad_active * up_value * (sigma + silu * (1.0 - sigma))).astype(jnp.bfloat16)
            ready[2, rows, :] = dot(active, grad_low[...], TN).astype(jnp.bfloat16)
            ready[0, rows, :] = dot(grad_gate, normed[...], TN).astype(jnp.bfloat16)
            ready[1, rows, :] = dot(grad_up, normed[...], TN).astype(jnp.bfloat16)
            out[...] += dot(grad_gate, store[0, rows, :]) + dot(grad_up, store[1, rows, :])
            while len(sends) < len(blocks) and blocks[len(sends)][3] <= at + tile:
                i = len(sends)
                span = pl.ds(blocks[i][2], rows_of_block)
                sends.append(
                    [
                        pltpu.make_async_copy(ready.at[kind, span], grads.at[i, kind], sent.at[kind, i])
                        for kind in range(3)
                    ]
                )
                for copy in sends[-1]:
                    copy.start()
        for block in sends:
            for copy in block:
                copy.wait()

    return call(
        body,
        [
            jax.ShapeDtypeStruct((len(blocks), 3, rows_of_block, width), jnp.bfloat16),
            jax.ShapeDtypeStruct((length, width), jnp.float32),
        ],
        [grad_low, normed, gate, upward, *before, *pieces],
        (),
        [
            pltpu.VMEM((3, units, width), jnp.bfloat16),
            pltpu.VMEM((3, units, width), jnp.bfloat16),
            pltpu.SemaphoreType.DMA((3, len(blocks))),
            pltpu.SemaphoreType.DMA((3, len(blocks))),
        ],
        in_specs=[pl.BlockSpec(memory_space=pltpu.VMEM)] * (4 + len(before))
        + [pl.BlockSpec(memory_space=pl.ANY)] * len(pieces),
        out_specs=[pl.BlockSpec(memory_space=pl.ANY), pl.BlockSpec(memory_space=pltpu.VMEM)],
        flops=11 * 10**9,
        nbytes=30 * MEGA,
    )


class Links:
    def __init__(self, dp, col):
        self.dp, self.col, self.line = dp, col, col // 2
        self.rest = [list(range(r, dp, 4)) for r in range(4)]
        self.quarter = lax.axis_index("dp") % 4
        self.core = lax.axis_index("col") % 2
        self.chip = lax.axis_index("col") // 2

    def x(self, value):
        return lax.ppermute(value, "dp", [(i, i ^ 1) for i in range(self.dp)])

    def y(self, value):
        return lax.ppermute(value, "dp", [(i, i ^ 2) for i in range(self.dp)])

    def other_core(self, value):
        return lax.ppermute(value, "col", [(i, i ^ 1) for i in range(self.col)])

    def both(self, value):
        return lax.ppermute(value, "dp", [(i, i ^ 3) for i in range(self.dp)])

    def send(self, value, step):
        return lax.ppermute(value, "col", [(i, (i + 2 * step) % self.col) for i in range(self.col)])


def add(*terms):
    total = terms[0].astype(jnp.float32)
    for term in terms[1:]:
        total = total + term.astype(jnp.float32)
    return total.astype(jnp.bfloat16)


class Transfer:
    def __init__(self, stages):
        self.stages = stages
        self.result = None
        self.flying = next(stages)

    def advance(self, arrays=None):
        try:
            self.flying = self.stages.send(self.flying if arrays is None else arrays)
        except StopIteration as stop:
            self.flying, self.result = [], stop.value

    def finish(self):
        while self.result is None:
            self.advance()
        return self.result


def settle(value, *arrays):
    return lax.optimization_barrier((value, arrays))[0]


def advance(value, *transfers):
    flying = [transfer.flying for transfer in transfers]
    value, flying = lax.optimization_barrier((value, flying))
    for transfer, arrays in zip(transfers, flying, strict=True):
        transfer.advance(arrays)
    return value


def gather_stages(links, part):
    far = yield [links.send(part, -step) for step in range(1, links.line)]
    own = jnp.stack([part, *far])
    half = links.line // 2
    from_x, from_y = yield [links.x(own), links.y(own)]
    low, high, own_c, x_c, y_c = yield [
        links.y(from_x[:half]),
        links.x(from_y[half:]),
        links.other_core(own),
        links.other_core(from_x),
        links.other_core(from_y),
    ]
    low_c, high_c = yield [links.other_core(low), links.other_core(high)]
    return [[own, from_x, from_y, low, high], [own_c, x_c, y_c, low_c, high_c]]


def scatter_stages(links, kept, there, pick, in_line):
    (got,) = yield [links.other_core(there)]
    here = kept[0]
    half = links.line // 2
    low, high = slice(0, half), slice(half, links.line)

    def part(place, piece):
        return add(pick(here, place, piece), pick(got, place, piece))

    from_x, from_y = yield [
        links.x(jnp.stack([part(3, high), part(1, high)])),
        links.y(jnp.stack([part(3, low), part(2, low)])),
    ]
    x_low, y_high = yield [
        links.x(add(pick(here, 1, low), pick(got, 1, low), from_y[0])),
        links.y(add(pick(here, 2, high), pick(got, 2, high), from_x[0])),
    ]
    own = jnp.concatenate(
        [
            add(pick(here, 0, low), pick(got, 0, low), from_y[1], x_low),
            add(pick(here, 0, high), pick(got, 0, high), from_x[1], y_high),
        ]
    )

    def chip(step):
        if not in_line:
            return own[step]
        return lax.dynamic_index_in_dim(own, (links.chip + step) % links.line, 0, False)

    far = yield [links.send(chip(step), step) for step in range(1, links.line)]
    total = add(chip(0), *far)
    if links.dp > 4:
        total = lax.psum(total, "dp", axis_index_groups=links.rest)
    return total


def quarter_stages(links, total):
    others = yield [links.x(total), links.y(total), links.both(total)]
    return (total, *others)


def in_order(links, quarters):
    whole = jnp.zeros((4, *quarters[0].shape), quarters[0].dtype)
    for place, block in enumerate(quarters):
        whole = lax.dynamic_update_index_in_dim(whole, block, links.quarter ^ place, 0)
    return whole


def own_quarter(links, packed, axis):
    shape = packed.shape[:axis] + (4, packed.shape[axis] // 4) + packed.shape[axis + 1 :]
    return lax.dynamic_index_in_dim(packed.reshape(shape), links.quarter, axis, False)


def attention_weights(links, blocks, rows):
    part, width = blocks[0][0].shape[2:]
    line = links.line
    places, starts = (0, 1, 2, 3, 3), (0, 0, 0, 0, line // 2)
    pieces = blocks[0] + blocks[1]
    total = sum(piece.shape[0] for piece in pieces)

    def body(*refs):
        whole, semaphores = refs[len(pieces) :]
        quarter = lax.axis_index("dp") % 4
        core = lax.axis_index("col") % 2
        chip = lax.axis_index("col") // 2
        copies = []
        for i, piece in enumerate(refs[: len(pieces)]):
            side, j = divmod(i, len(places))
            for z in range(piece.shape[0]):
                target = whole.at[(chip + starts[j] + z) % line, core ^ side, quarter ^ places[j]]
                copies.append(pltpu.make_async_copy(piece.at[z, 3], target, semaphores.at[len(copies)]))
        for copy in copies:
            copy.start()
        for copy in copies:
            copy.wait()

    (whole,) = call(
        body,
        [jax.ShapeDtypeStruct((line, 2, 4, part, width), jnp.bfloat16)],
        pieces,
        (),
        [pltpu.SemaphoreType.DMA((total,))],
        in_specs=[pl.BlockSpec(memory_space=pl.ANY)] * len(pieces),
        out_specs=[pl.BlockSpec(memory_space=pl.ANY)],
        limit=16,
        nbytes=10 * MEGA,
    )
    whole = whole.reshape(links.col, 4 * part, width)
    a, b = rows[0], rows[0] + rows[1]
    return (
        jnp.concatenate([whole[:, :a].reshape(-1, width), whole[:, a:b].reshape(-1, width)]),
        whole[:, b:].reshape(-1, width),
    )


def attention_shares(links, qkv_grad, output_grad, rows, everywhere=None):
    width = output_grad.shape[1]
    cut = rows[0] * links.col
    parts = [g.reshape(links.col, -1, width) for g in (qkv_grad[:cut], qkv_grad[cut:], output_grad)]
    whole = jnp.concatenate(parts, axis=1).reshape(links.line, 2, 4, -1, width)
    if everywhere is not None:
        more = jnp.broadcast_to(everywhere, (*whole.shape[:3], *everywhere.shape))
        whole = jnp.concatenate([whole, more], axis=3)
    return [lax.dynamic_index_in_dim(whole, links.core ^ core, 1, False) for core in range(2)]


def ffn_pieces(blocks):
    if blocks[0].shape[2] % 16 == 0:
        return blocks
    width = blocks[0].shape[-1]
    joined = [jnp.moveaxis(block[:, :3], 1, 0).reshape(3, -1, width) for block in blocks]
    return [jnp.concatenate(joined, axis=1)[None]]


def ffn_share(links, grads):
    if grads.shape[0] == 1:
        grads = jnp.moveaxis(grads.reshape(3, 4 * links.line, -1, grads.shape[-1]), 0, 1)
    return grads.reshape(4, links.line, *grads.shape[1:])


def per_device(
    dp,
    col,
    inputs,
    segment_ids,
    cotangent,
    attn_gain,
    query_weight,
    key_value_weight,
    output_weight,
    ffn_gain,
    gate_weight,
    upward_weight,
    down_weight,
):
    links = Links(dp, col)
    layers, width = attn_gain.shape
    rows = (query_weight.shape[2], key_value_weight.shape[2], output_weight.shape[1])
    segments = segment_ids[0]
    where = (*tables(segments, HEAD_WIDTH), segments[:, None], segments[None, :])
    attn_gains = attn_gain.astype(jnp.float32)
    ffn_gains = ffn_gain.astype(jnp.float32)

    parts = []
    for layer in range(layers):
        attn_part = jnp.concatenate([query_weight[layer].T, key_value_weight[layer].T, output_weight[layer]])
        ffn_part = jnp.stack([gate_weight[layer].T, upward_weight[layer].T, down_weight[layer]])
        parts.append(
            jnp.concatenate([own_quarter(links, ffn_part, 1), own_quarter(links, attn_part, 0)[None]])
        )

    hidden = inputs[0].astype(jnp.float32)
    gains = [(attn_gains[layer][None], ffn_gains[layer][None]) for layer in range(layers)]
    saved = []
    move = Transfer(gather_stages(links, parts[0]))
    for layer in range(layers):
        later = []
        if layer + 1 < layers:
            part = advance(parts[layer + 1], move)
            later = [Transfer(gather_stages(links, part))]
            move.flying = settle(move.flying, *later[0].flying)
            advance(None, move)
        hidden = advance(hidden, move, *later)
        blocks = move.finish()
        qkv_w, output_w = attention_weights(links, blocks, rows)
        ffn_w = [ffn_pieces(half) for half in blocks]
        normed, qkv, attended, logsum, middle, normed2 = attention_forward(
            hidden, *gains[layer], qkv_w, output_w, *where
        )
        normed2 = advance(normed2, *later)
        result, *products = ffn_forward(middle, normed2, *ffn_w)
        saved.append(((hidden, normed, qkv, attended, logsum, middle), normed2, products, (qkv_w, output_w), ffn_w))
        hidden = result
        if later:
            move = later[0]
    final = hidden.astype(jnp.bfloat16)[None]

    grad_low = cotangent[0]
    grad = grad_low.astype(jnp.float32)
    moves = [None] * layers
    gain_terms = [None] * layers
    attn_move = ffn_move = None

    def ffn_pick(share, place, part):
        return share[place, part]

    def attn_pick(share, place, part):
        return lax.dynamic_slice_in_dim(share[part], links.quarter ^ place, 1, 1)

    for layer in reversed(range(layers)):
        kept, normed2, products, attn_w, ffn_w = saved[layer]
        last_ffn = [] if ffn_move is None else [ffn_move]
        last_attn = [] if attn_move is None else [attn_move]
        there, grad_normed = ffn_backward(grad_low, normed2, *products[2:], ffn_w[1])
        there, grad_normed = advance((there, grad_normed), *last_ffn, *last_attn)
        here = []
        new_move = Transfer(scatter_stages(links, here, ffn_share(links, there), ffn_pick, False))
        own, grad_normed = ffn_backward(grad_low, normed2, *products[:2], ffn_w[0], grad_normed)
        own, grad_normed, *new_move.flying = advance((own, grad_normed, *new_move.flying), *last_attn)
        here.append(ffn_share(links, own))
        new_move.advance()
        results = attention_backward(grad, grad_normed, *kept, *gains[layer], *attn_w, *where)
        results = advance(results, new_move, *last_ffn, *last_attn)
        qkv_w_grad, output_grad, grad, grad_low, *gain_grads = results
        gain_terms[layer] = gain_grads
        everywhere = None
        if layer == 0:
            terms = [gain_terms[i][kind] for kind in range(2) for i in range(layers)]
            pad = jnp.zeros((-len(terms) % 16, width), jnp.float32)
            everywhere = jnp.concatenate([*terms, pad]).astype(jnp.bfloat16)
        ours, others = attention_shares(links, qkv_w_grad, output_grad, rows, everywhere)
        moves[layer] = (attn_move, ffn_move) = (
            Transfer(scatter_stages(links, [ours], others, attn_pick, True)),
            new_move,
        )
    advance(None, ffn_move, attn_move, *last_attn)
    rest = []
    for layer in range(1, layers):
        total = jnp.concatenate([moves[layer][1].finish(), moves[layer][0].finish()])
        total = settle(total, ffn_move.flying[len(ffn_move.flying) // 2], *attn_move.flying)
        rest.append(Transfer(quarter_stages(links, total)))
    advance(None, ffn_move, attn_move, *rest)
    last = Transfer(quarter_stages(links, ffn_move.finish()))
    advance(None, attn_move, last)
    done = settle([transfer.finish() for transfer in (last, *rest)], attn_move.flying[0])
    total = attn_move.finish()
    part = rows[0] + rows[1] + rows[2]
    gains = total[0, part // 4 :][: 2 * layers].astype(jnp.float32).reshape(2, layers, width)
    tail = Transfer(quarter_stages(links, total[:, : part // 4]))
    shares = [(done[0], tail.finish())]
    for quarters in done[1:]:
        shares.append(([q[:3] for q in quarters], [q[3:] for q in quarters]))

    sums = [[] for _ in range(6)]
    for ffn_part, attn_part in shares:
        total = in_order(links, attn_part).reshape(-1, width).astype(jnp.float32)
        a, b = rows[0], rows[0] + rows[1]
        sums[0].append(total[:a].T)
        sums[1].append(total[a:b].T)
        sums[2].append(total[b:])
        quarters = in_order(links, ffn_part)
        for kind in range(3):
            total = quarters[:, kind].reshape(-1, width).astype(jnp.float32)
            sums[3 + kind].append(total if kind == 2 else total.T)
    sums = [jnp.stack(values) for values in sums]
    return (final, grad[None], gains[0], *sums[:3], gains[1], *sums[3:])


def solution(mesh):
    placed = (
        P(("dp", "col"), None, None),
        P(("dp", "col"), None),
        P(("dp", "col"), None, None),
        P(),
        P(None, None, "col"),
        P(None, None, "col"),
        P(None, "col", None),
        P(),
        P(None, None, "col"),
        P(None, None, "col"),
        P(None, "col", None),
    )
    return jax.shard_map(
        functools.partial(per_device, mesh.shape["dp"], mesh.shape["col"]),
        mesh=mesh,
        in_specs=placed,
        out_specs=(
            P(("dp", "col"), None, None),
            P(("dp", "col"), None, None),
            P(),
            P(None, None, "col"),
            P(None, None, "col"),
            P(None, "col", None),
            P(),
            P(None, None, "col"),
            P(None, None, "col"),
            P(None, "col", None),
        ),
        check_vma=False,
    )
```

```python
import functools
import math

import jax
import jax.numpy as jnp
from jax import lax
from jax.experimental import pallas as pl
from jax.experimental.pallas import tpu as pltpu
from jax.sharding import PartitionSpec as P

QUERY_HEADS = 15
KEY_VALUE_HEADS = 5
HEAD_WIDTH = 64


epsilon = 1e-05
theta_base = 10000.0


def rms_norm(value_rows, gain):
    return (
        value_rows
        * lax.rsqrt(jnp.mean(value_rows * value_rows, axis=-1, keepdims=True) + epsilon)
        * gain
    )


def tables(segments, head_size):
    sequence_length = segments.shape[0]
    rows = jnp.arange(sequence_length, dtype=jnp.int32)
    before = jnp.sum((segments[None, :] < segments[:, None]).astype(jnp.int32), axis=1)
    places = (rows - before).astype(jnp.float32)
    half = head_size // 2
    freqs = jnp.exp(-math.log(theta_base) * (2.0 * jnp.arange(half, dtype=jnp.float32) / head_size))
    angles = places[:, None] * freqs[None, :]
    cosine, sine = jnp.cos(angles), jnp.sin(angles)
    return (jnp.tile(cosine, (1, 4)), jnp.tile(jnp.concatenate([-sine, sine], axis=1), (1, 2)))


BLOCK = 256
REACH = 384
MEGA = 2**20


def call(body, outs, args, after=(), scratch=(), limit=56, flops=0, nbytes=0, **grid):
    given = len(args)
    late = len(after)

    def run(*refs):
        body(*refs[:given], *refs[given + late :])

    specs = grid.pop("in_specs", None) or [pl.BlockSpec(memory_space=pltpu.VMEM)] * given
    out_specs = grid.pop("out_specs", None) or [pl.BlockSpec(memory_space=pltpu.VMEM)] * len(outs)
    return pl.pallas_call(
        run,
        out_shape=outs,
        in_specs=list(specs) + [pl.BlockSpec(memory_space=pl.ANY)] * late,
        out_specs=out_specs,
        scratch_shapes=list(scratch),
        compiler_params=pltpu.CompilerParams(vmem_limit_bytes=limit * MEGA),
        cost_estimate=pl.CostEstimate(flops=flops, bytes_accessed=nbytes, transcendentals=0),
        **grid,
    )(*args, *after)


def dot(left, right, dims=((1,), (0,))):
    return lax.dot_general(left, right, (dims, ((), ())), preferred_element_type=jnp.float32)


NT = ((1,), (1,))
TN = ((0,), (0,))


def swap_halves(value):
    lane = lax.broadcasted_iota(jnp.int32, value.shape, 1)
    return jnp.where(lane % HEAD_WIDTH < HEAD_WIDTH // 2, pltpu.roll(value, 96, 1), pltpu.roll(value, 32, 1))


def spans(length):
    for start in range(0, length, BLOCK):
        yield start, max(0, start - REACH + 1) // 128 * 128, start + BLOCK


def fill_bias(bias, seg_col, seg_row, length):
    for index, (start, low, high) in enumerate(spans(length)):
        shape = (high - low, BLOCK)
        key = lax.broadcasted_iota(jnp.int32, shape, 0) + low
        query = lax.broadcasted_iota(jnp.int32, shape, 1) + start
        same = seg_col[low:high, :] == seg_row[:, start : start + BLOCK]
        bias[index, : high - low, :] = jnp.where((key <= query) & same, 0.0, -1e30)


def scale_of(value):
    return lax.rsqrt(jnp.mean(value * value, axis=-1, keepdims=True) + epsilon)


def attention_forward(hidden, gain, next_gain, qkv_w, output_w, cosine, sine, seg_col, seg_row):
    length, model = hidden.shape
    width = qkv_w.shape[0]
    q_width = QUERY_HEADS * HEAD_WIDTH
    kv_width = KEY_VALUE_HEADS * HEAD_WIDTH
    group = QUERY_HEADS // KEY_VALUE_HEADS
    rotated = q_width + kv_width
    most = max(high - low for _, low, high in spans(length))

    def body(hidden, gain, next_gain, qkv_w, output_w, cosine, sine, seg_col, seg_row, *rest):
        normed, qkv, attended, logsum, middle, normed2, raw, bias, turned = rest
        value = hidden[...]
        normed[...] = (value * scale_of(value) * gain[...]).astype(jnp.bfloat16)
        raw[...] = dot(normed[...], qkv_w[...], NT)
        for lane in range(0, rotated, 128):
            value = raw[:, lane : lane + 128]
            qkv[:, lane : lane + 128] = (value * cosine[...] + swap_halves(value) * sine[...]).astype(jnp.bfloat16)
        qkv[:, rotated:] = raw[:, rotated:].astype(jnp.bfloat16)
        fill_bias(bias, seg_col, seg_row, length)
        logsum[...] = jnp.zeros_like(logsum)
        turned[...] = raw[:, rotated:].T.astype(jnp.bfloat16)
        for index, (start, low, high) in enumerate(spans(length)):
            columns = []
            for head in range(QUERY_HEADS):
                kv = head // group
                query = qkv[start : start + BLOCK, head * HEAD_WIDTH : (head + 1) * HEAD_WIDTH] * 0.125
                at = q_width + kv * HEAD_WIDTH
                key = qkv[low:high, at : at + HEAD_WIDTH]
                logits = dot(key, query, NT) + bias[index, : high - low, :]
                peak = jnp.max(logits, axis=0, keepdims=True)
                expo = jnp.exp(logits - peak)
                total = jnp.sum(expo, axis=0, keepdims=True)
                value = turned[kv * HEAD_WIDTH : (kv + 1) * HEAD_WIDTH, low:high]
                columns.append(dot(value, expo.astype(jnp.bfloat16)) / total)
                logsum[head : head + 1, start : start + BLOCK] = peak + jnp.log(total)
            attended[start : start + BLOCK, :] = jnp.concatenate(columns, axis=0).T.astype(jnp.bfloat16)
        value = hidden[...] + dot(attended[...], output_w[...])
        middle[...] = value
        normed2[...] = (value * scale_of(value) * next_gain[...]).astype(jnp.bfloat16)

    low = jax.ShapeDtypeStruct((length, model), jnp.bfloat16)
    return call(
        body,
        [
            low,
            jax.ShapeDtypeStruct((length, width), jnp.bfloat16),
            jax.ShapeDtypeStruct((length, q_width), jnp.bfloat16),
            jax.ShapeDtypeStruct((16, length), jnp.float32),
            jax.ShapeDtypeStruct((length, model), jnp.float32),
            low,
        ],
        [hidden, gain, next_gain, qkv_w, output_w, cosine, sine, seg_col, seg_row],
        (),
        [
            pltpu.VMEM((length, width), jnp.float32),
            pltpu.VMEM((length // BLOCK, most, BLOCK), jnp.float32),
            pltpu.VMEM((kv_width, length), jnp.bfloat16),
        ],
        flops=20 * 10**9,
        nbytes=20 * MEGA,
    )


def attention_backward(
    grad, grad_normed2, hidden, normed, qkv, attended, logsum, middle, gain, next_gain, qkv_w, output_w, *where
):
    length, model = hidden.shape
    width = qkv.shape[1]
    q_width = QUERY_HEADS * HEAD_WIDTH
    kv_width = KEY_VALUE_HEADS * HEAD_WIDTH
    group = QUERY_HEADS // KEY_VALUE_HEADS
    rotated = q_width + kv_width
    most = max(high - low for _, low, high in spans(length))

    def body(grad, grad_normed2, hidden, normed, qkv, attended, logsum, middle, gain, next_gain, qkv_w, output_w, *rest):
        cosine, sine, seg_col, seg_row, *rest = rest
        qkv_w_grad, output_w_grad, out, out_low, gain_grad, next_gain_grad, *rest = rest
        bias, turned, key_sum, value_sum, query_sum, upstream_all, qkv_grad = rest

        def pull(value, g, upstream, gain_out):
            scale = scale_of(value)
            scaled = value * scale
            gain_out[...] = jnp.sum(upstream * scaled, axis=0, keepdims=True)
            pulled = upstream * g
            return scale * (pulled - scaled * jnp.mean(pulled * scaled, axis=-1, keepdims=True))

        out[...] = grad[...] + pull(middle[...], next_gain[...], grad_normed2[...], next_gain_grad)
        out_low[...] = out[...].astype(jnp.bfloat16)
        output_w_grad[...] = dot(attended[...], out_low[...], TN).astype(jnp.bfloat16)
        upstream_all[...] = dot(out_low[...], output_w[...], NT).astype(jnp.bfloat16)
        fill_bias(bias, seg_col, seg_row, length)
        turned[...] = qkv[:, q_width:rotated].astype(jnp.float32).T.astype(jnp.bfloat16) * 0.125
        key_sum[...] = jnp.zeros_like(key_sum)
        value_sum[...] = jnp.zeros_like(value_sum)
        for index, (start, low, high) in enumerate(spans(length)):
            for head in range(QUERY_HEADS):
                kv = head // group
                lanes = slice(head * HEAD_WIDTH, (head + 1) * HEAD_WIDTH)
                query = qkv[start : start + BLOCK, lanes] * 0.125
                upstream = upstream_all[start : start + BLOCK, lanes]
                at = q_width + kv * HEAD_WIDTH
                key = qkv[low:high, at : at + HEAD_WIDTH]
                value = qkv[low:high, at + kv_width : at + kv_width + HEAD_WIDTH]
                logits = dot(key, query, NT) + bias[index, : high - low, :]
                probs = jnp.exp(logits - logsum[head : head + 1, start : start + BLOCK])
                grad_probs = dot(value, upstream, NT)
                inner = jnp.sum(probs * grad_probs, axis=0, keepdims=True)
                grad_logits = (probs * (grad_probs - inner)).astype(jnp.bfloat16)
                value_sum[kv, low:high, :] += dot(probs.astype(jnp.bfloat16), upstream)
                key_sum[kv, low:high, :] += dot(grad_logits, query)
                query_sum[lanes, start : start + BLOCK] = dot(
                    turned[kv * HEAD_WIDTH : (kv + 1) * HEAD_WIDTH, low:high], grad_logits
                )
        raw = [query_sum[...].T] + [key_sum[kv] for kv in range(KEY_VALUE_HEADS)]
        raw = jnp.concatenate(raw, axis=1)
        for lane in range(0, rotated, 128):
            value = raw[:, lane : lane + 128]
            qkv_grad[:, lane : lane + 128] = (value * cosine[...] - swap_halves(value) * sine[...]).astype(jnp.bfloat16)
        values = [value_sum[kv] for kv in range(KEY_VALUE_HEADS)]
        qkv_grad[:, rotated:] = jnp.concatenate(values, axis=1).astype(jnp.bfloat16)
        qkv_w_grad[...] = dot(qkv_grad[...], normed[...], TN).astype(jnp.bfloat16)
        pulled = pull(hidden[...], gain[...], dot(qkv_grad[...], qkv_w[...]), gain_grad)
        out[...] += pulled
        out_low[...] = out[...].astype(jnp.bfloat16)

    gains = jax.ShapeDtypeStruct((1, model), jnp.float32)
    args = [grad, grad_normed2, hidden, normed, qkv, attended, logsum, middle, gain, next_gain, qkv_w, output_w, *where]
    return call(
        body,
        [
            jax.ShapeDtypeStruct(qkv_w.shape, jnp.bfloat16),
            jax.ShapeDtypeStruct(output_w.shape, jnp.bfloat16),
            jax.ShapeDtypeStruct((length, model), jnp.float32),
            jax.ShapeDtypeStruct((length, model), jnp.bfloat16),
            gains,
            gains,
        ],
        args,
        (),
        [
            pltpu.VMEM((length // BLOCK, most, BLOCK), jnp.float32),
            pltpu.VMEM((kv_width, length), jnp.bfloat16),
            pltpu.VMEM((KEY_VALUE_HEADS, length, HEAD_WIDTH), jnp.float32),
            pltpu.VMEM((KEY_VALUE_HEADS, length, HEAD_WIDTH), jnp.float32),
            pltpu.VMEM((q_width, length), jnp.float32),
            pltpu.VMEM((length, q_width), jnp.bfloat16),
            pltpu.VMEM((length, width), jnp.bfloat16),
        ],
        flops=35 * 10**9,
        nbytes=40 * MEGA,
    )


TILE = 256


def block_list(pieces):
    blocks, at = [], 0
    for piece in pieces:
        for z in range(piece.shape[0]):
            blocks.append((piece, z, at, at + piece.shape[2]))
            at += piece.shape[2]
    return blocks, at


def collect(pieces, store, semaphores):
    blocks, _ = block_list(pieces)
    copies = [
        [
            pltpu.make_async_copy(piece.at[z, kind], store.at[kind, pl.ds(at, end - at)], semaphores.at[kind, i])
            for kind in range(3)
        ]
        for i, (piece, z, at, end) in enumerate(blocks)
    ]
    for block in copies:
        for copy in block:
            copy.start()
    waited = [0]

    def until(limit):
        while waited[0] < len(blocks) and blocks[waited[0]][2] < limit:
            for copy in copies[waited[0]]:
                copy.wait()
            waited[0] += 1

    return until


def ffn_forward(middle, normed, here, there):
    length, width = middle.shape
    blocks, units = block_list(here)
    tile = math.gcd(TILE, units)

    def body(middle, normed, *rest):
        pieces = rest[: len(here) + len(there)]
        out, gate_one, up_one, gate_two, up_two, store, semaphores = rest[len(pieces) :]
        untils = [
            collect(half, store.at[i], semaphores.at[i])
            for i, half in enumerate((pieces[: len(here)], pieces[len(here) :]))
        ]
        out[...] = middle[...]
        for i, (gate_out, upward_out) in enumerate(((gate_one, up_one), (gate_two, up_two))):
            for at in range(0, units, tile):
                untils[i](at + tile)
                rows = slice(at, at + tile)
                gate = dot(normed[...], store[i, 0, rows, :], NT)
                upward = dot(normed[...], store[i, 1, rows, :], NT)
                gate_out[:, rows] = gate.astype(jnp.bfloat16)
                upward_out[:, rows] = upward.astype(jnp.bfloat16)
                active = (gate * jax.nn.sigmoid(gate) * upward).astype(jnp.bfloat16)
                out[...] += dot(active, store[i, 2, rows, :])

    low = jax.ShapeDtypeStruct((length, units), jnp.bfloat16)
    return call(
        body,
        [jax.ShapeDtypeStruct((length, width), jnp.float32), low, low, low, low],
        [middle, normed, *here, *there],
        (),
        [
            pltpu.VMEM((2, 3, units, width), jnp.bfloat16),
            pltpu.SemaphoreType.DMA((2, 3, len(blocks))),
        ],
        in_specs=[pl.BlockSpec(memory_space=pltpu.VMEM)] * 2
        + [pl.BlockSpec(memory_space=pl.ANY)] * (len(here) + len(there)),
        flops=11 * 10**9,
        nbytes=30 * MEGA,
    )


def ffn_backward(grad_low, normed, gate, upward, pieces, earlier=None):
    length, width = normed.shape
    blocks, units = block_list(pieces)
    rows_of_block = blocks[0][3]
    tile = math.gcd(TILE, units)
    before = [] if earlier is None else [earlier]

    def body(grad_low, normed, gate, upward, *rest):
        before, rest = rest[: len(rest) - 6 - len(pieces)], rest[len(rest) - 6 - len(pieces) :]
        parts, (grads, out, store, ready, semaphores, sent) = rest[: len(pieces)], rest[len(pieces) :]
        until = collect(parts, store, semaphores)
        out[...] = before[0][...] if before else jnp.zeros_like(out)
        sends = []
        for at in range(0, units, tile):
            until(at + tile)
            rows = slice(at, at + tile)
            grad_active = dot(grad_low[...], store[2, rows, :], NT)
            gate_value = gate[:, rows].astype(jnp.float32)
            up_value = upward[:, rows].astype(jnp.float32)
            sigma = jax.nn.sigmoid(gate_value)
            silu = gate_value * sigma
            active = (silu * up_value).astype(jnp.bfloat16)
            grad_up = (grad_active * silu).astype(jnp.bfloat16)
            grad_gate = (grad_active * up_value * (sigma + silu * (1.0 - sigma))).astype(jnp.bfloat16)
            ready[2, rows, :] = dot(active, grad_low[...], TN).astype(jnp.bfloat16)
            ready[0, rows, :] = dot(grad_gate, normed[...], TN).astype(jnp.bfloat16)
            ready[1, rows, :] = dot(grad_up, normed[...], TN).astype(jnp.bfloat16)
            out[...] += dot(grad_gate, store[0, rows, :]) + dot(grad_up, store[1, rows, :])
            while len(sends) < len(blocks) and blocks[len(sends)][3] <= at + tile:
                i = len(sends)
                span = pl.ds(blocks[i][2], rows_of_block)
                sends.append(
                    [
                        pltpu.make_async_copy(ready.at[kind, span], grads.at[i, kind], sent.at[kind, i])
                        for kind in range(3)
                    ]
                )
                for copy in sends[-1]:
                    copy.start()
        for block in sends:
            for copy in block:
                copy.wait()

    return call(
        body,
        [
            jax.ShapeDtypeStruct((len(blocks), 3, rows_of_block, width), jnp.bfloat16),
            jax.ShapeDtypeStruct((length, width), jnp.float32),
        ],
        [grad_low, normed, gate, upward, *before, *pieces],
        (),
        [
            pltpu.VMEM((3, units, width), jnp.bfloat16),
            pltpu.VMEM((3, units, width), jnp.bfloat16),
            pltpu.SemaphoreType.DMA((3, len(blocks))),
            pltpu.SemaphoreType.DMA((3, len(blocks))),
        ],
        in_specs=[pl.BlockSpec(memory_space=pltpu.VMEM)] * (4 + len(before))
        + [pl.BlockSpec(memory_space=pl.ANY)] * len(pieces),
        out_specs=[pl.BlockSpec(memory_space=pl.ANY), pl.BlockSpec(memory_space=pltpu.VMEM)],
        flops=11 * 10**9,
        nbytes=30 * MEGA,
    )


class Links:
    def __init__(self, dp, col):
        self.dp, self.col, self.line = dp, col, col // 2
        self.rest = [list(range(r, dp, 4)) for r in range(4)]
        self.quarter = lax.axis_index("dp") % 4
        self.core = lax.axis_index("col") % 2
        self.chip = lax.axis_index("col") // 2

    def x(self, value):
        return lax.ppermute(value, "dp", [(i, i ^ 1) for i in range(self.dp)])

    def y(self, value):
        return lax.ppermute(value, "dp", [(i, i ^ 2) for i in range(self.dp)])

    def other_core(self, value):
        return lax.ppermute(value, "col", [(i, i ^ 1) for i in range(self.col)])

    def both(self, value):
        return lax.ppermute(value, "dp", [(i, i ^ 3) for i in range(self.dp)])

    def send(self, value, step):
        return lax.ppermute(value, "col", [(i, (i + 2 * step) % self.col) for i in range(self.col)])


def add(*terms):
    total = terms[0].astype(jnp.float32)
    for term in terms[1:]:
        total = total + term.astype(jnp.float32)
    return total.astype(jnp.bfloat16)


class Transfer:
    def __init__(self, stages):
        self.stages = stages
        self.result = None
        self.flying = next(stages)

    def advance(self, arrays=None):
        try:
            self.flying = self.stages.send(self.flying if arrays is None else arrays)
        except StopIteration as stop:
            self.flying, self.result = [], stop.value

    def finish(self):
        while self.result is None:
            self.advance()
        return self.result


def settle(value, *arrays):
    return lax.optimization_barrier((value, arrays))[0]


def advance(value, *transfers):
    flying = [transfer.flying for transfer in transfers]
    value, flying = lax.optimization_barrier((value, flying))
    for transfer, arrays in zip(transfers, flying, strict=True):
        transfer.advance(arrays)
    return value


def gather_stages(links, part):
    far = yield [links.send(part, -step) for step in range(1, links.line)]
    own = jnp.stack([part, *far])
    half = links.line // 2
    from_x, from_y = yield [links.x(own), links.y(own)]
    low, high, own_c, x_c, y_c = yield [
        links.y(from_x[:half]),
        links.x(from_y[half:]),
        links.other_core(own),
        links.other_core(from_x),
        links.other_core(from_y),
    ]
    low_c, high_c = yield [links.other_core(low), links.other_core(high)]
    return [[own, from_x, from_y, low, high], [own_c, x_c, y_c, low_c, high_c]]


def scatter_stages(links, kept, there, pick, in_line):
    (got,) = yield [links.other_core(there)]
    here = kept[0]
    half = links.line // 2
    low, high = slice(0, half), slice(half, links.line)

    def part(place, piece):
        return add(pick(here, place, piece), pick(got, place, piece))

    from_x, from_y = yield [
        links.x(jnp.stack([part(3, high), part(1, high)])),
        links.y(jnp.stack([part(3, low), part(2, low)])),
    ]
    x_low, y_high = yield [
        links.x(add(pick(here, 1, low), pick(got, 1, low), from_y[0])),
        links.y(add(pick(here, 2, high), pick(got, 2, high), from_x[0])),
    ]
    own = jnp.concatenate(
        [
            add(pick(here, 0, low), pick(got, 0, low), from_y[1], x_low),
            add(pick(here, 0, high), pick(got, 0, high), from_x[1], y_high),
        ]
    )

    def chip(step):
        if not in_line:
            return own[step]
        return lax.dynamic_index_in_dim(own, (links.chip + step) % links.line, 0, False)

    far = yield [links.send(chip(step), step) for step in range(1, links.line)]
    total = add(chip(0), *far)
    if links.dp > 4:
        total = lax.psum(total, "dp", axis_index_groups=links.rest)
    return total


def quarter_stages(links, total):
    others = yield [links.x(total), links.y(total), links.both(total)]
    return (total, *others)


def in_order(links, quarters):
    whole = jnp.zeros((4, *quarters[0].shape), quarters[0].dtype)
    for place, block in enumerate(quarters):
        whole = lax.dynamic_update_index_in_dim(whole, block, links.quarter ^ place, 0)
    return whole


def own_quarter(links, packed, axis):
    shape = packed.shape[:axis] + (4, packed.shape[axis] // 4) + packed.shape[axis + 1 :]
    return lax.dynamic_index_in_dim(packed.reshape(shape), links.quarter, axis, False)


def attention_weights(links, blocks, rows):
    part, width = blocks[0][0].shape[2:]
    line = links.line
    places, starts = (0, 1, 2, 3, 3), (0, 0, 0, 0, line // 2)
    pieces = blocks[0] + blocks[1]
    total = sum(piece.shape[0] for piece in pieces)

    def body(*refs):
        whole, semaphores = refs[len(pieces) :]
        quarter = lax.axis_index("dp") % 4
        core = lax.axis_index("col") % 2
        chip = lax.axis_index("col") // 2
        copies = []
        for i, piece in enumerate(refs[: len(pieces)]):
            side, j = divmod(i, len(places))
            for z in range(piece.shape[0]):
                target = whole.at[(chip + starts[j] + z) % line, core ^ side, quarter ^ places[j]]
                copies.append(pltpu.make_async_copy(piece.at[z, 3], target, semaphores.at[len(copies)]))
        for copy in copies:
            copy.start()
        for copy in copies:
            copy.wait()

    (whole,) = call(
        body,
        [jax.ShapeDtypeStruct((line, 2, 4, part, width), jnp.bfloat16)],
        pieces,
        (),
        [pltpu.SemaphoreType.DMA((total,))],
        in_specs=[pl.BlockSpec(memory_space=pl.ANY)] * len(pieces),
        out_specs=[pl.BlockSpec(memory_space=pl.ANY)],
        limit=16,
        nbytes=10 * MEGA,
    )
    whole = whole.reshape(links.col, 4 * part, width)
    a, b = rows[0], rows[0] + rows[1]
    return (
        jnp.concatenate([whole[:, :a].reshape(-1, width), whole[:, a:b].reshape(-1, width)]),
        whole[:, b:].reshape(-1, width),
    )


def attention_shares(links, qkv_grad, output_grad, rows, everywhere=None):
    width = output_grad.shape[1]
    cut = rows[0] * links.col
    parts = [g.reshape(links.col, -1, width) for g in (qkv_grad[:cut], qkv_grad[cut:], output_grad)]
    whole = jnp.concatenate(parts, axis=1).reshape(links.line, 2, 4, -1, width)
    if everywhere is not None:
        more = jnp.broadcast_to(everywhere, (*whole.shape[:3], *everywhere.shape))
        whole = jnp.concatenate([whole, more], axis=3)
    return [lax.dynamic_index_in_dim(whole, links.core ^ core, 1, False) for core in range(2)]


def ffn_pieces(blocks):
    if blocks[0].shape[2] % 16 == 0:
        return blocks
    width = blocks[0].shape[-1]
    joined = [jnp.moveaxis(block[:, :3], 1, 0).reshape(3, -1, width) for block in blocks]
    return [jnp.concatenate(joined, axis=1)[None]]


def ffn_share(links, grads):
    if grads.shape[0] == 1:
        grads = jnp.moveaxis(grads.reshape(3, 4 * links.line, -1, grads.shape[-1]), 0, 1)
    return grads.reshape(4, links.line, *grads.shape[1:])


def per_device(
    dp,
    col,
    inputs,
    segment_ids,
    cotangent,
    attn_gain,
    query_weight,
    key_value_weight,
    output_weight,
    ffn_gain,
    gate_weight,
    upward_weight,
    down_weight,
):
    links = Links(dp, col)
    layers, width = attn_gain.shape
    rows = (query_weight.shape[2], key_value_weight.shape[2], output_weight.shape[1])
    segments = segment_ids[0]
    where = (*tables(segments, HEAD_WIDTH), segments[:, None], segments[None, :])
    attn_gains = attn_gain.astype(jnp.float32)
    ffn_gains = ffn_gain.astype(jnp.float32)

    parts = []
    for layer in range(layers):
        attn_part = jnp.concatenate([query_weight[layer].T, key_value_weight[layer].T, output_weight[layer]])
        ffn_part = jnp.stack([gate_weight[layer].T, upward_weight[layer].T, down_weight[layer]])
        parts.append(
            jnp.concatenate([own_quarter(links, ffn_part, 1), own_quarter(links, attn_part, 0)[None]])
        )

    hidden = inputs[0].astype(jnp.float32)
    gains = [(attn_gains[layer][None], ffn_gains[layer][None]) for layer in range(layers)]
    saved = []
    move = Transfer(gather_stages(links, parts[0]))
    for layer in range(layers):
        later = []
        if layer + 1 < layers:
            part = advance(parts[layer + 1], move)
            later = [Transfer(gather_stages(links, part))]
            move.flying = settle(move.flying, *later[0].flying)
            advance(None, move)
        hidden = advance(hidden, move, *later)
        blocks = move.finish()
        qkv_w, output_w = attention_weights(links, blocks, rows)
        ffn_w = [ffn_pieces(half) for half in blocks]
        normed, qkv, attended, logsum, middle, normed2 = attention_forward(
            hidden, *gains[layer], qkv_w, output_w, *where
        )
        normed2 = advance(normed2, *later)
        result, *products = ffn_forward(middle, normed2, *ffn_w)
        saved.append(((hidden, normed, qkv, attended, logsum, middle), normed2, products, (qkv_w, output_w), ffn_w))
        hidden = result
        if later:
            move = later[0]
    final = hidden.astype(jnp.bfloat16)[None]

    grad_low = cotangent[0]
    grad = grad_low.astype(jnp.float32)
    moves = [None] * layers
    gain_terms = [None] * layers
    attn_move = ffn_move = None

    def ffn_pick(share, place, part):
        return share[place, part]

    def attn_pick(share, place, part):
        return lax.dynamic_slice_in_dim(share[part], links.quarter ^ place, 1, 1)

    for layer in reversed(range(layers)):
        kept, normed2, products, attn_w, ffn_w = saved[layer]
        last_ffn = [] if ffn_move is None else [ffn_move]
        last_attn = [] if attn_move is None else [attn_move]
        there, grad_normed = ffn_backward(grad_low, normed2, *products[2:], ffn_w[1])
        there, grad_normed = advance((there, grad_normed), *last_ffn, *last_attn)
        here = []
        new_move = Transfer(scatter_stages(links, here, ffn_share(links, there), ffn_pick, False))
        own, grad_normed = ffn_backward(grad_low, normed2, *products[:2], ffn_w[0], grad_normed)
        own, grad_normed, *new_move.flying = advance((own, grad_normed, *new_move.flying), *last_attn)
        here.append(ffn_share(links, own))
        new_move.advance()
        results = attention_backward(grad, grad_normed, *kept, *gains[layer], *attn_w, *where)
        results = advance(results, new_move, *last_ffn, *last_attn)
        qkv_w_grad, output_grad, grad, grad_low, *gain_grads = results
        gain_terms[layer] = gain_grads
        everywhere = None
        if layer == 0:
            terms = [gain_terms[i][kind] for kind in range(2) for i in range(layers)]
            pad = jnp.zeros((-len(terms) % 16, width), jnp.float32)
            everywhere = jnp.concatenate([*terms, pad]).astype(jnp.bfloat16)
        ours, others = attention_shares(links, qkv_w_grad, output_grad, rows, everywhere)
        moves[layer] = (attn_move, ffn_move) = (
            Transfer(scatter_stages(links, [ours], others, attn_pick, True)),
            new_move,
        )
    advance(None, ffn_move, attn_move, *last_attn)
    attn_move.flying = settle(attn_move.flying, ffn_move.flying[len(ffn_move.flying) // 2])
    attn_move.advance()
    advance(None, ffn_move, attn_move)
    total = [ffn_move.finish()]
    for attn, ffn in moves[1:]:
        total += [ffn.finish(), attn.finish()]
    last = Transfer(quarter_stages(links, jnp.concatenate(total)))
    advance(None, attn_move, last)
    done = last.finish()
    total = attn_move.finish()
    part = rows[0] + rows[1] + rows[2]
    gains = total[0, part // 4 :][: 2 * layers].astype(jnp.float32).reshape(2, layers, width)
    tail = Transfer(quarter_stages(links, total[:, : part // 4]))
    shares = [([q[:3] for q in done], tail.finish())]
    for at in range(3, 4 * layers - 1, 4):
        shares.append(([q[at : at + 3] for q in done], [q[at + 3 : at + 4] for q in done]))

    sums = [[] for _ in range(6)]
    for ffn_part, attn_part in shares:
        total = in_order(links, attn_part).reshape(-1, width).astype(jnp.float32)
        a, b = rows[0], rows[0] + rows[1]
        sums[0].append(total[:a].T)
        sums[1].append(total[a:b].T)
        sums[2].append(total[b:])
        quarters = in_order(links, ffn_part)
        for kind in range(3):
            total = quarters[:, kind].reshape(-1, width).astype(jnp.float32)
            sums[3 + kind].append(total if kind == 2 else total.T)
    sums = [jnp.stack(values) for values in sums]
    return (final, grad[None], gains[0], *sums[:3], gains[1], *sums[3:])


def solution(mesh):
    placed = (
        P(("dp", "col"), None, None),
        P(("dp", "col"), None),
        P(("dp", "col"), None, None),
        P(),
        P(None, None, "col"),
        P(None, None, "col"),
        P(None, "col", None),
        P(),
        P(None, None, "col"),
        P(None, None, "col"),
        P(None, "col", None),
    )
    return jax.shard_map(
        functools.partial(per_device, mesh.shape["dp"], mesh.shape["col"]),
        mesh=mesh,
        in_specs=placed,
        out_specs=(
            P(("dp", "col"), None, None),
            P(("dp", "col"), None, None),
            P(),
            P(None, None, "col"),
            P(None, None, "col"),
            P(None, "col", None),
            P(),
            P(None, None, "col"),
            P(None, None, "col"),
            P(None, "col", None),
        ),
        check_vma=False,
    )
```
